32 devices in a mesh: dp: 16 (over z, y, core), tensor: 2 (over x).
Axes of the slice: x: 2, y: 2, z: 4, core: 2. Of those that a mesh axis runs over, the one named last changes fastest.
Arguments:
- inputs: bfloat16 [128, 160, 768], P(('dp', 'tensor')), may hold values from -6 to 6
- lengths: int32 [128], P('dp'), may hold values from 95 to 160
- query_weight: bfloat16 [768, 768], P(None, 'tensor'), may hold values from -0.21875 to 0.21875
- query_bias: float32 [768], P('tensor'), may hold values from -3 to 3
- key_weight: bfloat16 [768, 768], P(None, 'tensor'), may hold values from -0.21875 to 0.21875
- value_weight: bfloat16 [768, 768], P(None, 'tensor'), may hold values from -0.21875 to 0.21875
- value_bias: float32 [768], P('tensor'), may hold values from -3 to 3
- output_weight: bfloat16 [768, 768], P('tensor'), may hold values from -0.875 to 0.875
- output_bias: float32 [768], replicated, may hold values from -3 to 3
- first_gain: float32 [768], replicated, may hold values from 0.1 to 1.9
- first_shift: float32 [768], replicated, may hold values from -3 to 3
- inner_weight: bfloat16 [768, 3072], P(None, 'tensor'), may hold values from -0.21875 to 0.21875
- inner_bias: float32 [3072], P('tensor'), may hold values from -3 to 3
- outer_weight: bfloat16 [3072, 768], P('tensor'), may hold values from -0.15625 to 0.15625
- outer_bias: float32 [768], replicated, may hold values from -3 to 3
- second_gain: float32 [768], replicated, may hold values from 0.1 to 1.9
- second_shift: float32 [768], replicated, may hold values from -3 to 3
- cotangent: bfloat16 [128, 160, 768], P(('dp', 'tensor')), may hold values from -6 to 6
Outputs:
- outputs: bfloat16 [128, 160, 768], P(('dp', 'tensor'))
- grad_inputs: float32 [128, 160, 768], P(('dp', 'tensor'))
- grad_query_weight: float32 [768, 768], P(None, 'tensor')
- grad_query_bias: float32 [768], P('tensor')
- grad_key_weight: float32 [768, 768], P(None, 'tensor')
- grad_value_weight: float32 [768, 768], P(None, 'tensor')
- grad_value_bias: float32 [768], P('tensor')
- grad_output_weight: float32 [768, 768], P('tensor')
- grad_output_bias: float32 [768], replicated
- grad_first_gain: float32 [768], replicated
- grad_first_shift: float32 [768], replicated
- grad_inner_weight: float32 [768, 3072], P(None, 'tensor')
- grad_inner_bias: float32 [3072], P('tensor')
- grad_outer_weight: float32 [3072, 768], P('tensor')
- grad_outer_bias: float32 [768], replicated
- grad_second_gain: float32 [768], replicated
- grad_second_shift: float32 [768], replicated
The draws below stay inside these ranges and needn't reach their ends.
All inputs are finite; a program needn't handle non-finite values.
Results may differ from the reference program's by a relative error of at most 0.014.
Values may be sent and summed in bfloat16 or wider, within the bound.
No kernel may reach another device: no remote copies, remote signals or barrier semaphores. Data moves between devices by JAX's collectives and lax.ppermute only.
A program may use at most 192 MiB of HBM per device.

```python
import math
import jax
import jax.numpy as jnp
from jax import lax

D = 768
HEADS = 12
HDIM = 64
FF = 3072
SLOTS = 160
CHAINS = 128


def with_ends(values, key, least, largest):
    index_at = [jax.random.randint(jax.random.fold_in(key, axis), (), 0, length) for axis, length in enumerate(values.shape)]
    main_axis = values.shape.index(max(values.shape))
    next_to = index_at[:main_axis] + [(index_at[main_axis] + 1) % values.shape[main_axis]] + index_at[main_axis + 1:]
    return values.at[tuple(index_at)].set(least).at[tuple(next_to)].set(largest)


def block_scale(own_key, shape, shards, least, top_value):
    def one(position, blocks):
        steps = jax.random.uniform(jax.random.fold_in(jax.random.fold_in(own_key, 6), position), (blocks,), jnp.float32, least / len(shards), top_value / len(shards))
        return jnp.repeat(jnp.exp(steps), shape[position] // blocks).reshape((-1,) + (1,) * (len(shape) - position - 1))

    loudness = one(*shards[0])
    for cut in shards[1:]:
        loudness = loudness * one(*cut)
    return loudness


def scatter_about(own_key, shape, width, limit, cuts=(), kind=jnp.bfloat16):
    entries = width * jax.random.normal(own_key, shape, jnp.float32)
    if cuts:
        entries = entries * block_scale(own_key, shape, cuts, -0.22, 0.18)
    return jnp.clip(entries, -limit, limit).astype(kind)


def setup_inputs(seed: int = 0) -> dict:
    seeds = jax.random.split(jax.random.key(seed), 19)
    inputs = scatter_about(seeds[0], (CHAINS, SLOTS, D), 1.0, 6.0, ((0, 32),))
    lengths = with_ends(jax.random.randint(seeds[1], (CHAINS,), SLOTS * 19 // 32, SLOTS + 1), jax.random.fold_in(seeds[1], 1), SLOTS * 19 // 32, SLOTS).astype(jnp.int32)
    query_weight = scatter_about(seeds[2], (D, D), D ** -0.5, 0.21875, ((1, 2),))
    query_bias = scatter_about(seeds[3], (D,), 0.5, 3.0, ((0, 2),), jnp.float32)
    key_weight = scatter_about(seeds[4], (D, D), D ** -0.5, 0.21875, ((1, 2),))
    value_weight = scatter_about(seeds[5], (D, D), D ** -0.5, 0.21875, ((1, 2),))
    value_bias = scatter_about(seeds[6], (D,), 0.5, 3.0, ((0, 2),), jnp.float32)
    output_weight = scatter_about(seeds[7], (D, D), (D // 16) ** -0.5, 0.875, ((0, 2),))
    output_bias = scatter_about(seeds[8], (D,), 0.5, 3.0, (), jnp.float32)
    first_gain = jnp.clip(1.0 + 0.18 * jax.random.normal(seeds[9], (D,), jnp.float32), 0.1, 1.9)
    first_shift = scatter_about(seeds[10], (D,), 0.5, 3.0, (), jnp.float32)
    inner_weight = scatter_about(seeds[11], (D, FF), D ** -0.5, 0.21875, ((1, 2),))
    inner_bias = scatter_about(seeds[12], (FF,), 0.5, 3.0, ((0, 2),), jnp.float32)
    outer_weight = scatter_about(seeds[13], (FF, D), (FF // 2) ** -0.5, 0.15625, ((0, 2),))
    outer_bias = scatter_about(seeds[14], (D,), 0.5, 3.0, (), jnp.float32)
    second_gain = jnp.clip(1.0 + 0.18 * jax.random.normal(seeds[15], (D,), jnp.float32), 0.1, 1.9)
    second_shift = scatter_about(seeds[16], (D,), 0.5, 3.0, (), jnp.float32)
    cotangent = scatter_about(seeds[17], (CHAINS, SLOTS, D), 1.0, 6.0, ((0, 32),))
    return {"inputs": inputs, "lengths": lengths, "query_weight": query_weight, "query_bias": query_bias, "key_weight": key_weight, "value_weight": value_weight, "value_bias": value_bias, "output_weight": output_weight, "output_bias": output_bias, "first_gain": first_gain, "first_shift": first_shift, "inner_weight": inner_weight, "inner_bias": inner_bias, "outer_weight": outer_weight, "outer_bias": outer_bias, "second_gain": second_gain, "second_shift": second_shift, "cotangent": cotangent}


highest = lax.Precision.HIGHEST

@jax.custom_vjp
def low(v):
    return lax.optimization_barrier(v.astype(jnp.bfloat16)).astype(jnp.float32)

@jax.custom_vjp
def low_back(v):
    return v

def low_keep(v):
    return (low(v), None)

def low_pass(kept, grad):
    return (grad,)

def back_keep(v):
    return (v, None)

def back_low(kept, grad):
    return (low(grad),)
low.defvjp(low_keep, low_pass)
low_back.defvjp(back_keep, back_low)

def matmul(first_op, second_op):
    return jnp.dot(first_op, second_op, precision=highest)

def norm_rows(row_data, gain_vec, shift_vec):
    center = row_data - lax.optimization_barrier(jnp.mean(row_data, -1, keepdims=True))
    spread = lax.optimization_barrier(jnp.mean(center * center, -1, keepdims=True))
    return center * lax.rsqrt(spread + 1e-05) * gain_vec + shift_vec

def block_layer(params_all, block_data):
    query_weight, query_bias, key_weight, value_weight, value_bias, output_weight, output_bias, first_gain, first_shift, inner_weight, inner_bias, outer_weight, outer_bias, second_gain, second_shift = params_all
    block_inputs, block_lengths = block_data
    chain_count = block_inputs.shape[0]
    row_data = block_inputs.reshape(chain_count * SLOTS, D)
    head_shape = (chain_count, SLOTS, HEADS, HDIM)
    queries = low_back(low(matmul(row_data, query_weight) + query_bias)).reshape(head_shape)
    key_rows = low_back(low(matmul(row_data, key_weight))).reshape(head_shape)
    values = low_back(low(matmul(row_data, value_weight) + value_bias)).reshape(head_shape)
    scaling = 1.0 / math.sqrt(HDIM)
    raw_scores = jnp.einsum('gqhe,gkhe->ghqk', queries, key_rows, precision=highest) * scaling
    scores = low_back(raw_scores)
    key_valid = jnp.arange(SLOTS, dtype=jnp.int32)[None, :] < block_lengths[:, None]
    masked = jnp.where(key_valid[:, None, None, :], scores, -1e+30)
    probs = low(jax.nn.softmax(masked, axis=-1))
    context = jnp.einsum('ghqk,gkhe->gqhe', probs, values, precision=highest)
    context = low_back(low(context)).reshape(chain_count * SLOTS, D)
    attended = low_back(matmul(context, output_weight) + output_bias)
    hidden = norm_rows(row_data + attended, first_gain, first_shift)
    inner_pre = low_back(matmul(low(hidden), inner_weight) + inner_bias)
    activated = low(jax.nn.gelu(inner_pre, approximate=False))
    outer_part = low_back(matmul(activated, outer_weight) + outer_bias)
    result = norm_rows(hidden + outer_part, second_gain, second_shift)
    return result.reshape(chain_count, SLOTS, D)

def reference(inputs, lengths, query_weight, query_bias, key_weight, value_weight, value_bias, output_weight, output_bias, first_gain, first_shift, inner_weight, inner_bias, outer_weight, outer_bias, second_gain, second_shift, cotangent):
    params_all = tuple((item.astype(jnp.float32) for item in (query_weight, query_bias, key_weight, value_weight, value_bias, output_weight, output_bias, first_gain, first_shift, inner_weight, inner_bias, outer_weight, outer_bias, second_gain, second_shift)))
    inputs_f = inputs.astype(jnp.float32)
    block_size = math.gcd(CHAINS, 16)
    block_count = CHAINS // block_size

    def forward(params_in, inputs_in):

        def one_block(block_data):
            return block_layer(params_in, block_data)
        mapped = lax.map(jax.checkpoint(one_block), (inputs_in.reshape(block_count, block_size, SLOTS, D), lengths.reshape(block_count, block_size)))
        return mapped.reshape(CHAINS, SLOTS, D)
    outputs, pullback = jax.vjp(forward, params_all, inputs_f)
    grad_params, grad_inputs = pullback(cotangent.astype(jnp.float32))
    return (outputs.astype(jnp.bfloat16), grad_inputs, grad_params[0], grad_params[1], grad_params[2], grad_params[3], grad_params[4], grad_params[5], grad_params[6], grad_params[7], grad_params[8], grad_params[9], grad_params[10], grad_params[11], grad_params[12], grad_params[13], grad_params[14])
```

```python
import math
from typing import NamedTuple

import jax
import jax.numpy as jnp
from jax import lax
from jax.experimental import pallas as pl
from jax.experimental.pallas import tpu as pltpu
from jax.sharding import PartitionSpec as P

HDIM = 64
PAIR = 2 * HDIM
SCALING = 1.0 / math.sqrt(HDIM)
VMEM_LIMIT = 56 * 1024 * 1024
BF16 = jnp.bfloat16
F32 = jnp.float32

ORDERS = {"outer": ("tyz", "zty"), "inner": ("tyz", "ytz"), "attn": ("tyz", "ytz")}


def dot(a, b):
    return lax.dot_general(a, b, (((1,), (0,)), ((), ())), preferred_element_type=F32)


def dot_t(a, b):
    return lax.dot_general(a, b, (((1,), (1,)), ((), ())), preferred_element_type=F32)


def dot_rows(a, b):
    return lax.dot_general(a, b, (((0,), (0,)), ((), ())), preferred_element_type=F32)


def row_stats(rows):
    center = rows - jnp.mean(rows, -1, keepdims=True)
    inverse = lax.rsqrt(jnp.mean(center * center, -1, keepdims=True) + 1e-05)
    return center * inverse, inverse


def norm_back(scaled, normed, inverse):
    return inverse * (
        scaled
        - jnp.mean(scaled, -1, keepdims=True)
        - normed * jnp.mean(scaled * normed, -1, keepdims=True)
    )


def lanes_of(ref):
    return ref[...].reshape(1, -1)


def strip(index, size, base=0):
    return pl.ds(pl.multiple_of(base + index * size, size), size)


class Place(NamedTuple):
    core: jax.Array
    y: jax.Array
    z: jax.Array


class Load(NamedTuple):
    shape: tuple
    dtype: jnp.dtype
    parts: list


def load(arr):
    return Load(arr.shape, arr.dtype, [(arr, None, None)])


def view(ref, at, place):
    return ref if at is None else ref.at[at(place)]


class Line:
    def __init__(self):
        self.last = []

    def __call__(self, name, body, loads, outs, stage=(), smem=(), n_out=24):
        parts = [part for item in loads for part in item.parts]
        after = self.last
        n_smem, n_parts, n_outs = len(smem), len(parts), len(outs)
        n_stage, n_loads = len(stage), len(loads)

        def run(*refs):
            refs = list(refs)

            def take(count):
                got = refs[:count]
                del refs[:count]
                return got

            smem_refs, part_refs = take(n_smem), take(n_parts)
            take(len(after))
            out_refs, held, staged = take(n_outs), take(n_loads), take(n_stage)
            in_sem, out_sem = refs
            spot = lax.axis_index("dp")
            place = Place(lax.rem(spot, 2), lax.rem(spot // 2, 2), lax.rem(spot // 4, 2))
            pending = []
            at = 0
            for ref, item in zip(held, loads):
                copies = []
                for _, src, dst in item.parts:
                    copies.append(
                        pltpu.make_async_copy(
                            view(part_refs[at], src, place), view(ref, dst, place), in_sem.at[at]
                        )
                    )
                    copies[-1].start()
                    at += 1
                pending.append(copies)
            stores = []

            def get(i):
                for copy in pending[i]:
                    copy.wait()
                pending[i] = []
                return held[i]

            def put(src, i, dst=None):
                ref = out_refs[i] if dst is None else out_refs[i].at[dst]
                copy = pltpu.make_async_copy(src, ref, out_sem.at[len(stores)])
                copy.start()
                stores.append(copy)

            body(place, get, staged, put, *smem_refs)
            for i in range(n_loads):
                get(i)
            for copy in stores:
                copy.wait()

        results = pl.pallas_call(
            run,
            out_shape=[jax.ShapeDtypeStruct(s, d) for s, d in outs],
            in_specs=[pl.BlockSpec(memory_space=pltpu.SMEM)] * n_smem
            + [pl.BlockSpec(memory_space=pl.ANY)] * (n_parts + len(after)),
            out_specs=[pl.BlockSpec(memory_space=pl.ANY)] * n_outs,
            scratch_shapes=[pltpu.VMEM(item.shape, item.dtype) for item in loads]
            + [pltpu.VMEM(s, d) for s, d in stage]
            + [pltpu.SemaphoreType.DMA((max(n_parts, 1),)), pltpu.SemaphoreType.DMA((n_out,))],
            compiler_params=pltpu.CompilerParams(vmem_limit_bytes=VMEM_LIMIT),
            cost_estimate=pl.CostEstimate(flops=0, bytes_accessed=0, transcendentals=0),
            name=name,
        )(*smem, *[arr for arr, _, _ in parts], *after)
        self.last = [results[-1]]
        return results


def attn_fwd_body(last, width, place, get, staged, put, len_ref):
    if last:
        X, W, BQ, BV, WO, ACC, OB, FG, FS = range(9)
        q_ref, k_ref, v_ref, ctx_ref, r1_ref, hid_ref = staged
    else:
        X, W, BQ, BV, WO = range(5)
        q_ref, k_ref, v_ref, ctx_ref, part_ref = staged
    x_ref = get(X)
    x = x_ref[...]
    w_ref = get(W)
    q_ref[...] = (dot(x, w_ref[:, :width]) + lanes_of(get(BQ))).astype(BF16)
    put(q_ref, 0)
    k_ref[...] = dot(x, w_ref[:, width : 2 * width]).astype(BF16)
    put(k_ref, 1)
    v_ref[...] = (dot(x, w_ref[:, 2 * width :]) + lanes_of(get(BV))).astype(BF16)
    put(v_ref, 2)
    chains = len_ref.shape[0]
    slots = x.shape[0] // chains
    first = lax.broadcasted_iota(jnp.int32, (slots, PAIR), 1) < HDIM
    spot = lax.broadcasted_iota(jnp.int32, (slots, 2 * slots), 0)
    for chain in range(chains):
        rows = slice(chain * slots, (chain + 1) * slots)
        valid = spot < len_ref[chain]
        for at in range(0, width, PAIR):
            q = q_ref[rows, at : at + PAIR]
            q_both = jnp.concatenate([jnp.where(first, q, 0), jnp.where(first, 0, q)], 0)
            scores = jnp.where(valid, dot_t(k_ref[rows, at : at + PAIR], q_both) * SCALING, -1e30)
            grown = jnp.exp(scores - jnp.max(scores, 0, keepdims=True))
            probs = (grown * (1.0 / jnp.sum(grown, 0, keepdims=True))).astype(BF16)
            both = dot_rows(probs, v_ref[rows, at : at + PAIR])
            ctx_ref[rows, at : at + PAIR] = jnp.where(first, both[:slots], both[slots:]).astype(BF16)
    put(ctx_ref, 3)
    attended = dot(ctx_ref[...], get(WO)[...])
    if last:
        r1 = x_ref[...].astype(F32) + (attended + get(ACC)[...]) + lanes_of(get(OB))
        r1_ref[...] = r1
        put(r1_ref, 4)
        normed, _ = row_stats(r1)
        hid_ref[...] = (normed * lanes_of(get(FG)) + lanes_of(get(FS))).astype(BF16)
        put(hid_ref, 5)
    else:
        part_ref[...] = attended
        put(part_ref, 4)


def ffn_fwd_body(last, place, get, staged, put):
    HID, WIA, BIA, WIB, BIB, WOA, WOB = range(7)
    hid = get(HID)[...]
    for g, (wi, bi) in enumerate(((WIA, BIA), (WIB, BIB))):
        act_ref, dg_ref = staged[2 * g], staged[2 * g + 1]
        pre = dot(hid, get(wi)[...]) + lanes_of(get(bi))
        cdf = 0.5 + 0.5 * lax.erf(pre * math.sqrt(0.5))
        act_ref[...] = (pre * cdf).astype(BF16)
        put(act_ref, 2 * g)
        bell = jnp.exp(pre * pre * -0.5) * (1.0 / math.sqrt(2 * math.pi))
        dg_ref[...] = (cdf + pre * bell).astype(BF16)
        put(dg_ref, 2 * g + 1)
    total = dot(staged[0][...], get(WOA)[...]) + dot(staged[2][...], get(WOB)[...])
    if not last:
        staged[4][...] = total
        put(staged[4], 4)
        return
    ACC, R1, FG, FS, OB, SG, SS, COT = range(7, 15)
    out_ref, dr2_ref, low_ref, sums_ref = staged[4:]
    normed, _ = row_stats(get(R1)[...])
    hidden = normed * lanes_of(get(FG)) + lanes_of(get(FS))
    r2 = hidden + (total + get(ACC)[...]) + lanes_of(get(OB))
    normed, inverse = row_stats(r2)
    gain = lanes_of(get(SG))
    out_ref[...] = (normed * gain + lanes_of(get(SS))).astype(BF16)
    put(out_ref, 4)
    cot = get(COT)[...].astype(F32)
    dr2 = norm_back(cot * gain, normed, inverse)
    low = dr2.astype(BF16)
    low_ref[...] = low
    put(low_ref, 6)
    dr2_ref[...] = dr2
    put(dr2_ref, 5)
    sums_ref[0:1, :] = jnp.sum(cot * normed, 0, keepdims=True)
    sums_ref[1:2, :] = jnp.sum(cot, 0, keepdims=True)
    sums_ref[2:3, :] = jnp.sum(low.astype(F32), 0, keepdims=True)
    put(sums_ref, 7)


def ffn_bwd_body(last, place, get, staged, put):
    LOW, WOA, DGA, WOB, DGB, WIA, WIB, ACC = range(8)
    low2 = get(LOW)[...]
    for g, (wo, dg) in enumerate(((WOA, DGA), (WOB, DGB))):
        dp_ref = staged[g]
        dp_ref[...] = (dot_t(low2, get(wo)[...]) * get(dg)[...].astype(F32)).astype(BF16)
        put(dp_ref, g)
    total = dot_t(staged[0][...], get(WIA)[...]) + dot_t(staged[1][...], get(WIB)[...])
    if not last:
        staged[2][...] = total + get(ACC)[...]
        put(staged[2], 2)
        return
    R1, FG = 8, 9
    dr1_ref, low_ref, sums_ref = staged[2:]
    dhid = total + get(ACC)[...]
    normed, inverse = row_stats(get(R1)[...])
    dr1 = norm_back(dhid * lanes_of(get(FG)), normed, inverse)
    low = dr1.astype(BF16)
    low_ref[...] = low
    put(low_ref, 3)
    half = low_ref.shape[1] // 2
    put(low_ref.at[:, strip(1 - place.core, half)], 4)
    dr1_ref[...] = dr1
    put(dr1_ref, 2)
    sums_ref[0:1, :] = jnp.sum(dhid * normed, 0, keepdims=True)
    sums_ref[1:2, :] = jnp.sum(dhid, 0, keepdims=True)
    sums_ref[2:3, :] = jnp.sum(low.astype(F32), 0, keepdims=True)
    put(sums_ref, 5)


def attn_bwd_body(width, place, get, staged, put, len_ref):
    LOW, WO, Q, K, V, W, ACC = range(7)
    d_ref, out_ref, dc_ref = staged
    dc_ref[...] = dot_t(get(LOW)[...], get(WO)[...]).astype(BF16)
    q_ref, k_ref, v_ref = get(Q), get(K), get(V)
    chains = len_ref.shape[0]
    slots = q_ref.shape[0] // chains
    first = lax.broadcasted_iota(jnp.int32, (slots, PAIR), 1) < HDIM
    spot = lax.broadcasted_iota(jnp.int32, (slots, 2 * slots), 0)

    def heads_apart(v):
        return jnp.concatenate([jnp.where(first, v, 0), jnp.where(first, 0, v)], 0)

    for chain in range(chains):
        rows = slice(chain * slots, (chain + 1) * slots)
        valid = spot < len_ref[chain]
        for at in range(0, width, PAIR):
            k = k_ref[rows, at : at + PAIR]
            q_both = heads_apart(q_ref[rows, at : at + PAIR])
            dc_both = heads_apart(dc_ref[rows, at : at + PAIR])
            scores = jnp.where(valid, dot_t(k, q_both) * SCALING, -1e30)
            grown = jnp.exp(scores - jnp.max(scores, 0, keepdims=True))
            probs = grown * (1.0 / jnp.sum(grown, 0, keepdims=True))
            dprobs = dot_t(v_ref[rows, at : at + PAIR], dc_both)
            dscores = (probs * (dprobs - jnp.sum(probs * dprobs, 0, keepdims=True))).astype(BF16)
            dq = dot_rows(dscores, k)
            dq = jnp.where(first, dq[:slots], dq[slots:])
            d_ref[rows, at : at + PAIR] = (dq * SCALING).astype(BF16)
            d_ref[rows, width + at : width + at + PAIR] = (dot(dscores, q_both) * SCALING).astype(BF16)
            d_ref[rows, 2 * width + at : 2 * width + at + PAIR] = dot(probs.astype(BF16), dc_both).astype(BF16)
        put(d_ref.at[rows], 0, rows)
    out_ref[...] = get(ACC)[...] + dot_t(d_ref[...], get(W)[...])
    put(out_ref, 1)


def block_index(order, stage, m, mine, place):
    left = [d for d in "tyz" if d not in order[:stage]]
    rest = [d for d in left if d != order[stage]]
    here = {"t": 0, "y": place.y, "z": place.z}[order[stage]]
    index = 0
    for d in left:
        if d == order[stage]:
            bit = here if mine else 1 - here
        else:
            bit = (m >> (len(rest) - 1 - rest.index(d))) & 1
        index = index * 2 + bit
    return index


def split_index(orders, stage, m, mine, place):
    a, b = (block_index(order, stage, m, mine, place) for order in orders)
    return a + place.core * (b - a)


def put_split(orders, staged, put, place):
    count = staged.shape[0] // 2
    for mine in (False, True):
        for m in range(count):
            put(staged.at[split_index(orders, 0, m, mine, place)], int(mine), m)


def outer_grad_body(orders, place, get, staged, put):
    LOW, LOW_NBR = 0, 1
    g_ref = staged[0]
    size = g_ref.shape[1]
    for t in range(2):
        grad = dot_rows(get(2 + 2 * t)[...], get(LOW)[...]) + dot_rows(get(3 + 2 * t)[...], get(LOW_NBR)[...])
        for b in range(4):
            g_ref[4 * t + b] = grad[b * size : (b + 1) * size].astype(BF16)
    put_split(orders, g_ref, put, place)


def inner_grad_body(orders, place, get, staged, put):
    HID, HID_NBR, LOW, LOW_NBR = range(4)
    g_ref, sums_ref = staged
    for t in range(2):
        dp, dp_nbr, ctx, ctx_nbr = (get(4 + 4 * t + i) for i in range(4))
        grad = dot_rows(get(HID)[...], dp[...]) + dot_rows(get(HID_NBR)[...], dp_nbr[...])
        out = dot_rows(ctx[...], get(LOW)[...]) + dot_rows(ctx_nbr[...], get(LOW_NBR)[...])
        size, piece = grad.shape[0] // 4, out.shape[0] // 8
        for b in range(4):
            g_ref[4 * t + b, :size, :] = grad[b * size : (b + 1) * size].astype(BF16)
            for side in range(2):
                at = (2 * b + side) * piece
                lanes = slice(side * out.shape[1], (side + 1) * out.shape[1])
                g_ref[4 * t + b, size:, lanes] = out[at : at + piece].astype(BF16)
        sums_ref[t : t + 1, :] = jnp.sum(dp[...].astype(F32), 0, keepdims=True) + jnp.sum(
            dp_nbr[...].astype(F32), 0, keepdims=True
        )
    put_split(orders, g_ref, put, place)
    put(sums_ref, 2)


def attn_grad_body(orders, place, get, staged, put):
    X, X_NBR, UNITS, SUMS2, SUMS2_NBR, SUMS1, SUMS1_NBR = range(7)
    (g_ref,) = staged
    size = g_ref.shape[1]
    wide = g_ref.shape[2] - 128
    width = wide // 3
    shared = [get(SUMS2)[i : i + 1, :] + get(SUMS2_NBR)[i : i + 1, :] for i in range(3)]
    shared += [get(SUMS1)[i : i + 1, :] + get(SUMS1_NBR)[i : i + 1, :] for i in range(3)]
    for t in range(2):
        d, d_nbr = get(7 + 2 * t)[...], get(8 + 2 * t)[...]
        grad = dot_rows(get(X)[...], d) + dot_rows(get(X_NBR)[...], d_nbr)
        for b in range(4):
            g_ref[4 * t + b, :, :wide] = grad[b * size : (b + 1) * size].astype(BF16)
            g_ref[4 * t + b, :, wide:] = jnp.zeros((size, 128), BF16)
        total = jnp.sum(d.astype(F32), 0, keepdims=True) + jnp.sum(d_nbr.astype(F32), 0, keepdims=True)
        rows = [*shared, total[:, :width], total[:, 2 * width :], get(UNITS)[t : t + 1, :]]
        flat = jnp.concatenate(
            [row[:, i : i + 128] for row in rows for i in range(0, row.shape[1], 128)], 0
        )
        g_ref[4 * t, : flat.shape[0], wide:] = flat.astype(BF16)
    put_split(orders, g_ref, put, place)


def halve_body(place, get, staged, put):
    kept, recv = get(0), get(1)
    count = kept.shape[0] // 2
    sums = staged[0]
    sums[...] = (kept[...].astype(F32) + recv[...].astype(F32)).astype(BF16)
    put(sums.at[:count], 0)
    put(sums.at[count:], 1)


def add_body(place, get, staged, put):
    staged[0][...] = (get(0)[...].astype(F32) + get(1)[...].astype(F32)).astype(BF16)
    put(staged[0], 0)


def piece_index(i, place):
    core = place.core if i < 4 else 1 - place.core
    y = place.y if i % 4 in (0, 2) else 1 - place.y
    z = place.z if i % 4 in (0, 1) else 1 - place.z
    return core, y, z


def outer_out_body(place, get, staged, put):
    for i in range(8):
        core, y, z = piece_index(i, place)
        ref = staged[i]
        ref[...] = get(i)[0].astype(F32)
        put(ref, 0, (strip(4 * core + 2 * y + z, ref.shape[0]), slice(None)))


def inner_out_body(size, place, get, staged, put):
    for i in range(8):
        core, y, z = piece_index(i, place)
        ref = staged[i]
        ref[...] = get(i)[0].astype(F32)
        wide = ref.shape[1]
        block = 2 * y + z
        put(ref.at[:size], 0, (strip(block, size), strip(core, wide)))
        piece = ref.shape[0] - size
        for side in range(2):
            put(
                ref.at[size:, side * (wide // 2) : (side + 1) * (wide // 2)],
                1,
                (strip(2 * block + side, piece), strip(core, wide // 2)),
            )


def attn_out_body(place, get, staged, put):
    for i in range(8):
        core, y, z = piece_index(i, place)
        ref = staged[i]
        ref[...] = get(i)[0].astype(F32)
        size, wide = ref.shape[0], ref.shape[1] - 128
        rows = strip(4 * core + 2 * y + z, size)
        for part in range(3):
            put(ref.at[:, part * (wide // 3) : (part + 1) * (wide // 3)], part, (rows, slice(None)))
        put(ref.at[:, wide:], 3, (rows, slice(None)))


def local(
    dp,
    inputs,
    lengths,
    query_weight,
    query_bias,
    key_weight,
    value_weight,
    value_bias,
    output_weight,
    output_bias,
    first_gain,
    first_shift,
    inner_weight,
    inner_bias,
    outer_weight,
    outer_bias,
    second_gain,
    second_shift,
    cotangent,
):
    chains, slots, model = inputs.shape
    rows = chains * slots
    width = query_weight.shape[1]
    units = inner_weight.shape[1]
    group = units // 2
    half = model // 2
    levels = int(math.log2(dp))
    line = Line()

    def bit_swap(v, bit):
        return lax.ppermute(v, "dp", [(i, i ^ (1 << bit)) for i in range(dp)])

    def core_swap(v):
        return bit_swap(v, 0)

    def y_swap(v):
        return bit_swap(v, 1)

    def z_swap(v):
        return bit_swap(v, 2)

    def x_swap(v):
        return lax.ppermute(v, "tensor", [(0, 1), (1, 0)])

    def order_swap(v, orders, stage):
        pairs = []
        for spot in range(dp):
            for t in range(2):
                d = orders[spot % 2][stage]
                to = (spot, 1 - t) if d == "t" else (spot ^ (2 if d == "y" else 4), t)
                pairs.append((2 * spot + t, 2 * to[0] + to[1]))
        return lax.ppermute(v, ("dp", "tensor"), pairs)

    x = inputs.reshape(rows, model)
    lens = lax.dynamic_slice_in_dim(lengths, lax.axis_index("tensor") * chains, chains, 0)
    cot = cotangent.reshape(rows, model)

    quarter = model // 4
    eighth = units // 8

    def pack(place, get, staged, put):
        for i in range(len(packed_loads)):
            put(get(i), *packed_to[i])

    def piece(arr, dims, src):
        return Load(dims, arr.dtype, [(arr, src, None)])

    all_rows = slice(None)
    packed_loads = [
        *(
            piece(w, (quarter, width), lambda p: (strip(2 * p.core + p.y, quarter), all_rows))
            for w in (query_weight, key_weight, value_weight)
        ),
        piece(output_weight, (width // 2, half), lambda p: (strip(p.y, width // 2), strip(p.core, half))),
        piece(inner_weight, (model, group // 2), lambda p: (all_rows, strip(2 * p.core + p.z, group // 2))),
        piece(outer_weight, (eighth, model), lambda p: (strip(4 * p.core + p.y, eighth), all_rows)),
        piece(outer_weight, (eighth, model), lambda p: (strip(4 * p.core + 2 + p.z, eighth), all_rows)),
        load(query_bias), load(value_bias), load(inner_bias),
        piece(x, (rows, half), lambda p: (all_rows, strip(1 - p.core, half))),
    ]
    packed_to = [
        (0, (all_rows, slice(0, width))),
        (0, (all_rows, slice(width, 2 * width))),
        (0, (all_rows, slice(2 * width, 3 * width))),
        (1,), (2,), (3,), (4,),
        (5, slice(0, width)),
        (5, slice(width, 2 * width)),
        (5, slice(2 * width, 2 * width + units)),
        (6,),
    ]
    qkv_cut, out_cut, wi_cut, woa_cut, wob_cut, biases, x_send = line(
        "pack", pack, packed_loads,
        [
            ((quarter, 3 * width), BF16), ((width // 2, half), BF16), ((model, group // 2), BF16),
            ((eighth, model), BF16), ((eighth, model), BF16), ((2 * width + units,), F32), ((rows, half), BF16),
        ],
    )
    biases_oth = x_swap(biases)
    qkv_mine = x_swap(qkv_cut)
    out_mine = x_swap(out_cut)
    wi_mine = x_swap(wi_cut)
    woa_mine = x_swap(woa_cut)
    wob_mine = x_swap(wob_cut)
    x_nbr = core_swap(x_send)

    def relay(name, *arrs):
        def body(place, get, staged, put):
            for i in range(len(arrs)):
                put(get(i), i)

        return line(name, body, [load(a) for a in arrs], [(a.shape, a.dtype) for a in arrs])

    def bias_part(at, size, own):
        if own is not None:
            return load(own)
        return Load((size,), F32, [(biases_oth, lambda p: (pl.ds(at, size),), None)])

    w_own = Load(
        (model, 3 * width), BF16,
        [
            (w, None, lambda p, i=i: (all_rows, slice(i * width, (i + 1) * width)))
            for i, w in enumerate((query_weight, key_weight, value_weight))
        ],
    )
    low_width = ((rows, width), BF16)
    low_wide = ((rows, model), BF16)
    wide = ((rows, model), F32)
    act = ((rows, group), BF16)
    sums_shape = ((8, model), F32)

    q_own, k_own, v_own, ctx_own, part_own = line(
        "attn_fwd_own", lambda *a: attn_fwd_body(False, width, *a),
        [load(x), w_own, load(query_bias), load(value_bias), load(output_weight)],
        [low_width] * 4 + [wide], [low_width] * 4 + [wide], smem=[lens],
    )
    (qkv_mine,) = relay("relay_qkv", qkv_mine)
    qkv_y = y_swap(qkv_mine)
    out_y = y_swap(out_mine)
    (wi_mine,) = relay("relay_wi", wi_mine)
    wi_z = z_swap(wi_mine)

    def corners(p, a, b):
        return [(p.core, a), (p.core, 1 - a), (1 - p.core, a), (1 - p.core, 1 - a)][b]

    def four(mine, nbr):
        return [mine, nbr, core_swap(mine), core_swap(nbr)]

    w_oth = Load(
        (model, 3 * width), BF16,
        [
            (v, None, lambda p, i=i: (strip(2 * corners(p, p.y, i)[0] + corners(p, p.y, i)[1], quarter), all_rows))
            for i, v in enumerate(four(qkv_mine, qkv_y))
        ],
    )
    wo_attn_oth = Load(
        (width, model), BF16,
        [
            (v, None, lambda p, i=i: (strip(corners(p, p.y, i)[1], width // 2), strip(corners(p, p.y, i)[0], half)))
            for i, v in enumerate(four(out_mine, out_y))
        ],
    )
    q_oth, k_oth, v_oth, ctx_oth, r1, hid = line(
        "attn_fwd_oth", lambda *a: attn_fwd_body(True, width, *a),
        [
            load(x), w_oth, bias_part(0, width, None), bias_part(width, width, None), wo_attn_oth,
            load(part_own), load(output_bias), load(first_gain), load(first_shift),
        ],
        [low_width] * 4 + [wide, low_wide], [low_width] * 4 + [wide, low_wide], smem=[lens],
    )
    woa_mine, wob_mine = relay("relay_wo", woa_mine, wob_mine)
    woa_y = y_swap(woa_mine)
    wob_z = z_swap(wob_mine)

    def wi_own(flip):
        return piece(inner_weight, (model, group), lambda p: (all_rows, strip((1 - p.core) if flip else p.core, group)))

    def wo_own(flip):
        return piece(outer_weight, (group, model), lambda p: (strip((1 - p.core) if flip else p.core, group), all_rows))

    def bi_own(flip):
        return piece(inner_bias, (group,), lambda p: (strip((1 - p.core) if flip else p.core, group),))

    def bi_oth(flip):
        return piece(
            biases_oth, (group,),
            lambda p: (pl.ds(pl.multiple_of(2 * width + ((1 - p.core) if flip else p.core) * group, group), group),),
        )

    def wi_oth(pair):
        return Load(
            (model, group), BF16,
            [
                (pair[0], None, lambda p: (all_rows, strip(p.z, group // 2))),
                (pair[1], None, lambda p: (all_rows, strip(1 - p.z, group // 2))),
            ],
        )

    def wo_oth(pieces):
        return Load(
            (group, model), BF16,
            [
                (pieces[0], None, lambda p: (strip(p.y, eighth), all_rows)),
                (pieces[1], None, lambda p: (strip(1 - p.y, eighth), all_rows)),
                (pieces[2], None, lambda p: (strip(2 + p.z, eighth), all_rows)),
                (pieces[3], None, lambda p: (strip(3 - p.z, eighth), all_rows)),
            ],
        )

    acta_own, dga_own, actb_own, dgb_own, ffn_own = line(
        "ffn_fwd_own", lambda *a: ffn_fwd_body(False, *a),
        [load(hid), wi_own(True), bi_own(True), wi_own(False), bi_own(False), wo_own(True), wo_own(False)],
        [act] * 4 + [wide], [act] * 4 + [wide],
    )
    wi_b = wi_oth([wi_mine, wi_z])
    wi_a = wi_oth([core_swap(wi_mine), core_swap(wi_z)])
    wo_pieces = [woa_mine, woa_y, wob_mine, wob_z]
    wo_b = wo_oth(wo_pieces)
    wo_a = wo_oth([core_swap(v) for v in wo_pieces])
    acta_oth, dga_oth, actb_oth, dgb_oth, result, dr2, low2, sums2 = line(
        "ffn_fwd_oth", lambda *a: ffn_fwd_body(True, *a),
        [
            load(hid), wi_a, bi_oth(True), wi_b, bi_oth(False), wo_a, wo_b,
            load(ffn_own), load(r1), load(first_gain), load(first_shift), load(outer_bias),
            load(second_gain), load(second_shift), load(cot),
        ],
        [act] * 4 + [low_wide, wide, low_wide, sums_shape],
        [act] * 4 + [low_wide, wide, low_wide, sums_shape],
    )

    low2_nbr = core_swap(low2)
    hid_nbr = core_swap(hid)
    acta_own_nbr, acta_oth_nbr = core_swap(acta_own), core_swap(acta_oth)
    ctx_own_nbr, ctx_oth_nbr = core_swap(ctx_own), core_swap(ctx_oth)
    sums2_nbr = core_swap(sums2)

    dpa_oth, dpb_oth, back = line(
        "ffn_bwd_oth", lambda *a: ffn_bwd_body(False, *a),
        [load(low2), wo_a, load(dga_oth), wo_b, load(dgb_oth), wi_a, wi_b, load(dr2)],
        [act] * 2 + [wide], [act] * 2 + [wide],
    )

    def split_outs(dims):
        return [((4, *dims), BF16), ((4, *dims), BF16)]

    outer_dims = (group // 4, model)
    inner_dims = (model // 4 + width // 8, group)
    attn_dims = (half // 4, 3 * width + 128)
    send, outer_kept = line(
        "outer_grad", lambda *a: outer_grad_body(ORDERS["outer"], *a),
        [load(low2), load(low2_nbr), load(actb_own), load(acta_own_nbr), load(actb_oth), load(acta_oth_nbr)],
        split_outs(outer_dims), [((8, *outer_dims), BF16)],
    )
    outer_recv = order_swap(send, ORDERS["outer"], 0)
    dpa_own, dpb_own, dr1, low1, low1_send, sums1 = line(
        "ffn_bwd_own", lambda *a: ffn_bwd_body(True, *a),
        [
            load(low2), wo_own(True), load(dga_own), wo_own(False), load(dgb_own), wi_own(True), wi_own(False),
            load(back), load(r1), load(first_gain),
        ],
        [act] * 2 + [wide, low_wide, ((rows, half), BF16), sums_shape],
        [act] * 2 + [wide, low_wide, sums_shape],
    )
    sums1_nbr = core_swap(sums1)
    send, inner_kept, unit_sums = line(
        "inner_grad", lambda *a: inner_grad_body(ORDERS["inner"], *a),
        [
            load(hid), load(hid_nbr),
            piece(low1, (rows, half), lambda p: (all_rows, strip(p.core, half))), load(core_swap(low1_send)),
            load(dpb_own), load(core_swap(dpa_own)), load(ctx_own), load(ctx_own_nbr),
            load(dpb_oth), load(core_swap(dpa_oth)), load(ctx_oth), load(ctx_oth_nbr),
        ],
        split_outs(inner_dims) + [((8, group), F32)], [((8, *inner_dims), BF16), ((8, group), F32)],
    )
    inner_recv = order_swap(send, ORDERS["inner"], 0)

    def halve(name, stage, kept, recv):
        orders = ORDERS[name]
        count = kept.shape[0]
        dims = kept.shape[1:]

        def parts(arr):
            return Load(
                arr.shape, BF16,
                [
                    (
                        arr,
                        lambda p, m=m, mine=mine: split_index(orders, stage, m, mine, p),
                        lambda p, at=m + (count // 2 if mine else 0): at,
                    )
                    for mine in (False, True)
                    for m in range(count // 2)
                ],
            )

        out = ((count // 2, *dims), BF16)
        sent, kept = line(
            f"{name}_sum{stage}", halve_body, [parts(kept), parts(recv)], [out, out], [(kept.shape, BF16)]
        )
        return order_swap(sent, orders, stage), kept

    def add(name, a, b):
        (total,) = line(name, add_body, [load(a), load(b)], [(a.shape, BF16)], [(a.shape, BF16)])
        return total

    def spread(total):
        over_y, over_z = y_swap(total), z_swap(total)
        pieces = [total, over_y, over_z, y_swap(over_z)]
        return [load(v) for v in pieces + [core_swap(v) for v in pieces]]

    def attn_bwd(name, qkv, wo, w, acc):
        return line(
            name, lambda *a: attn_bwd_body(width, *a),
            [load(low1), wo, *(load(v) for v in qkv), w, load(acc)],
            [((rows, 3 * width), BF16), wide],
            [((rows, 3 * width), BF16), wide, low_width], smem=[lens],
        )

    d_oth, back_in = attn_bwd("attn_bwd_oth", (q_oth, k_oth, v_oth), wo_attn_oth, w_oth, dr1)
    outer_recv, outer_kept = halve("outer", 1, outer_kept, outer_recv)
    d_own, grad_inputs = attn_bwd("attn_bwd_own", (q_own, k_own, v_own), load(output_weight), w_own, back_in)
    outer_recv, outer_kept = halve("outer", 2, outer_kept, outer_recv)
    send, attn_kept = line(
        "attn_grad", lambda *a: attn_grad_body(ORDERS["attn"], *a),
        [
            piece(x, (rows, half), lambda p: (all_rows, strip(p.core, half))), load(x_nbr), load(unit_sums),
            load(sums2), load(sums2_nbr), load(sums1), load(sums1_nbr),
            load(d_own), load(core_swap(d_own)), load(d_oth), load(core_swap(d_oth)),
        ],
        split_outs(attn_dims), [((8, *attn_dims), BF16)],
    )
    attn_recv = order_swap(send, ORDERS["attn"], 0)
    inner_recv, inner_kept = halve("inner", 1, inner_kept, inner_recv)
    outer = add("outer_sum3", outer_kept, outer_recv)
    for bit in range(3, levels):
        outer = add(f"outer_level{bit}", outer, bit_swap(outer, bit))
    outer_pieces = spread(outer)
    attn_recv, attn_kept = halve("attn", 1, attn_kept, attn_recv)
    inner_recv, inner_kept = halve("inner", 2, inner_kept, inner_recv)
    attn_recv, attn_kept = halve("attn", 2, attn_kept, attn_recv)
    inner = add("inner_sum3", inner_kept, inner_recv)
    for bit in range(3, levels):
        inner = add(f"inner_level{bit}", inner, bit_swap(inner, bit))
    inner_pieces = spread(inner)
    attn = add("attn_sum3", attn_kept, attn_recv)
    for bit in range(3, levels):
        attn = add(f"attn_level{bit}", attn, bit_swap(attn, bit))
    attn_pieces = spread(attn)

    def floats(dims):
        return [(dims, F32)] * 8

    (grad_outer,) = line("outer_out", outer_out_body, outer_pieces, [((units, model), F32)], floats(outer_dims))
    grad_inner, grad_out = line(
        "inner_out", lambda *a: inner_out_body(model // 4, *a), inner_pieces,
        [((model, units), F32), ((width, model), F32)], floats(inner_dims),
    )
    grad_q, grad_k, grad_v, sums = line(
        "attn_out", attn_out_body, attn_pieces,
        [((model, width), F32)] * 3 + [((model, 128), F32)], floats(attn_dims), n_out=32,
    )
    flat = sums[: (6 * model + 2 * width + group) // 128].reshape(-1)
    flat_two = sums[half : half + (6 * model + 2 * width + group) // 128].reshape(-1)
    parts = []
    at = 0
    for size in [model] * 6 + [width, width]:
        parts.append(flat[at : at + size])
        at += size
    g_sg, g_ss, g_ob2, g_fg, g_fs, g_ob1, g_qb, g_vb = parts
    g_ib = jnp.concatenate([flat[at : at + group], flat_two[at : at + group]])

    def back_to(v):
        return v.reshape(chains, slots, model)

    return (
        back_to(result), back_to(grad_inputs),
        grad_q, g_qb, grad_k, grad_v, g_vb, grad_out, g_ob1, g_fg, g_fs,
        grad_inner, g_ib, grad_outer, g_ob2, g_sg, g_ss,
    )


def solution(mesh):
    dp = mesh.shape["dp"]
    in_specs = (
        P(("dp", "tensor"), None, None),
        P("dp"),
        P(None, "tensor"),
        P("tensor"),
        P(None, "tensor"),
        P(None, "tensor"),
        P("tensor"),
        P("tensor", None),
        P(),
        P(),
        P(),
        P(None, "tensor"),
        P("tensor"),
        P("tensor", None),
        P(),
        P(),
        P(),
        P(("dp", "tensor"), None, None),
    )
    out_specs = (
        P(("dp", "tensor"), None, None),
        P(("dp", "tensor"), None, None),
        P(None, "tensor"),
        P("tensor"),
        P(None, "tensor"),
        P(None, "tensor"),
        P("tensor"),
        P("tensor", None),
        P(),
        P(),
        P(),
        P(None, "tensor"),
        P("tensor"),
        P("tensor", None),
        P(),
        P(),
        P(),
    )

    def run(*args):
        return local(dp, *args)

    return jax.shard_map(run, mesh=mesh, in_specs=in_specs, out_specs=out_specs, check_vma=False)
```

```python
import math
from typing import NamedTuple

import jax
import jax.numpy as jnp
from jax import lax
from jax.experimental import pallas as pl
from jax.experimental.pallas import tpu as pltpu
from jax.sharding import PartitionSpec as P

HDIM = 64
PAIR = 2 * HDIM
SCALING = 1.0 / math.sqrt(HDIM)
LONG = 3 * 10**10
SHORT = 5 * 10**9
ROWS = 320
BF16 = jnp.bfloat16
F32 = jnp.float32

ORDERS = {"outer": ("zty", "zyt"), "inner": ("tyz", "ytz"), "attn": ("tyz", "ytz")}


def dot(a, b):
    return lax.dot_general(a, b, (((1,), (0,)), ((), ())), preferred_element_type=F32)


def dot_t(a, b):
    return lax.dot_general(a, b, (((1,), (1,)), ((), ())), preferred_element_type=F32)


def dot_rows(a, b):
    return lax.dot_general(a, b, (((0,), (0,)), ((), ())), preferred_element_type=F32)


def row_stats(rows):
    center = rows - jnp.mean(rows, -1, keepdims=True)
    inverse = lax.rsqrt(jnp.mean(center * center, -1, keepdims=True) + 1e-05)
    return center * inverse, inverse


def norm_back(scaled, normed, inverse):
    return inverse * (
        scaled
        - jnp.mean(scaled, -1, keepdims=True)
        - normed * jnp.mean(scaled * normed, -1, keepdims=True)
    )


def lanes_of(ref):
    return ref[...].reshape(1, -1)


def strip(index, size, base=0):
    return pl.ds(pl.multiple_of(base + index * size, size), size)


class Place(NamedTuple):
    core: jax.Array
    y: jax.Array
    z: jax.Array
    t: jax.Array


class Load(NamedTuple):
    shape: tuple
    dtype: jnp.dtype
    parts: list


def load(arr):
    return Load(arr.shape, arr.dtype, [(arr, None, None)])


def piece(arr, dims, src):
    return Load(dims, arr.dtype, [(arr, src, None)])


def view(ref, at, place):
    return ref if at is None else ref.at[at(place)]


class Line:
    def __init__(self):
        self.token = []

    def __call__(self, name, body, loads, outs, hbm=(), hbm_outs=(), scratch=(), smem=(), copies=8, vmem=24, cost=0):
        parts = [part for item in loads for part in item.parts]
        copied = [item for item in loads if len(item.parts) > 1 or len(item.shape) == 1 and item.parts[0][1]]
        n_copied = sum(len(item.parts) for item in copied)
        n_token = len(self.token)

        def run(*refs):
            refs = list(refs)

            def take(count):
                got = refs[:count]
                del refs[:count]
                return got

            hbm_refs, part_refs = take(len(hbm)), take(len(parts))
            take(n_token)
            out_refs, hbm_out_refs, (token_ref,) = take(len(outs)), take(len(hbm_outs)), take(1)
            joined, scratch_refs, smem_refs = take(len(copied)), take(len(scratch)), take(len(smem))
            in_sem, out_sem = refs
            spot = lax.axis_index("dp")
            place = Place(
                lax.rem(spot, 2), lax.rem(spot // 2, 2), lax.rem(spot // 4, 2), lax.axis_index("tensor")
            )
            ready, pending = [], []
            sem = 0
            for item in loads:
                own = [part_refs.pop(0) for _ in item.parts]
                waits = []
                if any(item is c for c in copied):
                    ref = joined.pop(0)
                    for src_ref, (_, src, dst) in zip(own, item.parts):
                        waits.append(
                            pltpu.make_async_copy(
                                view(src_ref, src, place), view(ref, dst, place), in_sem.at[sem]
                            )
                        )
                        waits[-1].start()
                        sem += 1
                else:
                    ref = view(own[0], item.parts[0][1], place)
                ready.append(ref)
                pending.append(waits)
            stores, waited = [], []

            def wait(*copies):
                for copy in copies:
                    copy.wait()
                    waited.append(copy)

            def get(i):
                for copy in pending[i]:
                    copy.wait()
                pending[i] = []
                return ready[i]

            def put(src, dst):
                copy = pltpu.make_async_copy(src, dst, out_sem.at[len(stores)])
                copy.start()
                stores.append(copy)
                return copy

            body(place, get, [*out_refs, *scratch_refs], put, wait, hbm_refs, hbm_out_refs, *smem_refs)
            token_ref[...] = jnp.zeros(token_ref.shape, F32)
            for i in range(len(loads)):
                get(i)
            for copy in stores:
                if all(copy is not done for done in waited):
                    copy.wait()

        in_vmem = pl.BlockSpec(memory_space=pltpu.VMEM)
        in_hbm = pl.BlockSpec(memory_space=pltpu.HBM)
        *results, token = pl.pallas_call(
            run,
            out_shape=[jax.ShapeDtypeStruct(s, d) for s, d in [*outs, *hbm_outs, ((8, 128), F32)]],
            in_specs=[in_hbm] * len(hbm)
            + [in_vmem] * (len(parts) + n_token),
            out_specs=[in_vmem] * len(outs) + [in_hbm] * len(hbm_outs) + [in_vmem],
            scratch_shapes=[pltpu.VMEM(item.shape, item.dtype) for item in copied]
            + [pltpu.VMEM(s, d) for s, d in scratch]
            + [pltpu.SMEM(s, d) for s, d in smem]
            + [pltpu.SemaphoreType.DMA((max(n_copied, 1),)), pltpu.SemaphoreType.DMA((copies,))],
            compiler_params=pltpu.CompilerParams(vmem_limit_bytes=vmem << 20),
            cost_estimate=pl.CostEstimate(flops=cost, bytes_accessed=0, transcendentals=0),
            name=name,
        )(*hbm, *[arr for arr, _, _ in parts], *self.token)
        self.token = [token]
        return results


def three(get, at, count, width):
    if count == 3:
        return [get(at + i) for i in range(3)]
    return [get(at).at[:, i * width : (i + 1) * width] for i in range(3)]


def heads_apart(v, first):
    return jnp.concatenate([jnp.where(first, v, 0), jnp.where(first, 0, v)], 0)


def attend(q_ref, k_ref, v_ref, ctx_ref, len_ref, len_at, chains):
    slots = q_ref.shape[0] // chains
    first = lax.broadcasted_iota(jnp.int32, (slots, PAIR), 1) < HDIM
    spot = lax.broadcasted_iota(jnp.int32, (slots, 2 * slots), 0)
    for chain in range(chains):
        rows = slice(chain * slots, (chain + 1) * slots)
        valid = spot < len_ref[len_at + chain]
        for at in range(0, q_ref.shape[1], PAIR):
            q_both = heads_apart(q_ref[rows, at : at + PAIR], first)
            scores = jnp.where(valid, dot_t(k_ref[rows, at : at + PAIR], q_both) * SCALING, -1e30)
            grown = jnp.exp(scores - jnp.max(scores, 0, keepdims=True))
            probs = (grown * (1.0 / jnp.sum(grown, 0, keepdims=True))).astype(BF16)
            both = dot_rows(probs, v_ref[rows, at : at + PAIR])
            ctx_ref[rows, at : at + PAIR] = jnp.where(first, both[:slots], both[slots:]).astype(BF16)


def attn_fwd_own_body(chains, place, get, staged, put, wait, hbm, _, len_ref):
    x_ref, wq, wk, wv, wo = staged[:5]
    later = staged[5 : len(hbm) - 3]
    q_ref, k_ref, v_ref, ctx_ref, part_ref, bq, bv = staged[len(hbm) - 3 :]
    lens = put(hbm[-1], len_ref)
    first = [put(hbm[0], x_ref), put(hbm[1], wq), put(hbm[-3], bq)]
    second = [put(hbm[2], wk), put(hbm[3], wv), put(hbm[-2], bv)]
    wait(*first)
    third = put(hbm[4], wo)
    x = x_ref[...]
    q_ref[...] = (dot(x, wq[...]) + lanes_of(bq)).astype(BF16)
    wait(*second)
    for src, dst in zip(hbm[5:-3], later):
        put(src, dst)
    k_ref[...] = dot(x, wk[...]).astype(BF16)
    v_ref[...] = (dot(x, wv[...]) + lanes_of(bv)).astype(BF16)
    wait(lens)
    attend(q_ref, k_ref, v_ref, ctx_ref, len_ref, place.t * chains, chains)
    wait(third)
    part_ref[...] = dot(ctx_ref[...], wo[...])


def attn_fwd_oth_body(chains, width, place, get, staged, put, wait, hbm, _, len_ref):
    X, BQ, BV, WO, ACC, OB, FG, FS, W = range(9)
    q_ref, k_ref, v_ref, ctx_ref, r1_ref, hid_ref = staged
    lens = put(hbm[0], len_ref)
    x = get(X)[...]
    wq, wk, wv = three(get, W, 1, width)
    q_ref[...] = (dot(x, wq[...]) + lanes_of(get(BQ))).astype(BF16)
    k_ref[...] = dot(x, wk[...]).astype(BF16)
    v_ref[...] = (dot(x, wv[...]) + lanes_of(get(BV))).astype(BF16)
    wait(lens)
    attend(q_ref, k_ref, v_ref, ctx_ref, len_ref, place.t * chains, chains)
    r1_ref[...] = dot(ctx_ref[...], get(WO)[...])
    acc_ref, x_ref = get(ACC), get(X)
    bias, gain, shift = lanes_of(get(OB)), lanes_of(get(FG)), lanes_of(get(FS))

    for at in range(0, x.shape[0], ROWS):
        rows = slice(at, at + ROWS)
        r1 = x_ref[rows, :].astype(F32) + (r1_ref[rows, :] + acc_ref[rows, :]) + bias
        r1_ref[rows, :] = r1
        normed, _ = row_stats(r1)
        hid_ref[rows, :] = (normed * gain + shift).astype(BF16)


def ffn_fwd_body(last, place, get, staged, put, *_):
    HID, WIA, BIA, WIB, BIB, WOA, WOB = range(7)
    hid = get(HID)[...]
    for g, (wi, bi) in enumerate(((WIA, BIA), (WIB, BIB))):
        act_ref, dg_ref = staged[2 * g], staged[2 * g + 1]
        pre = dot(hid, get(wi)[...]) + lanes_of(get(bi))
        cdf = 0.5 + 0.5 * lax.erf(pre * math.sqrt(0.5))
        act_ref[...] = (pre * cdf).astype(BF16)
        bell = jnp.exp(pre * pre * -0.5) * (1.0 / math.sqrt(2 * math.pi))
        dg_ref[...] = (cdf + pre * bell).astype(BF16)
    total = dot(staged[0][...], get(WOA)[...]) + dot(staged[2][...], get(WOB)[...])
    if not last:
        staged[4][...] = total
        return
    ACC, R1, FG, FS, OB, SG, SS, COT = range(7, 15)
    out_ref, dr2_ref, low_ref, sums_ref = staged[4:]
    dr2_ref[...] = total
    acc_ref, r1_ref, cot_ref = get(ACC), get(R1), get(COT)
    first_gain, first_shift, bias = lanes_of(get(FG)), lanes_of(get(FS)), lanes_of(get(OB))
    gain, shift = lanes_of(get(SG)), lanes_of(get(SS))
    sums_ref[...] = jnp.zeros(sums_ref.shape, F32)

    for at in range(0, hid.shape[0], ROWS):
        rows = slice(at, at + ROWS)
        normed, _ = row_stats(r1_ref[rows, :])
        r2 = normed * first_gain + first_shift + (dr2_ref[rows, :] + acc_ref[rows, :]) + bias
        normed, inverse = row_stats(r2)
        out_ref[rows, :] = (normed * gain + shift).astype(BF16)
        cot = cot_ref[rows, :].astype(F32)
        dr2 = norm_back(cot * gain, normed, inverse)
        low = dr2.astype(BF16)
        low_ref[rows, :] = low
        dr2_ref[rows, :] = dr2
        for i, v in enumerate((cot * normed, cot, low.astype(F32))):
            sums_ref[8 * i : 8 * i + 8, :] += jnp.sum(v.reshape(-1, 8, v.shape[1]), 0)


def ffn_bwd_body(last, place, get, staged, put, *_):
    LOW, WOA, DGA, WOB, DGB, WIA, WIB, ACC = range(8)
    low2 = get(LOW)[...]
    for g, (wo, dg) in enumerate(((WOA, DGA), (WOB, DGB))):
        dp_ref = staged[g]
        dp_ref[...] = (dot_t(low2, get(wo)[...]) * get(dg)[...].astype(F32)).astype(BF16)
    total = dot_t(staged[0][...], get(WIA)[...]) + dot_t(staged[1][...], get(WIB)[...])
    if not last:
        staged[2][...] = total + get(ACC)[...]
        return
    R1, FG = 8, 9
    dr1_ref, low_ref, send_ref, sums_ref = staged[2:]
    dr1_ref[...] = total
    acc_ref, r1_ref, gain = get(ACC), get(R1), lanes_of(get(FG))
    half = low_ref.shape[1] // 2
    sums_ref[...] = jnp.zeros(sums_ref.shape, F32)

    for at in range(0, low2.shape[0], ROWS):
        rows = slice(at, at + ROWS)
        dhid = dr1_ref[rows, :] + acc_ref[rows, :]
        normed, inverse = row_stats(r1_ref[rows, :])
        dr1 = norm_back(dhid * gain, normed, inverse)
        low = dr1.astype(BF16)
        low_ref[rows, :] = low
        dr1_ref[rows, :] = dr1
        for i, v in enumerate((dhid * normed, dhid, low.astype(F32))):
            sums_ref[8 * i : 8 * i + 8, :] += jnp.sum(v.reshape(-1, 8, v.shape[1]), 0)

    send_ref[...] = low_ref[:, strip(1 - place.core, half)]


def attn_bwd_body(count, chains, width, place, get, staged, put, wait, hbm, _, len_ref):
    LOW, WO, Q, K, V, ACC, W = range(7)
    d_ref, out_ref, dc_ref = staged
    lens = put(hbm[0], len_ref)
    dc_ref[...] = dot_t(get(LOW)[...], get(WO)[...]).astype(BF16)
    q_ref, k_ref, v_ref = get(Q), get(K), get(V)
    slots = q_ref.shape[0] // chains
    first = lax.broadcasted_iota(jnp.int32, (slots, PAIR), 1) < HDIM
    spot = lax.broadcasted_iota(jnp.int32, (slots, 2 * slots), 0)
    wait(lens)
    for chain in range(chains):
        rows = slice(chain * slots, (chain + 1) * slots)
        valid = spot < len_ref[place.t * chains + chain]
        for at in range(0, width, PAIR):
            k = k_ref[rows, at : at + PAIR]
            q_both = heads_apart(q_ref[rows, at : at + PAIR], first)
            dc_both = heads_apart(dc_ref[rows, at : at + PAIR], first)
            scores = jnp.where(valid, dot_t(k, q_both) * SCALING, -1e30)
            grown = jnp.exp(scores - jnp.max(scores, 0, keepdims=True))
            probs = grown * (1.0 / jnp.sum(grown, 0, keepdims=True))
            dprobs = dot_t(v_ref[rows, at : at + PAIR], dc_both)
            dscores = (probs * (dprobs - jnp.sum(probs * dprobs, 0, keepdims=True))).astype(BF16)
            dq = dot_rows(dscores, k)
            dq = jnp.where(first, dq[:slots], dq[slots:])
            d_ref[rows, at : at + PAIR] = (dq * SCALING).astype(BF16)
            d_ref[rows, width + at : width + at + PAIR] = (dot(dscores, q_both) * SCALING).astype(BF16)
            d_ref[rows, 2 * width + at : 2 * width + at + PAIR] = dot(probs.astype(BF16), dc_both).astype(BF16)
    total = get(ACC)[...]
    for i, w in enumerate(three(get, W, count, width)):
        total = total + dot_t(d_ref[:, i * width : (i + 1) * width], w[...])
    out_ref[...] = total


def block_index(order, stage, m, mine, place):
    left = [d for d in "tyz" if d not in order[:stage]]
    rest = [d for d in left if d != order[stage]]
    here = {"t": 0, "y": place.y, "z": place.z}[order[stage]]
    index = 0
    for d in left:
        if d == order[stage]:
            bit = here if mine else 1 - here
        else:
            bit = (m >> (len(rest) - 1 - rest.index(d))) & 1
        index = index * 2 + bit
    return index


def split_index(orders, stage, m, mine, place):
    a, b = (block_index(order, stage, m, mine, place) for order in orders)
    return a + place.core * (b - a)


def give_split(orders, blocks, sent, kept, place):
    for mine, ref in ((False, sent), (True, kept)):
        for m in range(ref.shape[0]):
            ref[m] = blocks[split_index(orders, 0, m, mine, place)]


def outer_grad_body(orders, place, get, staged, put, *_):
    LOW, LOW_NBR = 0, 1
    sent, kept, g_ref = staged
    size = g_ref.shape[1]
    for t in range(2):
        grad = dot_rows(get(2 + 2 * t)[...], get(LOW)[...]) + dot_rows(get(3 + 2 * t)[...], get(LOW_NBR)[...])
        for b in range(4):
            g_ref[4 * t + b] = grad[b * size : (b + 1) * size].astype(BF16)
    give_split(orders, g_ref, sent, kept, place)


def inner_grad_body(orders, place, get, staged, put, *_):
    HID, HID_NBR, LOW, LOW_NBR = range(4)
    sent, kept, sums_ref, g_ref = staged
    for t in range(2):
        dp, dp_nbr, ctx, ctx_nbr = (get(4 + 4 * t + i) for i in range(4))
        grad = dot_rows(get(HID)[...], dp[...]) + dot_rows(get(HID_NBR)[...], dp_nbr[...])
        out = dot_rows(ctx[...], get(LOW)[...]) + dot_rows(ctx_nbr[...], get(LOW_NBR)[...])
        size, piece = grad.shape[0] // 4, out.shape[0] // 8
        for b in range(4):
            g_ref[4 * t + b, :size, :] = grad[b * size : (b + 1) * size].astype(BF16)
            for side in range(2):
                at = (2 * b + side) * piece
                lanes = slice(side * out.shape[1], (side + 1) * out.shape[1])
                g_ref[4 * t + b, size:, lanes] = out[at : at + piece].astype(BF16)
        sums_ref[t : t + 1, :] = jnp.sum(dp[...].astype(F32), 0, keepdims=True) + jnp.sum(
            dp_nbr[...].astype(F32), 0, keepdims=True
        )
    give_split(orders, g_ref, sent, kept, place)


def attn_grad_body(orders, place, get, staged, put, *_):
    X, X_NBR, UNITS, SUMS2, SUMS2_NBR, SUMS1, SUMS1_NBR = range(7)
    sent, kept, g_ref = staged
    size = g_ref.shape[1]
    wide = g_ref.shape[2] - 128
    width = wide // 3
    shared = [
        jnp.sum(get(mine)[8 * i : 8 * i + 8, :] + get(nbr)[8 * i : 8 * i + 8, :], 0, keepdims=True)
        for mine, nbr in ((SUMS2, SUMS2_NBR), (SUMS1, SUMS1_NBR))
        for i in range(3)
    ]
    for t in range(2):
        d, d_nbr = get(7 + 2 * t)[...], get(8 + 2 * t)[...]
        grad = dot_rows(get(X)[...], d) + dot_rows(get(X_NBR)[...], d_nbr)
        for b in range(4):
            g_ref[4 * t + b, :, :wide] = grad[b * size : (b + 1) * size].astype(BF16)
            g_ref[4 * t + b, :, wide:] = jnp.zeros((size, 128), BF16)
        total = jnp.sum(d.astype(F32), 0, keepdims=True) + jnp.sum(d_nbr.astype(F32), 0, keepdims=True)
        rows = [*shared, total[:, :width], total[:, 2 * width :], get(UNITS)[t : t + 1, :]]
        flat = jnp.concatenate(
            [row[:, i : i + 128] for row in rows for i in range(0, row.shape[1], 128)], 0
        )
        g_ref[4 * t, : flat.shape[0], wide:] = flat.astype(BF16)
    give_split(orders, g_ref, sent, kept, place)


def halve_body(orders, stage, place, get, staged, put, *_):
    a, b = get(0), get(1)
    for mine, ref in ((False, staged[0]), (True, staged[1])):
        for m in range(ref.shape[0]):
            k = split_index(orders, stage, m, mine, place)
            ref[m] = (a[k].astype(F32) + b[k].astype(F32)).astype(BF16)


def add_body(place, get, staged, put, *_):
    staged[0][...] = (get(0)[...].astype(F32) + get(1)[...].astype(F32)).astype(BF16)


def join_body(place, get, staged, put, *_):
    for i in range(4):
        y = place.y if i in (0, 2) else 1 - place.y
        z = place.z if i in (0, 1) else 1 - place.z
        staged[0][2 * y + z] = get(i)[0]


def cores(place, get):
    return (place.core, get(0)), (1 - place.core, get(1))


def outer_out_body(place, get, staged, put, _, __, outs):
    for i, (core, ref) in enumerate(cores(place, get)):
        for b in range(4):
            held = staged[4 * i + b]
            held[...] = ref[b].astype(F32)
            put(held, outs[0].at[strip(4 * core + b, held.shape[0]), :])


def inner_out_body(size, place, get, staged, put, _, __, outs):
    for i, (core, ref) in enumerate(cores(place, get)):
        for b in range(4):
            held = staged[4 * i + b]
            held[...] = ref[b].astype(F32)
            wide = held.shape[1]
            piece = held.shape[0] - size
            put(held.at[:size], outs[0].at[b * size : (b + 1) * size, strip(core, wide)])
            for side in range(2):
                at = (2 * b + side) * piece
                put(
                    held.at[size:, side * (wide // 2) : (side + 1) * (wide // 2)],
                    outs[1].at[at : at + piece, strip(core, wide // 2)],
                )


def attn_out_body(place, get, staged, put, _, __, outs):
    for i, (core, ref) in enumerate(cores(place, get)):
        for b in range(4):
            held = staged[4 * i + b]
            held[...] = ref[b].astype(F32)
            size, wide = held.shape[0], held.shape[1] - 128
            rows = strip(4 * core + b, size)
            for part in range(3):
                put(held.at[:, part * (wide // 3) : (part + 1) * (wide // 3)], outs[part].at[rows, :])
            put(held.at[:, wide:], outs[3].at[rows, :])


def local(
    dp,
    inputs,
    lengths,
    query_weight,
    query_bias,
    key_weight,
    value_weight,
    value_bias,
    output_weight,
    output_bias,
    first_gain,
    first_shift,
    inner_weight,
    inner_bias,
    outer_weight,
    outer_bias,
    second_gain,
    second_shift,
    cotangent,
):
    chains, slots, model = inputs.shape
    rows = chains * slots
    width = query_weight.shape[1]
    units = inner_weight.shape[1]
    group = units // 2
    half = model // 2
    levels = int(math.log2(dp))
    line = Line()

    def bit_swap(v, bit):
        return lax.ppermute(v, "dp", [(i, i ^ (1 << bit)) for i in range(dp)])

    def named(swap):
        def run(name, *v):
            with jax.named_scope(name):
                return swap(*v)

        return run

    @named
    def core_swap(v):
        return bit_swap(v, 0)

    @named
    def y_swap(v):
        return bit_swap(v, 1)

    @named
    def z_swap(v):
        return bit_swap(v, 2)

    @named
    def x_swap(v):
        return lax.ppermute(v, "tensor", [(0, 1), (1, 0)])

    @named
    def order_swap(v, orders, stage):
        pairs = []
        for spot in range(dp):
            for t in range(2):
                d = orders[spot % 2][stage]
                to = (spot, 1 - t) if d == "t" else (spot ^ (2 if d == "y" else 4), t)
                pairs.append((2 * spot + t, 2 * to[0] + to[1]))
        return lax.ppermute(v, ("dp", "tensor"), pairs)

    x = inputs.reshape(rows, model)
    cot = cotangent.reshape(rows, model)

    quarter = model // 4
    eighth = units // 8

    all_rows = slice(None)

    def pack(place, get, staged, put, wait, refs, _):
        wq, wk, wv, wo, w_in, w_out, bq, bv, bi, x_ref = refs
        attn_ref, wi_ref, wo_ref, bias_ref, x_out = staged
        core, y, z, _ = place
        for i, w in enumerate((wq, wk, wv)):
            put(w.at[strip(2 * core + y, quarter), :], attn_ref.at[:, i * width : (i + 1) * width])
        put(wo.at[strip(y, quarter), strip(core, half)], attn_ref.at[:, 3 * width :])
        put(w_in.at[:, strip(2 * core + z, group // 2)], wi_ref)
        put(w_out.at[strip(4 * core + y, eighth), :], wo_ref.at[:eighth])
        put(w_out.at[strip(4 * core + 2 + z, eighth), :], wo_ref.at[eighth:])
        put(bq, bias_ref.at[pl.ds(0, width)])
        put(bv, bias_ref.at[pl.ds(width, width)])
        put(bi, bias_ref.at[pl.ds(2 * width, units)])
        put(x_ref.at[:, strip(1 - core, half)], x_out)

    attn_cut, wi_cut, wo_cut, biases, x_send = line(
        "pack", pack, [],
        [
            ((quarter, 3 * width + half), BF16), ((model, group // 2), BF16), ((2 * eighth, model), BF16),
            ((2 * width + units,), F32), ((rows, half), BF16),
        ],
        hbm=[
            query_weight, key_weight, value_weight, output_weight, inner_weight, outer_weight,
            query_bias, value_bias, inner_bias, x,
        ],
        copies=11, vmem=56,
    )
    biases_oth = x_swap("biases_over_x", biases)
    attn_mine = x_swap("attn_over_x", attn_cut)
    wi_mine = x_swap("wi_over_x", wi_cut)
    wo_mine = x_swap("wo_over_x", wo_cut)
    x_nbr = core_swap("x_half", x_send)

    def relay(name, *arrs):
        def body(place, get, staged, put, *_):
            for i, ref in enumerate(staged):
                put(get(i), ref)

        return line(name, body, [load(a) for a in arrs], [(a.shape, a.dtype) for a in arrs])

    def spacer(name, cost=LONG, arrs=()):
        line(name, lambda *_: None, [load(arr) for arr in arrs], [], cost=cost)

    def bias_part(at, size, own):
        if own is not None:
            return load(own)
        return Load((size,), F32, [(biases_oth, lambda p: (pl.ds(at, size),), None)])

    low_width = ((rows, width), BF16)
    low_wide = ((rows, model), BF16)
    wide = ((rows, model), F32)
    act = ((rows, group), BF16)
    sums_shape = ((24, model), F32)

    len_smem = [(lengths.shape, jnp.int32)]
    kept_args = [
        x, query_weight, key_weight, value_weight, output_weight, inner_weight, outer_weight, inner_bias, cot,
        output_bias, first_gain, first_shift, outer_bias, second_gain, second_shift,
    ]
    *kept_args, q_own, k_own, v_own, ctx_own, part_own = line(
        "attn_fwd_own", lambda *a: attn_fwd_own_body(chains, *a), [],
        [(arr.shape, arr.dtype) for arr in kept_args] + [low_width] * 4 + [wide],
        hbm=[*kept_args, query_bias, value_bias, lengths],
        scratch=[(query_bias.shape, F32), (value_bias.shape, F32)], smem=len_smem, copies=len(kept_args) + 3, vmem=44,
    )
    (
        x, query_weight, key_weight, value_weight, output_weight, inner_weight, outer_weight, inner_bias, cot,
        output_bias, first_gain, first_shift, outer_bias, second_gain, second_shift,
    ) = kept_args
    w_own = [load(w) for w in (query_weight, key_weight, value_weight)]
    (attn_mine,) = relay("relay_attn", attn_mine)
    attn_y = y_swap("attn_over_y", attn_mine)
    (wi_mine,) = relay("relay_wi", wi_mine)
    wi_z = z_swap("wi_over_z", wi_mine)
    spacer("spacer_y")
    spacer("spacer_core")

    def corner(p, bit, i):
        return p.core if i < 2 else 1 - p.core, bit if i % 2 == 0 else 1 - bit

    def qkv_part(p, i):
        core, y = corner(p, p.y, i)
        return strip(2 * core + y, quarter), all_rows

    def out_part(p, i):
        core, y = corner(p, p.y, i)
        return strip(y, quarter), strip(core, half)

    attn_pieces = [attn_mine, attn_y, core_swap("attn_core", attn_mine), core_swap("attn_far_core", attn_y)]
    w_oth = Load(
        (model, 3 * width), BF16,
        [
            (v, lambda p: (all_rows, slice(0, 3 * width)), lambda p, i=i: qkv_part(p, i))
            for i, v in enumerate(attn_pieces)
        ],
    )
    wo_attn_oth = Load(
        (width, model), BF16,
        [
            (v, lambda p: (all_rows, slice(3 * width, 3 * width + half)), lambda p, i=i: out_part(p, i))
            for i, v in enumerate(attn_pieces)
        ],
    )
    q_oth, k_oth, v_oth, ctx_oth, r1, hid = line(
        "attn_fwd_oth", lambda *a: attn_fwd_oth_body(chains, width, *a),
        [
            load(x), bias_part(0, width, None), bias_part(width, width, None), wo_attn_oth,
            load(part_own), load(output_bias), load(first_gain), load(first_shift), w_oth,
        ],
        [low_width] * 4 + [wide, low_wide], hbm=[lengths], smem=len_smem,
    )
    woa_mine, wob_mine = line(
        "relay_wo", lambda p, get, staged, put, *_: [put(get(i), staged[i]) for i in range(2)],
        [piece(wo_mine, (eighth, model), lambda p, i=i: (slice(i * eighth, (i + 1) * eighth), all_rows)) for i in range(2)],
        [((eighth, model), BF16)] * 2,
    )
    woa_y = y_swap("woa_over_y", woa_mine)
    wob_z = z_swap("wob_over_z", wob_mine)

    def wi_own(flip):
        return piece(inner_weight, (model, group), lambda p: (all_rows, strip((1 - p.core) if flip else p.core, group)))

    def wo_own(flip):
        return piece(outer_weight, (group, model), lambda p: (strip((1 - p.core) if flip else p.core, group), all_rows))

    def bi_own(flip):
        return piece(inner_bias, (group,), lambda p: (strip((1 - p.core) if flip else p.core, group),))

    def bi_oth(flip):
        return piece(
            biases_oth, (group,),
            lambda p: (pl.ds(pl.multiple_of(2 * width + ((1 - p.core) if flip else p.core) * group, group), group),),
        )

    def wi_oth(pair):
        return Load(
            (model, group), BF16,
            [
                (pair[0], None, lambda p: (all_rows, strip(p.z, group // 2))),
                (pair[1], None, lambda p: (all_rows, strip(1 - p.z, group // 2))),
            ],
        )

    def wo_oth(pieces):
        return Load(
            (group, model), BF16,
            [
                (pieces[0], None, lambda p: (strip(p.y, eighth), all_rows)),
                (pieces[1], None, lambda p: (strip(1 - p.y, eighth), all_rows)),
                (pieces[2], None, lambda p: (strip(2 + p.z, eighth), all_rows)),
                (pieces[3], None, lambda p: (strip(3 - p.z, eighth), all_rows)),
            ],
        )

    acta_own, dga_own, actb_own, dgb_own, ffn_own = line(
        "ffn_fwd_own", lambda *a: ffn_fwd_body(False, *a),
        [load(hid), wi_own(True), bi_own(True), wi_own(False), bi_own(False), wo_own(True), wo_own(False)],
        [act] * 4 + [wide],
    )
    spacer("spacer_wo")
    wi_b = wi_oth([wi_mine, wi_z])
    wi_a = wi_oth([core_swap("wi_core", wi_mine), core_swap("wi_far_core", wi_z)])
    wo_pieces = [woa_mine, woa_y, wob_mine, wob_z]
    wo_b = wo_oth(wo_pieces)
    wo_a = wo_oth([core_swap(f"wo{i}_core", v) for i, v in enumerate(wo_pieces)])
    acta_oth, dga_oth, actb_oth, dgb_oth, result, dr2, low2, sums2 = line(
        "ffn_fwd_oth", lambda *a: ffn_fwd_body(True, *a),
        [
            load(hid), wi_a, bi_oth(True), wi_b, bi_oth(False), wo_a, wo_b,
            load(ffn_own), load(r1), load(first_gain), load(first_shift), load(outer_bias),
            load(second_gain), load(second_shift), load(cot),
        ],
        [act] * 4 + [low_wide, wide, low_wide, sums_shape],
    )

    low2_nbr = core_swap("low2_core", low2)
    hid_nbr = core_swap("hid_core", hid)
    acta_own_nbr, acta_oth_nbr = core_swap("acta_own_core", acta_own), core_swap("acta_oth_core", acta_oth)
    ctx_own_nbr, ctx_oth_nbr = core_swap("ctx_own_core", ctx_own), core_swap("ctx_oth_core", ctx_oth)
    sums2_nbr = core_swap("sums2_core", sums2)

    dpa_oth, dpb_oth, back = line(
        "ffn_bwd_oth", lambda *a: ffn_bwd_body(False, *a),
        [load(low2), wo_a, load(dga_oth), wo_b, load(dgb_oth), wi_a, wi_b, load(dr2)],
        [act] * 2 + [wide],
    )

    dpa_own, dpb_own, dr1, low1, low1_send, sums1 = line(
        "ffn_bwd_own", lambda *a: ffn_bwd_body(True, *a),
        [
            load(low2), wo_own(True), load(dga_own), wo_own(False), load(dgb_own), wi_own(True), wi_own(False),
            load(back), load(r1), load(first_gain),
        ],
        [act] * 2 + [wide, low_wide, ((rows, half), BF16), sums_shape],
    )
    sums1_nbr = core_swap("sums1_core", sums1)

    def split_outs(dims):
        return [((4, *dims), BF16), ((4, *dims), BF16)]

    def halve(name, stage, kept, recv, cost=0):
        orders = ORDERS[name]
        out = ((kept.shape[0] // 2, *kept.shape[1:]), BF16)
        sent, kept = line(
            f"{name}_sum{stage}", lambda *a: halve_body(orders, stage, *a), [load(kept), load(recv)], [out, out], cost=cost
        )
        return kept, order_swap(f"{name}_stage{stage}", sent, orders, stage)

    def add(name, a, b):
        (total,) = line(name, add_body, [load(a), load(b)], [(a.shape, BF16)])
        return total

    def total(name, kept, recv):
        return add(f"{name}_sum3", kept, recv)

    def levelled(name, v):
        for bit in range(3, levels):
            with jax.named_scope(f"{name}_bit{bit}"):
                recv = bit_swap(v, bit)
            v = add(f"{name}_level{bit}", v, recv)
        return v

    def near_far(name, v, over_z):
        far, near = (z_swap, y_swap) if over_z else (y_swap, z_swap)
        return near(f"{name}_near", v), far(f"{name}_far", v)

    def join(name, pieces):
        (joined,) = line(name, join_body, [load(v) for v in pieces], [((4, *pieces[0].shape[1:]), BF16)])
        return [load(joined), load(core_swap(f"{name}_core", joined))]

    def attn_bwd(name, qkv, wo, w, acc):
        return line(
            name, lambda *a: attn_bwd_body(len(w), chains, width, *a),
            [load(low1), wo, *(load(v) for v in qkv), load(acc), *w],
            [((rows, 3 * width), BF16), wide], hbm=[lengths], scratch=[low_width], smem=len_smem,
        )

    outer_dims = (group // 4, model)
    inner_dims = (model // 4 + width // 8, group)
    attn_dims = (half // 4, 3 * width + 128)
    outer_send, outer = line(
        "outer_grad", lambda *a: outer_grad_body(ORDERS["outer"], *a),
        [load(low2), load(low2_nbr), load(actb_own), load(acta_own_nbr), load(actb_oth), load(acta_oth_nbr)],
        split_outs(outer_dims), scratch=[((8, *outer_dims), BF16)],
    )
    outer_recv = order_swap("outer_stage0", outer_send, ORDERS["outer"], 0)
    spacer("spacer_outer0")
    inner_send, inner, unit_sums = line(
        "inner_grad", lambda *a: inner_grad_body(ORDERS["inner"], *a),
        [
            load(hid), load(hid_nbr),
            piece(low1, (rows, half), lambda p: (all_rows, strip(p.core, half))), load(core_swap("low1_send_core", low1_send)),
            load(dpb_own), load(core_swap("dpa_own_core", dpa_own)), load(ctx_own), load(ctx_own_nbr),
            load(dpb_oth), load(core_swap("dpa_oth_core", dpa_oth)), load(ctx_oth), load(ctx_oth_nbr),
        ],
        split_outs(inner_dims) + [((8, group), F32)], scratch=[((8, *inner_dims), BF16)],
    )
    inner_recv = order_swap("inner_stage0", inner_send, ORDERS["inner"], 0)
    d_oth, back_in = attn_bwd("attn_bwd_oth", (q_oth, k_oth, v_oth), wo_attn_oth, [w_oth], dr1)
    d_own, grad_inputs = attn_bwd("attn_bwd_own", (q_own, k_own, v_own), load(output_weight), w_own, back_in)
    outer, outer_recv = halve("outer", 1, outer, outer_recv)
    spacer("spacer_outer1", SHORT)
    inner, inner_recv = halve("inner", 1, inner, inner_recv)
    spacer("spacer_inner1")
    attn_send, attn = line(
        "attn_grad", lambda *a: attn_grad_body(ORDERS["attn"], *a),
        [
            piece(x, (rows, half), lambda p: (all_rows, strip(p.core, half))), load(x_nbr), load(unit_sums),
            load(sums2), load(sums2_nbr), load(sums1), load(sums1_nbr),
            load(d_own), load(core_swap("d_own_core", d_own)), load(d_oth), load(core_swap("d_oth_core", d_oth)),
        ],
        split_outs(attn_dims), scratch=[((8, *attn_dims), BF16)],
    )
    attn_recv = order_swap("attn_stage0", attn_send, ORDERS["attn"], 0)
    outer, outer_recv = halve("outer", 2, outer, outer_recv)
    inner, inner_recv = halve("inner", 2, inner, inner_recv)
    outer = total("outer", outer, outer_recv)
    spacer("spacer_2", 3 * 10**9)
    inner = total("inner", inner, inner_recv)
    attn, attn_recv = halve("attn", 1, attn, attn_recv)
    outer = levelled("outer", outer)
    spacer("spacer_3")
    attn, attn_recv = halve("attn", 2, attn, attn_recv)
    outer_near, outer_far = near_far("outer", outer, False)
    inner = levelled("inner", inner)
    spacer("spacer_4")
    attn = total("attn", attn, attn_recv)
    inner_near, inner_far = near_far("inner", inner, True)
    spacer("seen_outer", 0, [outer_near])
    outer_both = y_swap("outer_both", outer_near)
    spacer("seen_inner", 0, [inner_near])
    inner_both = z_swap("inner_both", inner_near)
    attn = levelled("attn", attn)
    attn_near, attn_far = near_far("attn", attn, True)
    spacer("spacer_5")
    outer_pieces = join("outer_join", [outer, outer_far, outer_near, outer_both])
    inner_pieces = join("inner_join", [inner, inner_near, inner_far, inner_both])
    spacer("seen_attn", LONG, [attn_near])
    attn_both = z_swap("attn_both", attn_near)
    attn_pieces = join("attn_join", [attn, attn_near, attn_far, attn_both])

    def floats(dims):
        return [(dims, F32)] * 8

    (grad_outer,) = line(
        "outer_out", outer_out_body, outer_pieces, [], hbm_outs=[((units, model), F32)], scratch=floats(outer_dims)
    )
    grad_inner, grad_out = line(
        "inner_out", lambda *a: inner_out_body(model // 4, *a), inner_pieces,
        [], hbm_outs=[((model, units), F32), ((width, model), F32)], scratch=floats(inner_dims), copies=24,
    )
    grad_q, grad_k, grad_v, sums = line(
        "attn_out", attn_out_body, attn_pieces,
        [], hbm_outs=[((model, width), F32)] * 3 + [((model, 128), F32)], scratch=floats(attn_dims), copies=32,
    )
    flat = sums[: (6 * model + 2 * width + group) // 128].reshape(-1)
    flat_two = sums[half : half + (6 * model + 2 * width + group) // 128].reshape(-1)
    parts = []
    at = 0
    for size in [model] * 6 + [width, width]:
        parts.append(flat[at : at + size])
        at += size
    g_sg, g_ss, g_ob2, g_fg, g_fs, g_ob1, g_qb, g_vb = parts
    g_ib = jnp.concatenate([flat[at : at + group], flat_two[at : at + group]])

    def back_to(v):
        return v.reshape(chains, slots, model)

    return (
        back_to(result), back_to(grad_inputs),
        grad_q, g_qb, grad_k, grad_v, g_vb, grad_out, g_ob1, g_fg, g_fs,
        grad_inner, g_ib, grad_outer, g_ob2, g_sg, g_ss,
    )


def solution(mesh):
    dp = mesh.shape["dp"]
    in_specs = (
        P(("dp", "tensor"), None, None),
        P("dp"),
        P(None, "tensor"),
        P("tensor"),
        P(None, "tensor"),
        P(None, "tensor"),
        P("tensor"),
        P("tensor", None),
        P(),
        P(),
        P(),
        P(None, "tensor"),
        P("tensor"),
        P("tensor", None),
        P(),
        P(),
        P(),
        P(("dp", "tensor"), None, None),
    )
    out_specs = (
        P(("dp", "tensor"), None, None),
        P(("dp", "tensor"), None, None),
        P(None, "tensor"),
        P("tensor"),
        P(None, "tensor"),
        P(None, "tensor"),
        P("tensor"),
        P("tensor", None),
        P(),
        P(),
        P(),
        P(None, "tensor"),
        P("tensor"),
        P("tensor", None),
        P(),
        P(),
        P(),
    )

    def run(*args):
        return local(dp, *args)

    return jax.shard_map(run, mesh=mesh, in_specs=in_specs, out_specs=out_specs, check_vma=False)
```

```python
import math
from types import SimpleNamespace
from typing import NamedTuple

import jax
import jax.numpy as jnp
from jax import lax
from jax.experimental import pallas as pl
from jax.experimental.pallas import tpu as pltpu
from jax.sharding import PartitionSpec as P

HDIM = 64
PAIR = 2 * HDIM
SCALING = 1.0 / math.sqrt(HDIM)
ORDER = (
    "p1", "p2", "f1", "ra", "rw", "ja", "s8", "s2", "s1", "f2", "ro", "n1", "jw", "jo", "s3", "m2", "n2", "k2",
    "k1", "O0", "I0", "b2", "O1", "b1", "I1", "O2", "s5", "A0", "I2", "O3", "A1", "A2", "I3", "A3", "Ol", "Il",
    "Oj", "s4", "Al", "Ij", "Ow", "Aj", "Iw", "Aw",
)
COSTS = {
    "s1": 300, "s2": 50, "s3": 300, "s4": 300, "s5": 300, "O3": 100, "Aj": 50, "n2": 50, "f2": 100, "ra": 300,
    "b2": 100, "s8": 5, "b1": 10, "A0": 5, "O0": 100, "rw": 15, "Ij": 15, "Il": 5, "Ow": 15, "I1": 15, "A1": 30,
    "A2": 300,
}
ROWS = 320
BF16 = jnp.bfloat16
F32 = jnp.float32

DP, TENSOR = "dp", "tensor"
OUTER, INNER, ATTN = "O", "I", "A"
ORDERS = {OUTER: ("tzy", "zyt"), INNER: ("tzy", "yzt"), ATTN: ("tyz", "yzt")}


def dot(a, b):
    return lax.dot_general(a, b, (((1,), (0,)), ((), ())), preferred_element_type=F32)


def dot_t(a, b):
    return lax.dot_general(a, b, (((1,), (1,)), ((), ())), preferred_element_type=F32)


def dot_rows(a, b):
    return lax.dot_general(a, b, (((0,), (0,)), ((), ())), preferred_element_type=F32)


def row_stats(rows):
    center = rows - jnp.mean(rows, -1, keepdims=True)
    inverse = lax.rsqrt(jnp.mean(center * center, -1, keepdims=True) + 1e-05)
    return center * inverse, inverse


def norm_back(scaled, normed, inverse):
    return inverse * (
        scaled
        - jnp.mean(scaled, -1, keepdims=True)
        - normed * jnp.mean(scaled * normed, -1, keepdims=True)
    )


def lanes_of(ref):
    return ref[...].reshape(1, -1)


def strip(index, size, base=0):
    return pl.ds(pl.multiple_of(base + index * size, size), size)


class Place(NamedTuple):
    core: jax.Array
    y: jax.Array
    z: jax.Array
    t: jax.Array


class Load(NamedTuple):
    shape: tuple
    dtype: jnp.dtype
    parts: list


def load(arr):
    return Load(arr.shape, arr.dtype, [(arr, None, None)])


def piece(arr, dims, src):
    return Load(dims, arr.dtype, [(arr, src, None)])


def view(ref, at, place):
    return ref if at is None else ref.at[at(place)]


class Line:
    def __init__(self):
        self.token = []

    def __call__(self, name, body, loads, outs, hbm=(), hbm_outs=(), scratch=(), smem=(), copies=8, vmem=24,
                 seen=()):
        loads = [*loads, *(load(arr) for arr in seen)]
        parts = [part for item in loads for part in item.parts]
        copied = [item for item in loads if len(item.parts) > 1 or len(item.shape) == 1 and item.parts[0][1]]
        n_copied = sum(len(item.parts) for item in copied)
        n_token = len(self.token)

        def run(*refs):
            refs = list(refs)

            def take(count):
                got = refs[:count]
                del refs[:count]
                return got

            hbm_refs, part_refs = take(len(hbm)), take(len(parts))
            take(n_token)
            out_refs, hbm_out_refs, (token_ref,) = take(len(outs)), take(len(hbm_outs)), take(1)
            joined, scratch_refs, smem_refs = take(len(copied)), take(len(scratch)), take(len(smem))
            in_sem, out_sem = refs
            spot = lax.axis_index(DP)
            place = Place(
                lax.rem(spot, 2), lax.rem(spot // 2, 2), lax.rem(spot // 4, 2), lax.axis_index(TENSOR)
            )
            ready, pending = [], []
            sem = 0
            for item in loads:
                own = [part_refs.pop(0) for _ in item.parts]
                waits = []
                if any(item is c for c in copied):
                    ref = joined.pop(0)
                    for src_ref, (_, src, dst) in zip(own, item.parts):
                        waits.append(
                            pltpu.make_async_copy(
                                view(src_ref, src, place), view(ref, dst, place), in_sem.at[sem]
                            )
                        )
                        waits[-1].start()
                        sem += 1
                else:
                    ref = view(own[0], item.parts[0][1], place)
                ready.append(ref)
                pending.append(waits)
            stores, waited = [], []

            def wait(*copies):
                for copy in copies:
                    copy.wait()
                    waited.append(copy)

            def get(i):
                for copy in pending[i]:
                    copy.wait()
                pending[i] = []
                return ready[i]

            def put(src, dst):
                copy = pltpu.make_async_copy(src, dst, out_sem.at[len(stores)])
                copy.start()
                stores.append(copy)
                return copy

            body(place, get, [*out_refs, *scratch_refs], put, wait, hbm_refs, hbm_out_refs, *smem_refs)
            token_ref[...] = jnp.zeros(token_ref.shape, F32)
            for i in range(len(loads)):
                get(i)
            for copy in stores:
                if all(copy is not done for done in waited):
                    copy.wait()

        in_vmem = pl.BlockSpec(memory_space=pltpu.VMEM)
        in_hbm = pl.BlockSpec(memory_space=pltpu.HBM)
        *results, token = pl.pallas_call(
            run,
            out_shape=[jax.ShapeDtypeStruct(s, d) for s, d in [*outs, *hbm_outs, ((8, 128), F32)]],
            in_specs=[in_hbm] * len(hbm)
            + [in_vmem] * (len(parts) + n_token),
            out_specs=[in_vmem] * len(outs) + [in_hbm] * len(hbm_outs) + [in_vmem],
            scratch_shapes=[pltpu.VMEM(item.shape, item.dtype) for item in copied]
            + [pltpu.VMEM(s, d) for s, d in scratch]
            + [pltpu.SMEM(s, d) for s, d in smem]
            + [pltpu.SemaphoreType.DMA((max(n_copied, 1),)), pltpu.SemaphoreType.DMA((copies,))],
            compiler_params=pltpu.CompilerParams(vmem_limit_bytes=vmem << 20),
            cost_estimate=pl.CostEstimate(flops=COSTS.get(name, 0) * 10**8, bytes_accessed=0, transcendentals=0),
            name=name,
        )(*hbm, *[arr for arr, _, _ in parts], *self.token)
        self.token = [token]
        return results


def three(get, at, count, width):
    if count == 3:
        return [get(at + i) for i in range(3)]
    return [get(at).at[:, i * width : (i + 1) * width] for i in range(3)]


def heads_apart(v, first):
    return jnp.concatenate([jnp.where(first, v, 0), jnp.where(first, 0, v)], 0)


def attend(q_ref, k_ref, v_ref, ctx_ref, len_ref, len_at, chains):
    slots = q_ref.shape[0] // chains
    first = lax.broadcasted_iota(jnp.int32, (slots, PAIR), 1) < HDIM
    spot = lax.broadcasted_iota(jnp.int32, (slots, 2 * slots), 0)
    for chain in range(chains):
        rows = slice(chain * slots, (chain + 1) * slots)
        valid = spot < len_ref[len_at + chain]
        for at in range(0, q_ref.shape[1], PAIR):
            q_both = heads_apart(q_ref[rows, at : at + PAIR], first)
            scores = jnp.where(valid, dot_t(k_ref[rows, at : at + PAIR], q_both) * SCALING, -1e30)
            grown = jnp.exp(scores - jnp.max(scores, 0, keepdims=True))
            probs = (grown * (1.0 / jnp.sum(grown, 0, keepdims=True))).astype(BF16)
            both = dot_rows(probs, v_ref[rows, at : at + PAIR])
            ctx_ref[rows, at : at + PAIR] = jnp.where(first, both[:slots], both[slots:]).astype(BF16)


def attn_fwd_own_body(chains, place, get, staged, put, wait, hbm, _, len_ref):
    x_ref, wq, wk, wv, wo = staged[:5]
    later = staged[5 : len(hbm) - 3]
    q_ref, k_ref, v_ref, joint_ref, part_ref, bq, bv = staged[len(hbm) - 3 :]
    width = q_ref.shape[1]
    half = joint_ref.shape[1] - width
    ctx_ref = joint_ref.at[:, :width]
    lens = put(hbm[-1], len_ref)
    first = [put(hbm[0], x_ref), put(hbm[1], wq), put(hbm[-3], bq)]
    second = [put(hbm[2], wk), put(hbm[3], wv), put(hbm[-2], bv)]
    wait(*first)
    third = put(hbm[4], wo)
    put(hbm[0].at[:, strip(1 - place.core, half)], joint_ref.at[:, width:])
    x = x_ref[...]
    q_ref[...] = (dot(x, wq[...]) + lanes_of(bq)).astype(BF16)
    wait(*second)
    for src, dst in zip(hbm[5:-3], later):
        put(src, dst)
    k_ref[...] = dot(x, wk[...]).astype(BF16)
    v_ref[...] = (dot(x, wv[...]) + lanes_of(bv)).astype(BF16)
    wait(lens)
    attend(q_ref, k_ref, v_ref, ctx_ref, len_ref, place.t * chains, chains)
    wait(third)
    part_ref[...] = dot(ctx_ref[...], wo[...])


def attn_fwd_oth_body(chains, width, place, get, staged, put, wait, hbm, _, len_ref):
    X, BQ, BV, WO, ACC, OB, FG, FS, W = range(9)
    q_ref, k_ref, v_ref, r1_ref, joint_ref = staged
    hid_ref, ctx_ref = joint_ref.at[:, : r1_ref.shape[1]], joint_ref.at[:, r1_ref.shape[1] :]
    lens = put(hbm[0], len_ref)
    x = get(X)[...]
    wq, wk, wv = three(get, W, 1, width)
    q_ref[...] = (dot(x, wq[...]) + lanes_of(get(BQ))).astype(BF16)
    k_ref[...] = dot(x, wk[...]).astype(BF16)
    v_ref[...] = (dot(x, wv[...]) + lanes_of(get(BV))).astype(BF16)
    wait(lens)
    attend(q_ref, k_ref, v_ref, ctx_ref, len_ref, place.t * chains, chains)
    r1_ref[...] = dot(ctx_ref[...], get(WO)[...])
    acc_ref, x_ref = get(ACC), get(X)
    bias, gain, shift = lanes_of(get(OB)), lanes_of(get(FG)), lanes_of(get(FS))

    for at in range(0, x.shape[0], ROWS):
        rows = slice(at, at + ROWS)
        r1 = x_ref[rows, :].astype(F32) + (r1_ref[rows, :] + acc_ref[rows, :]) + bias
        r1_ref[rows, :] = r1
        normed, _ = row_stats(r1)
        hid_ref[rows, :] = (normed * gain + shift).astype(BF16)


def gelu_all(hid, weights, biases, acts, slopes):
    for wi_ref, bi_ref, act_ref, slope_ref in zip(weights, biases, acts, slopes):
        pre = dot(hid, wi_ref[...]) + lanes_of(bi_ref)
        cdf = 0.5 + 0.5 * lax.erf(pre * math.sqrt(0.5))
        act_ref[...] = (pre * cdf).astype(BF16)
        bell = jnp.exp(pre * pre * -0.5) * (1.0 / math.sqrt(2 * math.pi))
        slope_ref[...] = (cdf + pre * bell).astype(BF16)


def ffn_own_body(place, get, staged, put, *_):
    HID, WIA, BIA, WIB, BIB, WOA, WOB = range(7)
    acts = staged[:2]
    gelu_all(get(HID)[...], (get(WIA), get(WIB)), (get(BIA), get(BIB)), acts, staged[2:4])
    staged[4][...] = dot(acts[0][...], get(WOA)[...]) + dot(acts[1][...], get(WOB)[...])


def ffn_pre_body(place, get, staged, put, *_):
    HID, WIA, BIA, WIB, BIB = range(5)
    gelu_all(get(HID)[...], (get(WIA), get(WIB)), (get(BIA), get(BIB)), staged[:2], staged[2:])


def ffn_post_body(place, get, staged, put, *_):
    ACTA, ACTB, WOA, WOB, ACC, R1, FG, FS, OB, SG, SS, COT = range(12)
    out_ref, dr2_ref, low_ref, sums_ref = staged
    dr2_ref[...] = dot(get(ACTA)[...], get(WOA)[...]) + dot(get(ACTB)[...], get(WOB)[...])
    acc_ref, r1_ref, cot_ref = get(ACC), get(R1), get(COT)
    first_gain, first_shift, bias = lanes_of(get(FG)), lanes_of(get(FS)), lanes_of(get(OB))
    gain, shift = lanes_of(get(SG)), lanes_of(get(SS))
    sums_ref[...] = jnp.zeros(sums_ref.shape, F32)

    for at in range(0, dr2_ref.shape[0], ROWS):
        rows = slice(at, at + ROWS)
        normed, _ = row_stats(r1_ref[rows, :])
        r2 = normed * first_gain + first_shift + (dr2_ref[rows, :] + acc_ref[rows, :]) + bias
        normed, inverse = row_stats(r2)
        out_ref[rows, :] = (normed * gain + shift).astype(BF16)
        cot = cot_ref[rows, :].astype(F32)
        dr2 = norm_back(cot * gain, normed, inverse)
        low = dr2.astype(BF16)
        low_ref[rows, :] = low
        dr2_ref[rows, :] = dr2
        for i, v in enumerate((cot * normed, cot, low.astype(F32))):
            sums_ref[8 * i : 8 * i + 8, :] += jnp.sum(v.reshape(-1, 8, v.shape[1]), 0)


def ffn_bwd_body(last, place, get, staged, put, *_):
    LOW, WOA, DGA, WOB, DGB, WIA, WIB, ACC = range(8)
    low2 = get(LOW)[...]
    if last:
        joint_ref, *staged = staged
        group = staged[0].shape[1]
        staged = [joint_ref.at[:, :group], *staged]
    for g, (wo, dg) in enumerate(((WOA, DGA), (WOB, DGB))):
        dp_ref = staged[g]
        dp_ref[...] = (dot_t(low2, get(wo)[...]) * get(dg)[...].astype(F32)).astype(BF16)
    total = dot_t(staged[0][...], get(WIA)[...]) + dot_t(staged[1][...], get(WIB)[...])
    if not last:
        staged[2][...] = total + get(ACC)[...]
        return
    R1, FG, SUMS2 = 8, 9, 10
    dr1_ref, low_ref, sums_ref = staged[2:]
    dr1_ref[...] = total
    acc_ref, r1_ref, gain = get(ACC), get(R1), lanes_of(get(FG))
    half = low_ref.shape[1] // 2
    sums_ref[:24, :] = get(SUMS2)[...]
    sums_ref[24:, :] = jnp.zeros((24, sums_ref.shape[1]), F32)

    for at in range(0, low2.shape[0], ROWS):
        rows = slice(at, at + ROWS)
        dhid = dr1_ref[rows, :] + acc_ref[rows, :]
        normed, inverse = row_stats(r1_ref[rows, :])
        dr1 = norm_back(dhid * gain, normed, inverse)
        low = dr1.astype(BF16)
        low_ref[rows, :] = low
        dr1_ref[rows, :] = dr1
        for i, v in enumerate((dhid * normed, dhid, low.astype(F32))):
            sums_ref[24 + 8 * i : 32 + 8 * i, :] += jnp.sum(v.reshape(-1, 8, v.shape[1]), 0)

    joint_ref[:, group:] = low_ref[:, strip(1 - place.core, half)]


def attn_bwd_body(count, chains, width, place, get, staged, put, wait, hbm, _, len_ref):
    LOW, WO, Q, K, V, ACC, W = range(7)
    d_ref, out_ref, dc_ref = staged
    lens = put(hbm[0], len_ref)
    dc_ref[...] = dot_t(get(LOW)[...], get(WO)[...]).astype(BF16)
    q_ref, k_ref, v_ref = get(Q), get(K), get(V)
    slots = q_ref.shape[0] // chains
    first = lax.broadcasted_iota(jnp.int32, (slots, PAIR), 1) < HDIM
    spot = lax.broadcasted_iota(jnp.int32, (slots, 2 * slots), 0)
    wait(lens)
    for chain in range(chains):
        rows = slice(chain * slots, (chain + 1) * slots)
        valid = spot < len_ref[place.t * chains + chain]
        for at in range(0, width, PAIR):
            k = k_ref[rows, at : at + PAIR]
            q_both = heads_apart(q_ref[rows, at : at + PAIR], first)
            dc_both = heads_apart(dc_ref[rows, at : at + PAIR], first)
            scores = jnp.where(valid, dot_t(k, q_both) * SCALING, -1e30)
            grown = jnp.exp(scores - jnp.max(scores, 0, keepdims=True))
            probs = grown * (1.0 / jnp.sum(grown, 0, keepdims=True))
            dprobs = dot_t(v_ref[rows, at : at + PAIR], dc_both)
            dscores = (probs * (dprobs - jnp.sum(probs * dprobs, 0, keepdims=True))).astype(BF16)
            dq = dot_rows(dscores, k)
            dq = jnp.where(first, dq[:slots], dq[slots:])
            d_ref[rows, at : at + PAIR] = (dq * SCALING).astype(BF16)
            d_ref[rows, width + at : width + at + PAIR] = (dot(dscores, q_both) * SCALING).astype(BF16)
            d_ref[rows, 2 * width + at : 2 * width + at + PAIR] = dot(probs.astype(BF16), dc_both).astype(BF16)
    total = get(ACC)[...]
    for i, w in enumerate(three(get, W, count, width)):
        total = total + dot_t(d_ref[:, i * width : (i + 1) * width], w[...])
    out_ref[...] = total


def block_index(order, stage, m, mine, place):
    left = [d for d in "tyz" if d not in order[:stage]]
    rest = [d for d in left if d != order[stage]]
    here = {"t": 0, "y": place.y, "z": place.z}[order[stage]]
    index = 0
    for d in left:
        if d == order[stage]:
            bit = here if mine else 1 - here
        else:
            bit = (m >> (len(rest) - 1 - rest.index(d))) & 1
        index = index * 2 + bit
    return index


def split_index(orders, stage, m, mine, place):
    a, b = (block_index(order, stage, m, mine, place) for order in orders)
    return a + place.core * (b - a)


def give_split(orders, blocks, sent, kept, place):
    for mine, ref in ((False, sent), (True, kept)):
        for m in range(ref.shape[0]):
            ref[m] = blocks[split_index(orders, 0, m, mine, place)]


def outer_grad_body(orders, place, get, staged, put, *_):
    LOW, LOW_NBR = 0, 1
    sent, kept, g_ref = staged
    size = g_ref.shape[1]
    for t in range(2):
        grad = dot_rows(get(2 + 2 * t)[...], get(LOW)[...]) + dot_rows(get(3 + 2 * t)[...], get(LOW_NBR)[...])
        for b in range(4):
            g_ref[4 * t + b] = grad[b * size : (b + 1) * size].astype(BF16)
    give_split(orders, g_ref, sent, kept, place)


def inner_grad_body(orders, place, get, staged, put, *_):
    HID, HID_NBR, LOW, LOW_NBR = range(4)
    sent, kept, sums_ref, g_ref = staged
    for t in range(2):
        dp, dp_nbr, ctx, ctx_nbr = (get(4 + 4 * t + i) for i in range(4))
        grad = dot_rows(get(HID)[...], dp[...]) + dot_rows(get(HID_NBR)[...], dp_nbr[...])
        out = dot_rows(ctx[...], get(LOW)[...]) + dot_rows(ctx_nbr[...], get(LOW_NBR)[...])
        size, piece = grad.shape[0] // 4, out.shape[0] // 8
        for b in range(4):
            g_ref[4 * t + b, :size, :] = grad[b * size : (b + 1) * size].astype(BF16)
            for side in range(2):
                at = (2 * b + side) * piece
                lanes = slice(side * out.shape[1], (side + 1) * out.shape[1])
                g_ref[4 * t + b, size:, lanes] = out[at : at + piece].astype(BF16)
        sums_ref[t : t + 1, :] = jnp.sum(dp[...].astype(F32), 0, keepdims=True) + jnp.sum(
            dp_nbr[...].astype(F32), 0, keepdims=True
        )
    give_split(orders, g_ref, sent, kept, place)


def attn_grad_body(orders, place, get, staged, put, *_):
    X, X_NBR, UNITS, SUMS, SUMS_NBR = range(5)
    sent, kept, g_ref = staged
    size = g_ref.shape[1]
    wide = g_ref.shape[2] - 128
    width = wide // 3
    shared = [
        jnp.sum(get(SUMS)[8 * i : 8 * i + 8, :] + get(SUMS_NBR)[8 * i : 8 * i + 8, :], 0, keepdims=True)
        for i in range(6)
    ]
    for t in range(2):
        d, d_nbr = get(5 + 2 * t)[...], get(6 + 2 * t)[...]
        grad = dot_rows(get(X)[...], d) + dot_rows(get(X_NBR)[...], d_nbr)
        for b in range(4):
            g_ref[4 * t + b, :, :wide] = grad[b * size : (b + 1) * size].astype(BF16)
            g_ref[4 * t + b, :, wide:] = jnp.zeros((size, 128), BF16)
        total = jnp.sum(d.astype(F32), 0, keepdims=True) + jnp.sum(d_nbr.astype(F32), 0, keepdims=True)
        rows = [*shared, total[:, :width], total[:, 2 * width :], get(UNITS)[t : t + 1, :]]
        flat = jnp.concatenate(
            [row[:, i : i + 128] for row in rows for i in range(0, row.shape[1], 128)], 0
        )
        g_ref[4 * t, : flat.shape[0], wide:] = flat.astype(BF16)
    give_split(orders, g_ref, sent, kept, place)


def halve_body(orders, stage, place, get, staged, put, *_):
    a, b = get(0), get(1)
    for mine, ref in ((False, staged[0]), (True, staged[1])):
        for m in range(ref.shape[0]):
            k = split_index(orders, stage, m, mine, place)
            ref[m] = (a[k].astype(F32) + b[k].astype(F32)).astype(BF16)


def add_body(place, get, staged, put, *_):
    staged[0][...] = (get(0)[...].astype(F32) + get(1)[...].astype(F32)).astype(BF16)


def square(place):
    y, z = place.y, place.z
    return (2 * y + z, 2 - 2 * y + z, 2 * y + 1 - z, 3 - 2 * y - z)


def pairs(place):
    y, z = place.y, place.z
    return (y, 1 - y, 2 + z, 3 - z)


def join_body(where, place, get, staged, put, *_):
    ref = staged[0]
    size = ref.shape[0] // 4
    for i, at in enumerate(where(place)):
        ref[strip(at, size), :] = get(i)[...]


def join_blocks_body(place, get, staged, put, *_):
    for i, at in enumerate(square(place)):
        staged[0][at] = get(i)[0]


def cores(place, get):
    return (place.core, get(0)), (1 - place.core, get(1))


def outer_out_body(place, get, staged, put, _, __, outs):
    for i, (core, ref) in enumerate(cores(place, get)):
        for b in range(4):
            held = staged[4 * i + b]
            held[...] = ref[b].astype(F32)
            put(held, outs[0].at[strip(4 * core + b, held.shape[0]), :])


def inner_out_body(size, place, get, staged, put, _, __, outs):
    for i, (core, ref) in enumerate(cores(place, get)):
        for b in range(4):
            held = staged[4 * i + b]
            held[...] = ref[b].astype(F32)
            wide = held.shape[1]
            piece = held.shape[0] - size
            put(held.at[:size], outs[0].at[b * size : (b + 1) * size, strip(core, wide)])
            for side in range(2):
                at = (2 * b + side) * piece
                put(
                    held.at[size:, side * (wide // 2) : (side + 1) * (wide // 2)],
                    outs[1].at[at : at + piece, strip(core, wide // 2)],
                )


def attn_out_body(sizes, place, get, staged, put, _, __, outs):
    for i, (core, ref) in enumerate(cores(place, get)):
        for b in range(4):
            held = staged[4 * i + b]
            held[...] = ref[b].astype(F32)
            size, wide = held.shape[0], held.shape[1] - 128
            rows = strip(4 * core + b, size)
            for part in range(3):
                put(held.at[:, part * (wide // 3) : (part + 1) * (wide // 3)], outs[part].at[rows, :])

    def flat(held, at, size):
        wide = held.shape[1] - 128
        parts = [held[at + i : at + i + 1, wide:] for i in range(size // 128)]
        return jnp.concatenate(parts, 1).reshape(size)

    at = 0
    for ref, out, size in zip(staged[8:], outs[3:], sizes):
        ref[...] = jnp.where(place.core == 0, flat(staged[0], at, size), flat(staged[4], at, size))
        put(ref, out)
        at += size // 128
    size = staged[-1].shape[0]
    for ref, held, core in ((staged[-2], staged[0], place.core), (staged[-1], staged[4], 1 - place.core)):
        ref[...] = flat(held, at, size)
        put(ref, outs[-1].at[strip(core, size)])


def local(
    dp,
    inputs,
    lengths,
    query_weight,
    query_bias,
    key_weight,
    value_weight,
    value_bias,
    output_weight,
    output_bias,
    first_gain,
    first_shift,
    inner_weight,
    inner_bias,
    outer_weight,
    outer_bias,
    second_gain,
    second_shift,
    cotangent,
):
    chains, slots, model = inputs.shape
    rows = chains * slots
    width = query_weight.shape[1]
    units = inner_weight.shape[1]
    group = units // 2
    half = model // 2
    levels = int(math.log2(dp))
    line = Line()

    def bit_swap(v, bit):
        return lax.ppermute(v, DP, [(i, i ^ (1 << bit)) for i in range(dp)])

    def named(swap):
        def run(name, *v):
            with jax.named_scope(name):
                return swap(*v)

        return run

    @named
    def core_swap(v):
        return bit_swap(v, 0)

    @named
    def y_swap(v):
        return bit_swap(v, 1)

    @named
    def z_swap(v):
        return bit_swap(v, 2)

    @named
    def x_swap(v):
        return lax.ppermute(v, TENSOR, [(0, 1), (1, 0)])

    @named
    def diagonal_swap(v):
        return lax.ppermute(v, DP, [(i, i ^ 6) for i in range(dp)])

    def neighbours(name, v):
        return [v, y_swap(name + "y", v), z_swap(name + "z", v), diagonal_swap(name + "d", v)]

    @named
    def order_swap(v, orders, stage):
        pairs = []
        for spot in range(dp):
            for t in range(2):
                d = orders[spot % 2][stage]
                to = (spot, 1 - t) if d == "t" else (spot ^ (2 if d == "y" else 4), t)
                pairs.append((2 * spot + t, 2 * to[0] + to[1]))
        return lax.ppermute(v, (DP, TENSOR), pairs)

    x = inputs.reshape(rows, model)
    cot = cotangent.reshape(rows, model)

    quarter, bit, eighth = model // 4, model // 8, units // 8
    all_rows = slice(None)
    low_width = ((rows, width), BF16)
    low_wide = ((rows, model), BF16)
    wide = ((rows, model), F32)
    act = ((rows, group), BF16)
    len_smem = [(lengths.shape, jnp.int32)]
    g = SimpleNamespace()

    def lanes(arr, at, count):
        return piece(arr, (rows, count), lambda p: (all_rows, slice(at, at + count)))

    def spacer(name):
        line(name, lambda *_: None, [], [], vmem=4)

    def pack_attn():
        def body(place, get, staged, put, wait, refs, _):
            core, y, z, _ = place
            for at, row in ((0, y), (1, 2 + z)):
                to = staged[0].at[at * bit : (at + 1) * bit]
                for i, w in enumerate(refs[:3]):
                    put(w.at[strip(4 * core + row, bit), :], to.at[:, i * width : (i + 1) * width])
                put(refs[3].at[strip(row, bit), strip(core, half)], to.at[:, 3 * width :])

        (cut,) = line(
            "p1", body, [], [((2 * bit, 3 * width + half), BF16)],
            hbm=[query_weight, key_weight, value_weight, output_weight], vmem=56,
        )
        g.attn_mine = x_swap("ax", cut)

    def pack_rest():
        def body(place, get, staged, put, wait, refs, _):
            w_in, w_out, bq, bv, bi = refs
            wi_ref, wo_ref, bias_ref = staged
            core, y, z, _ = place
            put(w_in.at[strip(2 * y + z, quarter), strip(core, group)], wi_ref)
            put(w_out.at[strip(4 * core + y, eighth), :], wo_ref.at[:eighth])
            put(w_out.at[strip(4 * core + 2 + z, eighth), :], wo_ref.at[eighth:])
            put(bq, bias_ref.at[pl.ds(0, width)])
            put(bv, bias_ref.at[pl.ds(width, width)])
            put(bi, bias_ref.at[pl.ds(2 * width, units)])

        wi_cut, wo_cut, biases = line(
            "p2", body, [],
            [
                ((quarter, group), BF16), ((2 * eighth, model), BF16), ((2 * width + units,), F32),
            ],
            hbm=[inner_weight, outer_weight, query_bias, value_bias, inner_bias], vmem=56,
        )
        g.biases = x_swap("bx", biases)
        g.wi_mine = x_swap("wix", wi_cut)
        g.wo_mine = x_swap("wox", wo_cut)

    def relay(name, arr, parts, seen=()):
        dims = (arr.shape[0] // parts, arr.shape[1])
        return line(
            name, lambda p, get, staged, put, *_: [put(get(i), staged[i]) for i in range(parts)],
            [
                piece(arr, dims, lambda p, i=i: (slice(i * dims[0], (i + 1) * dims[0]), all_rows))
                for i in range(parts)
            ],
            [(dims, BF16)] * parts, seen=seen,
        )

    def join_four(name, where, pieces):
        dims = (4 * pieces[0].shape[0], pieces[0].shape[1])
        (own,) = line(name, lambda *a: join_body(where, *a), [load(v) for v in pieces], [(dims, BF16)])
        return own, core_swap(name + "c", own)

    def relay_attn():
        g.attn_a, g.attn_b = relay("ra", g.attn_mine, 2, [g.biases])
        g.attn_y, g.attn_z = y_swap("ay", g.attn_a), z_swap("az", g.attn_b)

    def relay_in():
        (g.wi_own,) = relay("rw", g.wi_mine, 1, [g.joint_nbr])
        g.wi_pieces = neighbours("wi", g.wi_own)

    def relay_out():
        g.wo_a, g.wo_b = relay("ro", g.wo_mine, 2)
        g.wo_y, g.wo_z = y_swap("woy", g.wo_a), z_swap("woz", g.wo_b)

    def join_attn():
        both = join_four("ja", pairs, [g.attn_a, g.attn_y, g.attn_b, g.attn_z])

        def part(cols, dims, to):
            return Load(
                dims, BF16,
                [
                    (v, lambda p: (all_rows, cols), lambda p, i=i: to(strip(1 - p.core if i else p.core, half)))
                    for i, v in enumerate(both)
                ],
            )

        g.w_oth = part(slice(0, 3 * width), (model, 3 * width), lambda at: (at, all_rows))
        g.wo_attn_oth = part(slice(3 * width, 3 * width + half), (width, model), lambda at: (all_rows, at))

    def join_in():
        g.wi_b, g.wi_a = join_four("jw", square, g.wi_pieces)

    def join_out():
        g.wo_b, g.wo_a = join_four("jo", pairs, [g.wo_a, g.wo_y, g.wo_b, g.wo_z])

    def attn_fwd_own():
        args = [
            x, query_weight, key_weight, value_weight, output_weight, inner_weight, outer_weight, inner_bias, cot,
            output_bias, first_gain, first_shift, outer_bias, second_gain, second_shift,
        ]
        *args, g.q_own, g.k_own, g.v_own, joint, g.part_own = line(
            "f1", lambda *a: attn_fwd_own_body(chains, *a), [],
            [(arr.shape, arr.dtype) for arr in args] + [low_width] * 3 + [((rows, width + half), BF16), wide],
            hbm=[*args, query_bias, value_bias, lengths],
            scratch=[(query_bias.shape, F32), (value_bias.shape, F32)], smem=len_smem, copies=len(args) + 4, vmem=44,
        )
        (
            g.x, g.wq, g.wk, g.wv, g.wo_attn, g.wi, g.wo, g.bi, g.cot,
            g.output_bias, g.first_gain, g.first_shift, g.outer_bias, g.second_gain, g.second_shift,
        ) = args
        g.w_own = [load(w) for w in (g.wq, g.wk, g.wv)]
        g.joint_nbr = core_swap("c1", joint)
        g.ctx_own, g.ctx_own_nbr = lanes(joint, 0, width), lanes(g.joint_nbr, 0, width)
        g.x_nbr = lanes(g.joint_nbr, width, half)

    def bias_oth(at, size):
        return Load((size,), F32, [(g.biases, lambda p: (pl.ds(pl.multiple_of(at(p), 128), size),), None)])

    def attn_fwd_oth():
        g.q_oth, g.k_oth, g.v_oth, g.r1, joint = line(
            "f2", lambda *a: attn_fwd_oth_body(chains, width, *a),
            [
                load(g.x), bias_oth(lambda p: 0, width), bias_oth(lambda p: width, width), g.wo_attn_oth,
                load(g.part_own), load(g.output_bias), load(g.first_gain), load(g.first_shift), g.w_oth,
            ],
            [low_width] * 3 + [wide, ((rows, model + width), BF16)], hbm=[lengths], smem=len_smem,
        )
        g.hid, g.ctx_oth = lanes(joint, 0, model), lanes(joint, model, width)
        g.hid_nbr_all = core_swap("hc", joint)
        g.hid_nbr, g.ctx_oth_nbr = lanes(g.hid_nbr_all, 0, model), lanes(g.hid_nbr_all, model, width)

    def flipped(p, flip):
        return 1 - p.core if flip else p.core

    def wi_own(flip):
        return piece(g.wi, (model, group), lambda p: (all_rows, strip(flipped(p, flip), group)))

    def wo_own(flip):
        return piece(g.wo, (group, model), lambda p: (strip(flipped(p, flip), group), all_rows))

    def bi_own(flip):
        return piece(g.bi, (group,), lambda p: (strip(flipped(p, flip), group),))

    def bi_oth(flip):
        return bias_oth(lambda p: 2 * width + flipped(p, flip) * group, group)

    def ffn_own():
        g.acta_own, g.actb_own, g.dga_own, g.dgb_own, g.ffn_own = line(
            "n1", ffn_own_body,
            [g.hid, wi_own(True), bi_own(True), wi_own(False), bi_own(False), wo_own(True), wo_own(False)],
            [act] * 4 + [wide],
        )
        g.acta_own_nbr = core_swap("a1", g.acta_own)

    def ffn_oth_pre():
        g.acta_oth, g.actb_oth, g.dga_oth, g.dgb_oth = line(
            "m2", ffn_pre_body, [g.hid, load(g.wi_a), bi_oth(True), load(g.wi_b), bi_oth(False)], [act] * 4,
            seen=[g.hid_nbr_all],
        )
        g.acta_oth_nbr = core_swap("a2", g.acta_oth)

    def ffn_oth_post():
        names = (g.outer_bias, g.second_gain, g.second_shift, g.cot)
        g.result, g.dr2, g.low2, g.sums2 = line(
            "n2", ffn_post_body,
            [
                load(v)
                for v in (
                    g.acta_oth, g.actb_oth, g.wo_a, g.wo_b, g.ffn_own, g.r1, g.first_gain, g.first_shift, *names,
                )
            ],
            [low_wide, wide, low_wide, ((24, model), F32)], seen=[g.acta_own_nbr],
        )
        g.low2_nbr = core_swap("lo", g.low2)

    def ffn_bwd_oth():
        g.dpa_oth, g.dpb_oth, g.back = line(
            "k2", lambda *a: ffn_bwd_body(False, *a),
            [load(v) for v in (g.low2, g.wo_a, g.dga_oth, g.wo_b, g.dgb_oth, g.wi_a, g.wi_b, g.dr2)],
            [act] * 2 + [wide], seen=[g.acta_oth_nbr],
        )
        g.dpa_oth_nbr = core_swap("pb", g.dpa_oth)

    def ffn_bwd_own():
        joint, g.dpb_own, g.dr1, g.low1, g.sums = line(
            "k1", lambda *a: ffn_bwd_body(True, *a),
            [
                load(g.low2), wo_own(True), load(g.dga_own), wo_own(False), load(g.dgb_own),
                wi_own(True), wi_own(False), load(g.back), load(g.r1), load(g.first_gain), load(g.sums2),
            ],
            [((rows, group + half), BF16), act, wide, low_wide, ((48, model), F32)], seen=[g.low2_nbr],
        )
        joint_nbr = core_swap("pl", joint)
        g.dpa_own_nbr, g.low1_nbr = lanes(joint_nbr, 0, group), lanes(joint_nbr, group, half)
        g.sums_nbr = core_swap("s", g.sums)

    def split_outs(dims):
        return [((4, *dims), BF16), ((4, *dims), BF16)]

    dims_of = {
        OUTER: (group // 4, model),
        INNER: (model // 4 + width // 8, group),
        ATTN: (half // 4, 3 * width + 128),
    }
    held, made = {}, {}

    def grad(name, body, loads, outs=(), seen=()):
        sent, kept, *rest = line(
            name + "0", lambda *a: body(ORDERS[name], *a), loads, split_outs(dims_of[name]) + [*outs],
            scratch=[((8, *dims_of[name]), BF16)], seen=seen,
        )
        held[name] = kept, order_swap(name + "0", sent, ORDERS[name], 0)
        return rest

    def outer_grad():
        names = (g.low2, g.low2_nbr, g.actb_own, g.acta_own_nbr, g.actb_oth, g.acta_oth_nbr)
        grad(OUTER, outer_grad_body, [load(v) for v in names], seen=[g.dpa_oth_nbr])

    def inner_grad():
        loads = [
            g.hid, g.hid_nbr, piece(g.low1, (rows, half), lambda p: (all_rows, strip(p.core, half))), g.low1_nbr,
            load(g.dpb_own), g.dpa_own_nbr, g.ctx_own, g.ctx_own_nbr,
            load(g.dpb_oth), load(g.dpa_oth_nbr), g.ctx_oth, g.ctx_oth_nbr,
        ]
        (g.unit_sums,) = grad(INNER, inner_grad_body, loads, [((8, group), F32)])

    def attn_grad():
        x_cut = piece(g.x, (rows, half), lambda p: (all_rows, strip(p.core, half)))
        names = (g.unit_sums, g.sums, g.sums_nbr, g.d_own, g.d_own_nbr, g.d_oth, g.d_oth_nbr)
        grad(ATTN, attn_grad_body, [x_cut, g.x_nbr, *(load(v) for v in names)])

    def attn_bwd(name, qkv, wo, w, acc):
        d, g.back_in = line(
            name, lambda *a: attn_bwd_body(len(w), chains, width, *a),
            [load(g.low1), wo, *(load(v) for v in qkv), load(acc), *w],
            [((rows, 3 * width), BF16), wide], hbm=[lengths], scratch=[low_width], smem=len_smem,
        )
        return d, core_swap(name + "c", d)

    def attn_bwd_oth():
        g.d_oth, g.d_oth_nbr = attn_bwd("b2", (g.q_oth, g.k_oth, g.v_oth), g.wo_attn_oth, [g.w_oth], g.dr1)

    def attn_bwd_own():
        g.d_own, g.d_own_nbr = attn_bwd("b1", (g.q_own, g.k_own, g.v_own), load(g.wo_attn), g.w_own, g.back_in)

    def halve(name, stage):
        kept, recv = held[name]
        orders = ORDERS[name]
        out = ((kept.shape[0] // 2, *kept.shape[1:]), BF16)
        sent, kept = line(
            name + str(stage), lambda *a: halve_body(orders, stage, *a), [load(kept), load(recv)], [out, out]
        )
        held[name] = kept, order_swap(name + str(stage), sent, orders, stage)

    def add(kernel, name, bit):
        a, b = held[name]
        (v,) = line(kernel, add_body, [load(a), load(b)], [(a.shape, BF16)])
        if bit < levels:
            with jax.named_scope(name + str(bit)):
                held[name] = v, bit_swap(v, bit)
            return
        held[name] = neighbours(name, v)

    def level(name):
        for bit in range(4, levels + 1):
            add(name + "l", name, bit)

    def join(name):
        (v,) = line(
            name + "j", join_blocks_body, [load(v) for v in held[name]], [((4, *dims_of[name]), BF16)]
        )
        held[name] = v, core_swap(name + "c", v)

    def write(name, body, outs, copies, more=()):
        made[name] = line(
            name + "w", body, [load(v) for v in held[name]], [], hbm_outs=[(dims, F32) for dims in outs],
            scratch=[(dims_of[name], F32)] * 8 + [((size,), F32) for size in more], copies=copies,
        )

    sizes = [model] * 6 + [width] * 2
    attn_outs = [(model, width)] * 3 + [(size,) for size in sizes] + [(units,)]
    steps = {
        "p1": pack_attn, "p2": pack_rest, "ra": relay_attn, "rw": relay_in, "ro": relay_out,
        "ja": join_attn, "jw": join_in, "jo": join_out,
        "f1": attn_fwd_own, "f2": attn_fwd_oth, "n1": ffn_own, "m2": ffn_oth_pre, "n2": ffn_oth_post,
        "k2": ffn_bwd_oth, "k1": ffn_bwd_own, "b2": attn_bwd_oth, "b1": attn_bwd_own,
        "O0": outer_grad, "I0": inner_grad, "A0": attn_grad,
        "Ow": lambda: write(OUTER, outer_out_body, [(units, model)], 8),
        "Iw": lambda: write(
            INNER, lambda *a: inner_out_body(model // 4, *a), [(model, units), (width, model)], 24
        ),
        "Aw": lambda: write(
            ATTN, lambda *a: attn_out_body(sizes, *a), attn_outs, 34, [*sizes, group, group]
        ),
    }
    for name in (OUTER, INNER, ATTN):
        steps[name + "1"] = lambda name=name: halve(name, 1)
        steps[name + "2"] = lambda name=name: halve(name, 2)
        steps[name + "3"] = lambda name=name: add(name + "3", name, 3)
        steps[name + "l"] = lambda name=name: level(name)
        steps[name + "j"] = lambda name=name: join(name)
    for step in ORDER:
        steps.get(step, lambda step=step: spacer(step))()
    (grad_outer,) = made[OUTER]
    grad_inner, grad_out = made[INNER]
    grad_q, grad_k, grad_v, g_sg, g_ss, g_ob2, g_fg, g_fs, g_ob1, g_qb, g_vb, g_ib = made[ATTN]

    def back_to(v):
        return v.reshape(chains, slots, model)

    return (
        back_to(g.result), back_to(g.back_in),
        grad_q, g_qb, grad_k, grad_v, g_vb, grad_out, g_ob1, g_fg, g_fs,
        grad_inner, g_ib, grad_outer, g_ob2, g_sg, g_ss,
    )


def solution(mesh):
    dp = mesh.shape[DP]
    rows, cols, low = P((DP, TENSOR), None, None), P(None, TENSOR), P(TENSOR, None)
    part, full = P(TENSOR), P()
    in_specs = (
        rows, P(DP), cols, part, cols, cols, part, low, full, full, full, cols, part, low, full, full, full, rows,
    )
    out_specs = (
        rows, rows, cols, part, cols, cols, part, low, full, full, full, cols, part, low, full, full, full,
    )

    def run(*args):
        return local(dp, *args)

    return jax.shard_map(run, mesh=mesh, in_specs=in_specs, out_specs=out_specs, check_vma=False)
```

```python
import math
from types import SimpleNamespace
from typing import NamedTuple

import jax
import jax.numpy as jnp
from jax import lax
from jax.experimental import pallas as pl
from jax.experimental.pallas import tpu as pltpu
from jax.sharding import PartitionSpec as P

HDIM = 64
PAIR = 2 * HDIM
SCALING = 1.0 / math.sqrt(HDIM)
ORDER = (
    "p1", "p2", "f1", "ra", "rw", "ja", "ro", "f2", "jw", "n1", "jo", "m2", "n2", "k2", "O0", "k1", "ba", "O1",
    "I0", "A0", "bb", "O2", "I1", "A1", "O3", "B0", "I2", "A2", "Ol", "B1", "I3", "A3", "Om", "Il", "B2", "Oj",
    "B3", "Al", "Im", "Bl", "Am", "Ow", "Ij", "Bm", "Aj", "Iw", "Bj", "Aw", "Bw",
)
COSTS = {
    "p1": 150, "p2": 150, "f1": 0, "ra": 150, "rw": 150, "ja": 150, "ro": 150, "f2": 150, "jw": 150, "n1": 10,
    "jo": 150, "m2": 150, "n2": 10, "k2": 150, "O0": 150, "k1": 0, "ba": 10, "O1": 150, "I0": 150, "A0": 150,
    "bb": 0, "O2": 150, "I1": 0, "A1": 0, "O3": 0, "B0": 150, "I2": 0, "A2": 150, "Ol": 0, "I3": 150, "B1": 30,
    "A3": 150, "Om": 0, "Il": 150, "B2": 30, "Oj": 150, "Al": 150, "B3": 150, "Im": 150, "Am": 150, "Bl": 150,
    "Ow": 150, "Ij": 150, "Bm": 150, "Aj": 150, "Iw": 150, "Bj": 150, "Aw": 150, "Bw": 150,
}
ROWS = 320
VMEM = {"p1": 56, "p2": 56, "f1": 44, "n2": 14}
BF16 = jnp.bfloat16
F32 = jnp.float32

DP, TENSOR = "dp", "tensor"
OUTER, INNER, ATTN, LAST = "O", "I", "A", "B"
ORDERS = {OUTER: ("yzt", "tzy"), INNER: ("tyz", "yzt"), ATTN: ("zty", "zyt"), LAST: ("ytz", "tzy")}
GATHER = {OUTER: ("yz", "zy"), INNER: ("yz", "zy"), ATTN: ("yz", "zy"), LAST: ("zy", "yz")}


def dot(a, b):
    return lax.dot_general(a, b, (((1,), (0,)), ((), ())), preferred_element_type=F32)


def dot_t(a, b):
    return lax.dot_general(a, b, (((1,), (1,)), ((), ())), preferred_element_type=F32)


def dot_rows(a, b):
    return lax.dot_general(a, b, (((0,), (0,)), ((), ())), preferred_element_type=F32)


def row_stats(rows):
    center = rows - jnp.mean(rows, -1, keepdims=True)
    inverse = lax.rsqrt(jnp.mean(center * center, -1, keepdims=True) + 1e-05)
    return center * inverse, inverse


def norm_back(scaled, normed, inverse):
    return inverse * (
        scaled
        - jnp.mean(scaled, -1, keepdims=True)
        - normed * jnp.mean(scaled * normed, -1, keepdims=True)
    )


def lanes_of(ref):
    return ref[...].reshape(1, -1)


def strip(index, size, base=0):
    return pl.ds(pl.multiple_of(base + index * size, size), size)


class Place(NamedTuple):
    core: jax.Array
    y: jax.Array
    z: jax.Array
    t: jax.Array


class Load(NamedTuple):
    shape: tuple
    dtype: jnp.dtype
    parts: list


def load(arr):
    return Load(arr.shape, arr.dtype, [(arr, None, None)])


def piece(arr, dims, src):
    return Load(dims, arr.dtype, [(arr, src, None)])


def view(ref, at, place):
    return ref if at is None else ref.at[at(place)]


class Line:
    def __init__(self):
        self.token = []

    def __call__(self, name, body, loads, outs, hbm=(), hbm_outs=(), scratch=(), smem=(), copies=8,
                 seen=(), aliases=None):
        loads = [*loads, *(load(arr) for arr in seen)]
        parts = [part for item in loads for part in item.parts]
        copied = [item for item in loads if len(item.parts) > 1 or len(item.shape) == 1 and item.parts[0][1]]
        n_copied = sum(len(item.parts) for item in copied)
        n_token = len(self.token)

        def run(*refs):
            refs = list(refs)

            def take(count):
                got = refs[:count]
                del refs[:count]
                return got

            hbm_refs, part_refs = take(len(hbm)), take(len(parts))
            take(n_token)
            out_refs, hbm_out_refs, (token_ref,) = take(len(outs)), take(len(hbm_outs)), take(1)
            joined, scratch_refs, smem_refs = take(len(copied)), take(len(scratch)), take(len(smem))
            in_sem, out_sem = refs
            spot = lax.axis_index(DP)
            place = Place(
                lax.rem(spot, 2), lax.rem(spot // 2, 2), lax.rem(spot // 4, 2), lax.axis_index(TENSOR)
            )
            ready, pending = [], []
            sem = 0
            for item in loads:
                own = [part_refs.pop(0) for _ in item.parts]
                waits = []
                if any(item is c for c in copied):
                    ref = joined.pop(0)
                    for src_ref, (_, src, dst) in zip(own, item.parts):
                        waits.append(
                            pltpu.make_async_copy(
                                view(src_ref, src, place), view(ref, dst, place), in_sem.at[sem]
                            )
                        )
                        waits[-1].start()
                        sem += 1
                else:
                    ref = view(own[0], item.parts[0][1], place)
                ready.append(ref)
                pending.append(waits)
            stores, waited = [], []

            def wait(*copies):
                for copy in copies:
                    copy.wait()
                    waited.append(copy)

            def get(i):
                for copy in pending[i]:
                    copy.wait()
                pending[i] = []
                return ready[i]

            def put(src, dst):
                copy = pltpu.make_async_copy(src, dst, out_sem.at[len(stores)])
                copy.start()
                stores.append(copy)
                return copy

            body(place, get, [*out_refs, *scratch_refs], put, wait, hbm_refs, hbm_out_refs, *smem_refs)
            token_ref[...] = jnp.zeros(token_ref.shape, F32)
            for i in range(len(loads)):
                get(i)
            for copy in stores:
                if all(copy is not done for done in waited):
                    copy.wait()

        in_vmem = pl.BlockSpec(memory_space=pltpu.VMEM)
        in_hbm = pl.BlockSpec(memory_space=pltpu.HBM)
        *results, token = pl.pallas_call(
            run,
            out_shape=[jax.ShapeDtypeStruct(s, d) for s, d in [*outs, *hbm_outs, ((8, 128), F32)]],
            in_specs=[in_hbm] * len(hbm)
            + [in_vmem] * (len(parts) + n_token),
            out_specs=[in_vmem] * len(outs) + [in_hbm] * len(hbm_outs) + [in_vmem],
            scratch_shapes=[pltpu.VMEM(item.shape, item.dtype) for item in copied]
            + [pltpu.VMEM(s, d) for s, d in scratch]
            + [pltpu.SMEM(s, d) for s, d in smem]
            + [pltpu.SemaphoreType.DMA((max(n_copied, 1),)), pltpu.SemaphoreType.DMA((copies,))],
            compiler_params=pltpu.CompilerParams(vmem_limit_bytes=VMEM.get(name, 10) << 20),
            input_output_aliases=aliases or {},
            cost_estimate=pl.CostEstimate(flops=COSTS.get(name, 0) * 10**8, bytes_accessed=0, transcendentals=0),
            name=name,
        )(*hbm, *[arr for arr, _, _ in parts], *self.token)
        self.token = [token]
        return results


def heads_apart(v, first):
    return jnp.concatenate([jnp.where(first, v, 0), jnp.where(first, 0, v)], 0)


def attend(q_ref, k_ref, v_ref, probs_ref, ctx_ref, len_ref, len_at, chains):
    slots = q_ref.shape[0] // chains
    first = lax.broadcasted_iota(jnp.int32, (slots, PAIR), 1) < HDIM
    spot = lax.broadcasted_iota(jnp.int32, (slots, 2 * slots), 0)
    for chain in range(chains):
        rows = slice(chain * slots, (chain + 1) * slots)
        valid = spot < len_ref[len_at + chain]
        for at in range(0, q_ref.shape[1], PAIR):
            q_both = heads_apart(q_ref[rows, at : at + PAIR], first)
            scores = jnp.where(valid, dot_t(k_ref[rows, at : at + PAIR], q_both) * SCALING, -1e30)
            grown = jnp.exp(scores - jnp.max(scores, 0, keepdims=True))
            probs = (grown * (1.0 / jnp.sum(grown, 0, keepdims=True))).astype(BF16)
            probs_ref[(chain * q_ref.shape[1] + at) // PAIR] = probs
            both = dot_rows(probs, v_ref[rows, at : at + PAIR])
            ctx_ref[rows, at : at + PAIR] = jnp.where(first, both[:slots], both[slots:]).astype(BF16)


def attn_fwd_own_body(chains, place, get, staged, put, wait, hbm, _, len_ref):
    x_ref, wq, wk, wv, wo = staged[:5]
    later = staged[5 : len(hbm) - 3]
    q_ref, k_ref, v_ref, probs_ref, joint_ref, part_ref, bq, bv = staged[len(hbm) - 3 :]
    width = q_ref.shape[1]
    half = joint_ref.shape[1] - width
    ctx_ref = joint_ref.at[:, :width]
    lens = put(hbm[-1], len_ref)
    first = [put(hbm[0], x_ref), put(hbm[1], wq), put(hbm[-3], bq)]
    second = [put(hbm[2], wk), put(hbm[3], wv), put(hbm[-2], bv)]
    wait(*first)
    third = put(hbm[4], wo)
    put(hbm[0].at[:, strip(1 - place.core, half)], joint_ref.at[:, width:])
    x = x_ref[...]
    q_ref[...] = (dot(x, wq[...]) + lanes_of(bq)).astype(BF16)
    wait(*second)
    for src, dst in zip(hbm[5:-3], later):
        put(src, dst)
    k_ref[...] = dot(x, wk[...]).astype(BF16)
    v_ref[...] = (dot(x, wv[...]) + lanes_of(bv)).astype(BF16)
    wait(lens)
    attend(q_ref, k_ref, v_ref, probs_ref, ctx_ref, len_ref, place.t * chains, chains)
    wait(third)
    part_ref[...] = dot(ctx_ref[...], wo[...])


def attn_fwd_oth_body(chains, width, place, get, staged, put, wait, hbm, _, len_ref):
    X, BQ, BV, ACC, OB, FG, FS, MINE, OTHER, OWN = range(10)
    q_ref, k_ref, v_ref, probs_ref, r1_ref, joint_ref, w_ref, wo_ref = staged
    copies = []
    for core, i in ((place.core, MINE), (1 - place.core, OTHER)):
        ref = get(i)
        half = ref.shape[0]
        copies.append(put(ref.at[:, : 3 * width], w_ref.at[strip(core, half), :]))
        copies.append(put(ref.at[:, 3 * width :], wo_ref.at[:, strip(core, half)]))
    model = r1_ref.shape[1]
    hid_ref, ctx_ref = joint_ref.at[:, :model], joint_ref.at[:, model : model + width]
    put(get(OWN), joint_ref.at[:, model + width :])
    lens = put(hbm[0], len_ref)
    x = get(X)[...]
    wait(*copies)
    wq, wk, wv = (w_ref.at[:, i * width : (i + 1) * width] for i in range(3))
    q_ref[...] = (dot(x, wq[...]) + lanes_of(get(BQ))).astype(BF16)
    k_ref[...] = dot(x, wk[...]).astype(BF16)
    v_ref[...] = (dot(x, wv[...]) + lanes_of(get(BV))).astype(BF16)
    wait(lens)
    attend(q_ref, k_ref, v_ref, probs_ref, ctx_ref, len_ref, place.t * chains, chains)
    r1_ref[...] = dot(ctx_ref[...], wo_ref[...])
    acc_ref, x_ref = get(ACC), get(X)
    bias, gain, shift = lanes_of(get(OB)), lanes_of(get(FG)), lanes_of(get(FS))

    for at in range(0, x.shape[0], ROWS):
        rows = slice(at, at + ROWS)
        r1 = x_ref[rows, :].astype(F32) + (r1_ref[rows, :] + acc_ref[rows, :]) + bias
        r1_ref[rows, :] = r1
        normed, _ = row_stats(r1)
        hid_ref[rows, :] = (normed * gain + shift).astype(BF16)


def gelu_all(hid, weights, biases, acts, slopes):
    for wi_ref, bi_ref, act_ref, slope_ref in zip(weights, biases, acts, slopes):
        pre = dot(hid, wi_ref[...]) + lanes_of(bi_ref)
        cdf = 0.5 + 0.5 * lax.erf(pre * math.sqrt(0.5))
        act_ref[...] = (pre * cdf).astype(BF16)
        bell = jnp.exp(pre * pre * -0.5) * (1.0 / math.sqrt(2 * math.pi))
        slope_ref[...] = (cdf + pre * bell).astype(BF16)


def ffn_own_body(place, get, staged, put, *_):
    HID, WIA, BIA, WIB, BIB, WOA, WOB = range(7)
    acts = staged[:2]
    gelu_all(get(HID)[...], (get(WIA), get(WIB)), (get(BIA), get(BIB)), acts, staged[2:4])
    staged[4][...] = dot(acts[0][...], get(WOA)[...]) + dot(acts[1][...], get(WOB)[...])


def ffn_pre_body(place, get, staged, put, *_):
    HID, WIA, BIA, WIB, BIB = range(5)
    gelu_all(get(HID)[...], (get(WIA), get(WIB)), (get(BIA), get(BIB)), staged[:2], staged[2:])


def ffn_post_body(place, get, staged, put, *_):
    ACTA, ACTB, WOA, WOB, ACC, R1, FG, FS, OB, SG, SS, COT = range(12)
    out_ref, dr2_ref, low_ref, sums_ref = staged
    dr2_ref[...] = dot(get(ACTA)[...], get(WOA)[...]) + dot(get(ACTB)[...], get(WOB)[...])
    acc_ref, r1_ref, cot_ref = get(ACC), get(R1), get(COT)
    first_gain, first_shift, bias = lanes_of(get(FG)), lanes_of(get(FS)), lanes_of(get(OB))
    gain, shift = lanes_of(get(SG)), lanes_of(get(SS))
    sums_ref[...] = jnp.zeros(sums_ref.shape, F32)

    for at in range(0, dr2_ref.shape[0], ROWS):
        rows = slice(at, at + ROWS)
        normed, _ = row_stats(r1_ref[rows, :])
        r2 = normed * first_gain + first_shift + (dr2_ref[rows, :] + acc_ref[rows, :]) + bias
        normed, inverse = row_stats(r2)
        out_ref[rows, :] = (normed * gain + shift).astype(BF16)
        cot = cot_ref[rows, :].astype(F32)
        dr2 = norm_back(cot * gain, normed, inverse)
        low = dr2.astype(BF16)
        low_ref[rows, :] = low
        dr2_ref[rows, :] = dr2
        for i, v in enumerate((cot * normed, cot, low.astype(F32))):
            sums_ref[8 * i : 8 * i + 8, :] += jnp.sum(v.reshape(-1, 8, v.shape[1]), 0)


def ffn_bwd_body(last, place, get, staged, put, *_):
    LOW, WOA, DGA, WOB, DGB, WIA, WIB, ACC = range(8)
    low2 = get(LOW)[...]
    if last:
        joint_ref, *staged = staged
        group = staged[0].shape[1]
        staged = [joint_ref.at[:, :group], *staged]
    for g, (wo, dg) in enumerate(((WOA, DGA), (WOB, DGB))):
        dp_ref = staged[g]
        dp_ref[...] = (dot_t(low2, get(wo)[...]) * get(dg)[...].astype(F32)).astype(BF16)
    total = dot_t(staged[0][...], get(WIA)[...]) + dot_t(staged[1][...], get(WIB)[...])
    if not last:
        staged[2][...] = total + get(ACC)[...]
        return
    R1, FG, SUMS2 = 8, 9, 10
    dr1_ref, low_ref, sums_ref = staged[2:]
    dr1_ref[...] = total
    acc_ref, r1_ref, gain = get(ACC), get(R1), lanes_of(get(FG))
    half = low_ref.shape[1] // 2
    sums_ref[:24, :] = get(SUMS2)[...]
    sums_ref[24:, :] = jnp.zeros((24, sums_ref.shape[1]), F32)

    for at in range(0, low2.shape[0], ROWS):
        rows = slice(at, at + ROWS)
        dhid = dr1_ref[rows, :] + acc_ref[rows, :]
        normed, inverse = row_stats(r1_ref[rows, :])
        dr1 = norm_back(dhid * gain, normed, inverse)
        low = dr1.astype(BF16)
        low_ref[rows, :] = low
        dr1_ref[rows, :] = dr1
        for i, v in enumerate((dhid * normed, dhid, low.astype(F32))):
            sums_ref[24 + 8 * i : 32 + 8 * i, :] += jnp.sum(v.reshape(-1, 8, v.shape[1]), 0)

    joint_ref[:, group:] = low_ref[:, strip(1 - place.core, half)]


def attn_bwd_body(first_pair, last_pair, chains, place, get, staged, put, wait, *_):
    LOW, ACC = 0, 1
    d_ref, out_ref, dc_ref, w_ref = staged
    wide = dc_ref.shape[1]
    slots = d_ref.shape[0] // chains
    first = lax.broadcasted_iota(jnp.int32, (slots, PAIR), 1) < HDIM
    cols = slice(first_pair * PAIR, last_pair * PAIR)
    copies = [
        put(get(7 + 8 * half + i).at[:, cols], w_ref.at[:, (3 * half + i) * wide : (3 * half + i + 1) * wide])
        for half in range(2)
        for i in range(3)
    ]
    for half in range(2):
        wo_ref, q_ref, k_ref, v_ref, probs_ref = (get(2 + 8 * half + i) for i in range(5))
        base = 3 * half * wide
        dc_ref[...] = dot_t(get(LOW)[...], wo_ref[cols, :]).astype(BF16)
        for chain in range(chains):
            rows = slice(chain * slots, (chain + 1) * slots)
            for pair in range(first_pair, last_pair):
                lanes = slice(pair * PAIR, (pair + 1) * PAIR)
                at = (pair - first_pair) * PAIR
                k = k_ref[rows, lanes]
                q_both = heads_apart(q_ref[rows, lanes], first)
                dc_both = heads_apart(dc_ref[rows, at : at + PAIR], first)
                probs_low = probs_ref[chain * (q_ref.shape[1] // PAIR) + pair]
                probs = probs_low.astype(F32)
                dprobs = dot_t(v_ref[rows, lanes], dc_both)
                dscores = (probs * (dprobs - jnp.sum(probs * dprobs, 0, keepdims=True))).astype(BF16)
                dq = dot_rows(dscores, k)
                dq = jnp.where(first, dq[:slots], dq[slots:])
                at += base
                d_ref[rows, at : at + PAIR] = (dq * SCALING).astype(BF16)
                d_ref[rows, at + wide : at + wide + PAIR] = (dot(dscores, q_both) * SCALING).astype(BF16)
                d_ref[rows, at + 2 * wide : at + 2 * wide + PAIR] = dot(probs_low, dc_both).astype(BF16)
    wait(*copies)
    out_ref[...] = get(ACC)[...] + dot_t(d_ref[...], w_ref[...])


def block_index(order, stage, m, mine, place):
    left = [d for d in "tyz" if d not in order[:stage]]
    rest = [d for d in left if d != order[stage]]
    here = {"t": 0, "y": place.y, "z": place.z}[order[stage]]
    index = 0
    for d in left:
        if d == order[stage]:
            bit = here if mine else 1 - here
        else:
            bit = (m >> (len(rest) - 1 - rest.index(d))) & 1
        index = index * 2 + bit
    return index


def split_index(orders, stage, m, mine, place):
    a, b = (block_index(order, stage, m, mine, place) for order in orders)
    return a + place.core * (b - a)


def give_split(orders, blocks, sent, kept, place):
    for mine, ref in ((False, sent), (True, kept)):
        for m in range(ref.shape[0]):
            ref[m] = blocks[split_index(orders, 0, m, mine, place)]


def outer_grad_body(orders, place, get, staged, put, *_):
    LOW, LOW_NBR = 0, 1
    sent, kept, g_ref = staged
    size = g_ref.shape[1]
    for t in range(2):
        grad = dot_rows(get(2 + 2 * t)[...], get(LOW)[...]) + dot_rows(get(3 + 2 * t)[...], get(LOW_NBR)[...])
        for b in range(4):
            g_ref[4 * t + b] = grad[b * size : (b + 1) * size].astype(BF16)
    give_split(orders, g_ref, sent, kept, place)


def inner_grad_body(orders, place, get, staged, put, *_):
    HID, HID_NBR, LOW, LOW_NBR = range(4)
    sent, kept, sums_ref, g_ref = staged
    for t in range(2):
        dp, dp_nbr, ctx, ctx_nbr = (get(4 + 4 * t + i) for i in range(4))
        grad = dot_rows(get(HID)[...], dp[...]) + dot_rows(get(HID_NBR)[...], dp_nbr[...])
        out = dot_rows(ctx[...], get(LOW)[...]) + dot_rows(ctx_nbr[...], get(LOW_NBR)[...])
        size, piece = grad.shape[0] // 4, out.shape[0] // 8
        for b in range(4):
            g_ref[4 * t + b, :size, :] = grad[b * size : (b + 1) * size].astype(BF16)
            for side in range(2):
                at = (2 * b + side) * piece
                lanes = slice(side * out.shape[1], (side + 1) * out.shape[1])
                g_ref[4 * t + b, size:, lanes] = out[at : at + piece].astype(BF16)
        sums_ref[t : t + 1, :] = jnp.sum(dp[...].astype(F32), 0, keepdims=True) + jnp.sum(
            dp_nbr[...].astype(F32), 0, keepdims=True
        )
    give_split(orders, g_ref, sent, kept, place)


def attn_grad_body(last, orders, place, get, staged, put, *_):
    X, X_NBR, D, D_NBR, BIAS, UNITS, SUMS, SUMS_NBR = range(8)
    if last:
        sent, kept, g_ref = staged
        shared = [
            jnp.sum(get(SUMS)[8 * i : 8 * i + 8, :] + get(SUMS_NBR)[8 * i : 8 * i + 8, :], 0, keepdims=True)
            for i in range(6)
        ]
    else:
        sent, kept, bias_ref, g_ref = staged
    size = g_ref.shape[1]
    wide = g_ref.shape[2] - (128 if last else 0)
    for t in range(2):
        cols = slice(t * wide, (t + 1) * wide)
        d, d_nbr = get(D)[:, cols], get(D_NBR)[:, cols]
        grad = dot_rows(get(X)[...], d) + dot_rows(get(X_NBR)[...], d_nbr)
        for b in range(4):
            g_ref[4 * t + b, :, :wide] = grad[b * size : (b + 1) * size].astype(BF16)
        total = jnp.sum(d.astype(F32), 0, keepdims=True) + jnp.sum(d_nbr.astype(F32), 0, keepdims=True)
        if not last:
            bias_ref[t : t + 1, :] = total
            continue
        before = get(BIAS)[t : t + 1, :]
        third, before_third = wide // 3, before.shape[1] // 3
        rows = [
            *shared, before[:, :before_third], total[:, :third], before[:, 2 * before_third :],
            total[:, 2 * third :], get(UNITS)[t : t + 1, :],
        ]
        flat = jnp.concatenate(
            [row[:, i : i + 128] for row in rows for i in range(0, row.shape[1], 128)], 0
        )
        for b in range(4):
            g_ref[4 * t + b, :, wide:] = jnp.zeros((size, 128), BF16)
        g_ref[4 * t, : flat.shape[0], wide:] = flat.astype(BF16)
    give_split(orders, g_ref, sent, kept, place)


def halve_body(orders, stage, place, get, staged, put, *_):
    a, b = get(0), get(1)
    for mine, ref in ((False, staged[0]), (True, staged[1])):
        for m in range(ref.shape[0]):
            k = split_index(orders, stage, m, mine, place)
            ref[m] = (a[k].astype(F32) + b[k].astype(F32)).astype(BF16)


def add_body(place, get, staged, put, *_):
    staged[0][...] = (get(0)[...].astype(F32) + get(1)[...].astype(F32)).astype(BF16)


def square(place):
    y, z = place.y, place.z
    return (2 * y + z, 2 - 2 * y + z, 2 * y + 1 - z, 3 - 2 * y - z)


def pairs(place):
    y, z = place.y, place.z
    return (y, 1 - y, 2 + z, 3 - z)


def join_body(where, place, get, staged, put, *_):
    ref = staged[0]
    size = ref.shape[0] // 4
    for i, at in enumerate(where(place)):
        ref[strip(at, size), :] = get(i)[...]


def blend(place, pair):
    return pair[0] + place.core * (pair[1] - pair[0])


def join_pair_body(axes, place, get, staged, put, *_):
    at = blend(place, [{"y": place.y, "z": place.z}[axis[0]] for axis in axes])
    staged[0][at] = get(0)[0]
    staged[0][1 - at] = get(1)[0]


def join_blocks_body(axes, place, get, staged, put, *_):
    for i in range(2):
        y, z = (place.y, place.z) if i == 0 else (1 - place.y, 1 - place.z)
        for b in range(2):
            at = blend(place, [2 * y + b if axis[0] == "z" else 2 * b + z for axis in axes])
            staged[0][at] = get(i)[b]


def cores(place, get):
    return (place.core, get(0)), (1 - place.core, get(1))


def outer_out_body(place, get, staged, put, _, __, outs):
    for i in (1, 2):
        put(get(1 + i), outs[i])
    for i, (core, ref) in enumerate(cores(place, get)):
        for b in range(4):
            held = staged[4 * i + b]
            held[...] = ref[b].astype(F32)
            put(held, outs[0].at[strip(4 * core + b, held.shape[0]), :])


def inner_out_body(size, place, get, staged, put, _, __, outs):
    for i, (core, ref) in enumerate(cores(place, get)):
        for b in range(4):
            held = staged[4 * i + b]
            held[...] = ref[b].astype(F32)
            wide = held.shape[1]
            piece = held.shape[0] - size
            put(held.at[:size], outs[0].at[b * size : (b + 1) * size, strip(core, wide)])
            for side in range(2):
                at = (2 * b + side) * piece
                put(
                    held.at[size:, side * (wide // 2) : (side + 1) * (wide // 2)],
                    outs[1].at[at : at + piece, strip(core, wide // 2)],
                )


def attn_out_body(first_col, sizes, place, get, staged, put, _, __, outs):
    for i, (core, ref) in enumerate(cores(place, get)):
        for b in range(4):
            held = staged[4 * i + b]
            held[...] = ref[b].astype(F32)
            size, wide = held.shape[0], held.shape[1] - (128 if sizes else 0)
            rows = strip(4 * core + b, size)
            third = wide // 3
            for part in range(3):
                cols = slice(first_col, first_col + third)
                put(held.at[:, part * third : (part + 1) * third], outs[part].at[rows, cols])
    if not sizes:
        return

    def flat(held, at, size):
        wide = held.shape[1] - 128
        parts = [held[at + i : at + i + 1, wide:] for i in range(size // 128)]
        return jnp.concatenate(parts, 1).reshape(size)

    at = 0
    for ref, out, size in zip(staged[8:], outs[3:], sizes):
        ref[...] = jnp.where(place.core == 0, flat(staged[0], at, size), flat(staged[4], at, size))
        put(ref, out)
        at += size // 128
    size = staged[-1].shape[0]
    for ref, held, core in ((staged[-2], staged[0], place.core), (staged[-1], staged[4], 1 - place.core)):
        ref[...] = flat(held, at, size)
        put(ref, outs[-1].at[strip(core, size)])


def local(
    dp,
    inputs,
    lengths,
    query_weight,
    query_bias,
    key_weight,
    value_weight,
    value_bias,
    output_weight,
    output_bias,
    first_gain,
    first_shift,
    inner_weight,
    inner_bias,
    outer_weight,
    outer_bias,
    second_gain,
    second_shift,
    cotangent,
):
    chains, slots, model = inputs.shape
    rows = chains * slots
    width = query_weight.shape[1]
    units = inner_weight.shape[1]
    group = units // 2
    half = model // 2
    levels = int(math.log2(dp))
    line = Line()

    def bit_swap(v, bit):
        return lax.ppermute(v, DP, [(i, i ^ (1 << bit)) for i in range(dp)])

    def named(swap):
        def run(name, *v):
            with jax.named_scope(name):
                return swap(*v)

        return run

    @named
    def core_swap(v):
        return bit_swap(v, 0)

    @named
    def y_swap(v):
        return bit_swap(v, 1)

    @named
    def z_swap(v):
        return bit_swap(v, 2)

    @named
    def x_swap(v):
        return lax.ppermute(v, TENSOR, [(0, 1), (1, 0)])

    @named
    def diagonal_swap(v):
        return lax.ppermute(v, DP, [(i, i ^ 6) for i in range(dp)])

    @named
    def gather_swap(v, axes, step):
        return lax.ppermute(v, DP, [(i, i ^ (2 if axes[i % 2][step] == "y" else 4)) for i in range(dp)])

    @named
    def order_swap(v, orders, stage):
        pairs = []
        for spot in range(dp):
            for t in range(2):
                d = orders[spot % 2][stage]
                to = (spot, 1 - t) if d == "t" else (spot ^ (2 if d == "y" else 4), t)
                pairs.append((2 * spot + t, 2 * to[0] + to[1]))
        return lax.ppermute(v, (DP, TENSOR), pairs)

    x = inputs.reshape(rows, model)
    cot = cotangent.reshape(rows, model)

    quarter, bit, eighth = model // 4, model // 8, units // 8
    all_rows = slice(None)
    low_width = ((rows, width), BF16)
    low_wide = ((rows, model), BF16)
    wide = ((rows, model), F32)
    act = ((rows, group), BF16)
    pairs_here = width // PAIR
    probs_shape = ((chains * pairs_here, slots, 2 * slots), BF16)
    len_smem = [(lengths.shape, jnp.int32)]
    g = SimpleNamespace()

    def lanes(arr, at, count):
        return piece(arr, (rows, count), lambda p: (all_rows, slice(at, at + count)))

    def spacer(name):
        line(name, lambda *_: None, [], [])

    def pack_attn():
        def body(place, get, staged, put, wait, refs, _):
            core, y, z, _ = place
            for at, row in ((0, y), (1, 2 + z)):
                to = staged[0].at[at * bit : (at + 1) * bit]
                for i, w in enumerate(refs[:3]):
                    put(w.at[strip(4 * core + row, bit), :], to.at[:, i * width : (i + 1) * width])
                put(refs[3].at[strip(row, bit), strip(core, half)], to.at[:, 3 * width :])

        (cut,) = line(
            "p1", body, [], [((2 * bit, 3 * width + half), BF16)],
            hbm=[query_weight, key_weight, value_weight, output_weight],
        )
        g.attn_mine = x_swap("ax", cut)

    def pack_rest():
        def body(place, get, staged, put, wait, refs, _):
            w_in, w_out, bq, bv, bi = refs
            wi_ref, wo_ref, bias_ref = staged
            core, y, z, _ = place
            put(w_in.at[strip(2 * y + z, quarter), strip(core, group)], wi_ref)
            put(w_out.at[strip(4 * core + y, eighth), :], wo_ref.at[:eighth])
            put(w_out.at[strip(4 * core + 2 + z, eighth), :], wo_ref.at[eighth:])
            put(bq, bias_ref.at[pl.ds(0, width)])
            put(bv, bias_ref.at[pl.ds(width, width)])
            put(bi, bias_ref.at[pl.ds(2 * width, units)])

        wi_cut, wo_cut, biases = line(
            "p2", body, [],
            [
                ((quarter, group), BF16), ((2 * eighth, model), BF16), ((2 * width + units,), F32),
            ],
            hbm=[inner_weight, outer_weight, query_bias, value_bias, inner_bias],
        )
        g.biases = x_swap("bx", biases)
        g.wi_mine = x_swap("wix", wi_cut)
        g.wo_mine = x_swap("wox", wo_cut)

    def relay(name, arr, parts, seen=()):
        dims = (arr.shape[0] // parts, arr.shape[1])
        return line(
            name, lambda p, get, staged, put, *_: [put(get(i), staged[i]) for i in range(parts)],
            [
                piece(arr, dims, lambda p, i=i: (slice(i * dims[0], (i + 1) * dims[0]), all_rows))
                for i in range(parts)
            ],
            [(dims, BF16)] * parts, seen=seen,
        )

    def join_four(name, where, pieces):
        dims = (4 * pieces[0].shape[0], pieces[0].shape[1])
        (own,) = line(name, lambda *a: join_body(where, *a), [load(v) for v in pieces], [(dims, BF16)])
        return own, core_swap(name + "c", own)

    def relay_attn():
        g.attn_a, g.attn_b = relay("ra", g.attn_mine, 2, [g.biases])
        g.attn_y, g.attn_z = y_swap("ay", g.attn_a), z_swap("az", g.attn_b)

    def relay_in():
        (g.wi_own,) = relay("rw", g.wi_mine, 1)
        v = g.wi_own
        g.wi_pieces = [v, y_swap("wiy", v), z_swap("wiz", v), diagonal_swap("wid", v)]

    def relay_out():
        g.wo_a, g.wo_b = relay("ro", g.wo_mine, 2)
        g.wo_y, g.wo_z = y_swap("woy", g.wo_a), z_swap("woz", g.wo_b)

    def join_attn():
        g.attn_weights = join_four("ja", pairs, [g.attn_a, g.attn_y, g.attn_b, g.attn_z])

    def join_in():
        g.wi_b, g.wi_a = join_four("jw", square, g.wi_pieces)

    def join_out():
        g.wo_b, g.wo_a = join_four("jo", pairs, [g.wo_a, g.wo_y, g.wo_b, g.wo_z])

    def attn_fwd_own():
        args = [
            x, query_weight, key_weight, value_weight, output_weight, inner_weight, outer_weight, inner_bias, cot,
            output_bias, first_gain, first_shift, outer_bias, second_gain, second_shift,
        ]
        *args, q, k, v, probs, g.joint, g.part_own = line(
            "f1", lambda *a: attn_fwd_own_body(chains, *a), [],
            [(arr.shape, arr.dtype) for arr in args] + [low_width] * 3 + [probs_shape, ((rows, width + half), BF16), wide],
            hbm=[*args, query_bias, value_bias, lengths],
            scratch=[(query_bias.shape, F32), (value_bias.shape, F32)], smem=len_smem, copies=len(args) + 4,
        )
        (
            g.x, g.wq, g.wk, g.wv, g.wo_attn, g.wi, g.wo, g.bi, g.cot,
            g.output_bias, g.first_gain, g.first_shift, g.outer_bias, g.second_gain, g.second_shift,
        ) = args
        g.own = [load(arr) for arr in (g.wo_attn, q, k, v, probs, g.wq, g.wk, g.wv)]

    def bias_oth(at, size):
        return Load((size,), F32, [(g.biases, lambda p: (pl.ds(pl.multiple_of(at(p), 128), size),), None)])

    def attn_fwd_oth():
        q, k, v, probs, g.r1, joint, w, wo = line(
            "f2", lambda *a: attn_fwd_oth_body(chains, width, *a),
            [
                load(g.x), bias_oth(lambda p: 0, width), bias_oth(lambda p: width, width),
                *(load(v) for v in (g.part_own, g.output_bias, g.first_gain, g.first_shift, *g.attn_weights, g.joint)),
            ],
            [low_width] * 3
            + [probs_shape, wide, ((rows, model + 2 * width + half), BF16)]
            + [((model, 3 * width), BF16), ((width, model), BF16)],
            hbm=[lengths], smem=len_smem,
        )
        g.oth = [load(arr) for arr in (wo, q, k, v, probs)] + [
            piece(w, (model, width), lambda p, i=i: (all_rows, slice(i * width, (i + 1) * width))) for i in range(3)
        ]
        g.hid, g.ctx_oth = lanes(joint, 0, model), lanes(joint, model, width)
        g.hid_nbr_all = core_swap("hc", joint)
        g.hid_nbr, g.ctx_oth_nbr = lanes(g.hid_nbr_all, 0, model), lanes(g.hid_nbr_all, model, width)
        g.ctx_own, g.ctx_own_nbr = (lanes(v, model + width, width) for v in (joint, g.hid_nbr_all))
        g.x_nbr = lanes(g.hid_nbr_all, model + 2 * width, half)

    def flipped(p, flip):
        return 1 - p.core if flip else p.core

    def wi_own(flip):
        return piece(g.wi, (model, group), lambda p: (all_rows, strip(flipped(p, flip), group)))

    def wo_own(flip):
        return piece(g.wo, (group, model), lambda p: (strip(flipped(p, flip), group), all_rows))

    def bi_own(flip):
        return piece(g.bi, (group,), lambda p: (strip(flipped(p, flip), group),))

    def bi_oth(flip):
        return bias_oth(lambda p: 2 * width + flipped(p, flip) * group, group)

    def ffn_own():
        g.acta_own, g.actb_own, g.dga_own, g.dgb_own, g.ffn_own = line(
            "n1", ffn_own_body,
            [g.hid, wi_own(True), bi_own(True), wi_own(False), bi_own(False), wo_own(True), wo_own(False)],
            [act] * 4 + [wide],
        )
        g.acta_own_nbr = core_swap("a1", g.acta_own)

    def ffn_oth_pre():
        g.acta_oth, g.actb_oth, g.dga_oth, g.dgb_oth = line(
            "m2", ffn_pre_body, [g.hid, load(g.wi_a), bi_oth(True), load(g.wi_b), bi_oth(False)], [act] * 4,
            seen=[g.hid_nbr_all],
        )
        g.acta_oth_nbr = core_swap("a2", g.acta_oth)

    def ffn_oth_post():
        names = (g.outer_bias, g.second_gain, g.second_shift, g.cot)
        g.result, g.dr2, g.low2, g.sums2 = line(
            "n2", ffn_post_body,
            [
                load(v)
                for v in (
                    g.acta_oth, g.actb_oth, g.wo_a, g.wo_b, g.ffn_own, g.r1, g.first_gain, g.first_shift, *names,
                )
            ],
            [low_wide, wide, low_wide, ((24, model), F32)], seen=[g.acta_own_nbr],
        )
        g.low2_nbr = core_swap("lo", g.low2)

    def ffn_bwd_oth():
        g.dpa_oth, g.dpb_oth, g.back = line(
            "k2", lambda *a: ffn_bwd_body(False, *a),
            [load(v) for v in (g.low2, g.wo_a, g.dga_oth, g.wo_b, g.dgb_oth, g.wi_a, g.wi_b, g.dr2)],
            [act] * 2 + [wide],
        )
        g.dpa_oth_nbr = core_swap("pb", g.dpa_oth)

    def ffn_bwd_own():
        joint, g.dpb_own, g.dr1, g.low1, g.sums = line(
            "k1", lambda *a: ffn_bwd_body(True, *a),
            [
                load(g.low2), wo_own(True), load(g.dga_own), wo_own(False), load(g.dgb_own),
                wi_own(True), wi_own(False), load(g.back), load(g.r1), load(g.first_gain), load(g.sums2),
            ],
            [((rows, group + half), BF16), act, wide, low_wide, ((48, model), F32)],
        )
        joint_nbr = core_swap("pl", joint)
        g.dpa_own_nbr, g.low1_nbr = lanes(joint_nbr, 0, group), lanes(joint_nbr, group, half)
        g.sums_nbr = core_swap("s", g.sums)

    def split_outs(dims):
        return [((4, *dims), BF16), ((4, *dims), BF16)]

    dims_of = {
        OUTER: (group // 4, model),
        INNER: (model // 4 + width // 8, group),
        ATTN: (half // 4, 3 * (pairs_here - 1) * PAIR),
        LAST: (half // 4, 3 * PAIR + 128),
    }
    held, made = {}, {}

    def grad(name, body, loads, outs=(), seen=()):
        sent, kept, *rest = line(
            name + "0", lambda *a: body(ORDERS[name], *a), loads, split_outs(dims_of[name]) + [*outs],
            scratch=[((8, *dims_of[name]), BF16)], seen=seen,
        )
        held[name] = kept, order_swap(name + "0", sent, ORDERS[name], 0)
        return rest

    def outer_grad():
        names = (g.low2, g.low2_nbr, g.actb_own, g.acta_own_nbr, g.actb_oth, g.acta_oth_nbr)
        grad(OUTER, outer_grad_body, [load(v) for v in names])

    def inner_grad():
        loads = [
            g.hid, g.hid_nbr, piece(g.low1, (rows, half), lambda p: (all_rows, strip(p.core, half))), g.low1_nbr,
            load(g.dpb_own), g.dpa_own_nbr, g.ctx_own, g.ctx_own_nbr,
            load(g.dpb_oth), load(g.dpa_oth_nbr), g.ctx_oth, g.ctx_oth_nbr,
        ]
        (g.unit_sums,) = grad(INNER, inner_grad_body, loads, [((8, group), F32)])

    def attn_bwd(name, first_pair, last_pair, acc):
        count = last_pair - first_pair
        d, g.back_in = line(
            name, lambda *a: attn_bwd_body(first_pair, last_pair, chains, *a),
            [load(g.low1), load(acc), *g.own, *g.oth],
            [((rows, 6 * count * PAIR), BF16), wide],
            scratch=[((rows, count * PAIR), BF16), ((model, 6 * count * PAIR), BF16)],
        )
        return d, core_swap(name + "c", d)

    def attn_bwd_most():
        g.d_most = attn_bwd("ba", 0, pairs_here - 1, g.dr1)

    def attn_bwd_rest():
        g.d_rest = attn_bwd("bb", pairs_here - 1, pairs_here, g.back_in)

    def attn_grad(name, d, more, outs=()):
        x_cut = piece(g.x, (rows, half), lambda p: (all_rows, strip(p.core, half)))
        loads = [x_cut, g.x_nbr, *(load(v) for v in (*d, *more))]
        return grad(name, lambda *a: attn_grad_body(name == LAST, *a), loads, outs)

    def attn_grad_most():
        (g.bias_sums,) = attn_grad(ATTN, g.d_most, [], [((8, dims_of[ATTN][1]), F32)])

    def attn_grad_rest():
        attn_grad(LAST, g.d_rest, [g.bias_sums, g.unit_sums, g.sums, g.sums_nbr])

    def halve(name, stage):
        kept, recv = held[name]
        orders = ORDERS[name]
        out = ((kept.shape[0] // 2, *kept.shape[1:]), BF16)
        sent, kept = line(
            name + str(stage), lambda *a: halve_body(orders, stage, *a), [load(kept), load(recv)], [out, out]
        )
        held[name] = kept, order_swap(name + str(stage), sent, orders, stage)

    def add(kernel, name, bit):
        a, b = held[name]
        (v,) = line(kernel, add_body, [load(a), load(b)], [(a.shape, BF16)])
        if bit < levels:
            with jax.named_scope(name + str(bit)):
                held[name] = v, bit_swap(v, bit)
            return
        held[name] = v, gather_swap(name + "n", v, GATHER[name], 0)

    def level(name):
        for bit in range(4, levels + 1):
            add(name + "l", name, bit)

    def join_pair(name):
        (v,) = line(
            name + "m", lambda *a: join_pair_body(GATHER[name], *a), [load(v) for v in held[name]],
            [((2, *dims_of[name]), BF16)],
        )
        held[name] = v, gather_swap(name + "p", v, GATHER[name], 1)

    def join(name):
        (v,) = line(
            name + "j", lambda *a: join_blocks_body(GATHER[name], *a), [load(v) for v in held[name]],
            [((4, *dims_of[name]), BF16)],
        )
        held[name] = v, core_swap(name + "c", v)

    def write(name, body, outs, copies, more=(), onto=(), loads=(), low_outs=()):
        made[name] = line(
            name + "w", body, [load(v) for v in (*held[name], *loads)], [], hbm=onto,
            hbm_outs=[(dims, F32) for dims in outs] + [(dims, BF16) for dims in low_outs],
            scratch=[(dims_of[name], F32)] * 8 + [((size,), F32) for size in more], copies=copies,
            aliases={i: i for i in range(len(onto))},
        )

    sizes = [model] * 6 + [width] * 2
    attn_outs = [(model, width)] * 3
    last_outs = attn_outs + [(size,) for size in sizes] + [(units,)]
    steps = {
        "p1": pack_attn, "p2": pack_rest, "ra": relay_attn, "rw": relay_in, "ro": relay_out,
        "ja": join_attn, "jw": join_in, "jo": join_out,
        "f1": attn_fwd_own, "f2": attn_fwd_oth, "n1": ffn_own, "m2": ffn_oth_pre, "n2": ffn_oth_post,
        "k2": ffn_bwd_oth, "k1": ffn_bwd_own, "ba": attn_bwd_most, "bb": attn_bwd_rest,
        "O0": outer_grad, "I0": inner_grad, "A0": attn_grad_most, "B0": attn_grad_rest,
        "Ow": lambda: write(
            OUTER, outer_out_body, [(units, model), (rows, model)], 10, loads=[g.back_in, g.result],
            low_outs=[(rows, model)],
        ),
        "Iw": lambda: write(
            INNER, lambda *a: inner_out_body(model // 4, *a), [(model, units), (width, model)], 24
        ),
        "Aw": lambda: write(ATTN, lambda *a: attn_out_body(0, (), *a), attn_outs, 24),
        "Bw": lambda: write(
            LAST, lambda *a: attn_out_body((pairs_here - 1) * PAIR, sizes, *a), last_outs, 34,
            [*sizes, group, group], made[ATTN],
        ),
    }
    for name in (OUTER, INNER, ATTN, LAST):
        steps[name + "1"] = lambda name=name: halve(name, 1)
        steps[name + "2"] = lambda name=name: halve(name, 2)
        steps[name + "3"] = lambda name=name: add(name + "3", name, 3)
        steps[name + "l"] = lambda name=name: level(name)
        steps[name + "m"] = lambda name=name: join_pair(name)
        steps[name + "j"] = lambda name=name: join(name)
    for step in ORDER:
        steps.get(step, lambda step=step: spacer(step))()
    grad_outer, grad_inputs, result = made[OUTER]
    grad_inner, grad_out = made[INNER]
    grad_q, grad_k, grad_v, g_sg, g_ss, g_ob2, g_fg, g_fs, g_ob1, g_qb, g_vb, g_ib = made[LAST]

    def back_to(v):
        return v.reshape(chains, slots, model)

    return (
        back_to(result), back_to(grad_inputs),
        grad_q, g_qb, grad_k, grad_v, g_vb, grad_out, g_ob1, g_fg, g_fs,
        grad_inner, g_ib, grad_outer, g_ob2, g_sg, g_ss,
    )


def solution(mesh):
    dp = mesh.shape[DP]
    rows, cols, low = P((DP, TENSOR), None, None), P(None, TENSOR), P(TENSOR, None)
    part, full = P(TENSOR), P()
    in_specs = (
        rows, P(DP), cols, part, cols, cols, part, low, full, full, full, cols, part, low, full, full, full, rows,
    )
    out_specs = (
        rows, rows, cols, part, cols, cols, part, low, full, full, full, cols, part, low, full, full, full,
    )

    def run(*args):
        return local(dp, *args)

    return jax.shard_map(run, mesh=mesh, in_specs=in_specs, out_specs=out_specs, check_vma=False)
```

```python
import math
from types import SimpleNamespace
from typing import NamedTuple

import jax
import jax.numpy as jnp
from jax import lax
from jax.experimental import pallas as pl
from jax.experimental.pallas import tpu as pltpu
from jax.sharding import PartitionSpec as P

HDIM = 64
PAIR = 2 * HDIM
SCALING = 1.0 / math.sqrt(HDIM)
ORDER = (
    "p1", "p2", "f1", "ra", "rw", "ja", "ro", "f2", "jw", "n1", "jo", "m2", "n2", "k2", "O0", "k1", "ba", "O1",
    "I0", "A0", "bb", "O2", "I1", "A1", "O3", "B0", "I2", "A2", "Ol", "B1", "I3", "A3", "Om", "Il", "B2", "Oj",
    "B3", "Al", "Im", "Bl", "Am", "Ow", "Ij", "Bm", "Aj", "Iw", "Bj", "Aw", "Bw",
)
COSTS = {
    "p1": 150, "p2": 150, "f1": 0, "ra": 150, "rw": 150, "ja": 150, "ro": 150, "f2": 150, "jw": 150, "n1": 10,
    "jo": 150, "m2": 150, "n2": 10, "k2": 150, "O0": 150, "k1": 0, "ba": 10, "O1": 150, "I0": 150, "A0": 150,
    "bb": 0, "O2": 150, "I1": 0, "A1": 0, "O3": 0, "B0": 150, "I2": 0, "A2": 150, "Ol": 0, "I3": 150, "B1": 30,
    "A3": 150, "Om": 0, "Il": 150, "B2": 30, "Oj": 150, "Al": 150, "B3": 150, "Im": 150, "Am": 150, "Bl": 150,
    "Ow": 150, "Ij": 150, "Bm": 150, "Aj": 150, "Iw": 150, "Bj": 150, "Aw": 150, "Bw": 150,
}
ROWS = 320
VMEM = {"p1": 56, "p2": 56, "f1": 30, "n2": 14}
BF16 = jnp.bfloat16
F32 = jnp.float32

DP, TENSOR = "dp", "tensor"
OUTER, INNER, ATTN, LAST = "O", "I", "A", "B"
ORDERS = {OUTER: ("yzt", "tzy"), INNER: ("tyz", "yzt"), ATTN: ("zty", "zyt"), LAST: ("yzt", "tyz")}
GATHER = {OUTER: ("zy", "yz"), INNER: ("yz", "zy"), ATTN: ("yz", "zy"), LAST: ("zy", "yz")}


def dot(a, b):
    return lax.dot_general(a, b, (((1,), (0,)), ((), ())), preferred_element_type=F32)


def dot_t(a, b):
    return lax.dot_general(a, b, (((1,), (1,)), ((), ())), preferred_element_type=F32)


def dot_rows(a, b):
    return lax.dot_general(a, b, (((0,), (0,)), ((), ())), preferred_element_type=F32)


def row_stats(rows):
    center = rows - jnp.mean(rows, -1, keepdims=True)
    inverse = lax.rsqrt(jnp.mean(center * center, -1, keepdims=True) + 1e-05)
    return center * inverse, inverse


def norm_back(scaled, normed, inverse):
    return inverse * (
        scaled
        - jnp.mean(scaled, -1, keepdims=True)
        - normed * jnp.mean(scaled * normed, -1, keepdims=True)
    )


def lanes_of(ref):
    return ref[...].reshape(1, -1)


def strip(index, size, base=0):
    return pl.ds(pl.multiple_of(base + index * size, size), size)


class Place(NamedTuple):
    core: jax.Array
    y: jax.Array
    z: jax.Array
    t: jax.Array


class Load(NamedTuple):
    shape: tuple
    dtype: jnp.dtype
    parts: list


def load(arr):
    return Load(arr.shape, arr.dtype, [(arr, None, None)])


def piece(arr, dims, src):
    return Load(dims, arr.dtype, [(arr, src, None)])


def view(ref, at, place):
    return ref if at is None else ref.at[at(place)]


class Line:
    def __init__(self):
        self.token = []

    def __call__(self, name, body, loads, outs, hbm=(), hbm_outs=(), scratch=(), smem=(), copies=8,
                 seen=(), aliases=None):
        loads = [*loads, *(load(arr) for arr in seen)]
        parts = [part for item in loads for part in item.parts]
        copied = [item for item in loads if len(item.parts) > 1 or len(item.shape) == 1 and item.parts[0][1]]
        n_copied = sum(len(item.parts) for item in copied)
        n_token = len(self.token)

        def run(*refs):
            refs = list(refs)

            def take(count):
                got = refs[:count]
                del refs[:count]
                return got

            hbm_refs, part_refs = take(len(hbm)), take(len(parts))
            take(n_token)
            out_refs, hbm_out_refs, (token_ref,) = take(len(outs)), take(len(hbm_outs)), take(1)
            joined, scratch_refs, smem_refs = take(len(copied)), take(len(scratch)), take(len(smem))
            in_sem, out_sem = refs
            spot = lax.axis_index(DP)
            place = Place(
                lax.rem(spot, 2), lax.rem(spot // 2, 2), lax.rem(spot // 4, 2), lax.axis_index(TENSOR)
            )
            ready, pending = [], []
            sem = 0
            for item in loads:
                own = [part_refs.pop(0) for _ in item.parts]
                waits = []
                if any(item is c for c in copied):
                    ref = joined.pop(0)
                    for src_ref, (_, src, dst) in zip(own, item.parts):
                        waits.append(
                            pltpu.make_async_copy(
                                view(src_ref, src, place), view(ref, dst, place), in_sem.at[sem]
                            )
                        )
                        waits[-1].start()
                        sem += 1
                else:
                    ref = view(own[0], item.parts[0][1], place)
                ready.append(ref)
                pending.append(waits)
            stores, waited = [], []

            def wait(*copies):
                for copy in copies:
                    copy.wait()
                    waited.append(copy)

            def get(i):
                for copy in pending[i]:
                    copy.wait()
                pending[i] = []
                return ready[i]

            def put(src, dst):
                copy = pltpu.make_async_copy(src, dst, out_sem.at[len(stores)])
                copy.start()
                stores.append(copy)
                return copy

            body(place, get, [*out_refs, *scratch_refs], put, wait, hbm_refs, hbm_out_refs, *smem_refs)
            token_ref[...] = jnp.zeros(token_ref.shape, F32)
            for i in range(len(loads)):
                get(i)
            for copy in stores:
                if all(copy is not done for done in waited):
                    copy.wait()

        in_vmem = pl.BlockSpec(memory_space=pltpu.VMEM)
        in_hbm = pl.BlockSpec(memory_space=pltpu.HBM)
        *results, token = pl.pallas_call(
            run,
            out_shape=[jax.ShapeDtypeStruct(s, d) for s, d in [*outs, *hbm_outs, ((8, 128), F32)]],
            in_specs=[in_hbm] * len(hbm)
            + [in_vmem] * (len(parts) + n_token),
            out_specs=[in_vmem] * len(outs) + [in_hbm] * len(hbm_outs) + [in_vmem],
            scratch_shapes=[pltpu.VMEM(item.shape, item.dtype) for item in copied]
            + [pltpu.VMEM(s, d) for s, d in scratch]
            + [pltpu.SMEM(s, d) for s, d in smem]
            + [pltpu.SemaphoreType.DMA((max(n_copied, 1),)), pltpu.SemaphoreType.DMA((copies,))],
            compiler_params=pltpu.CompilerParams(vmem_limit_bytes=VMEM.get(name, 10) << 20),
            input_output_aliases=aliases or {},
            cost_estimate=pl.CostEstimate(flops=COSTS.get(name, 0) * 10**8, bytes_accessed=0, transcendentals=0),
            name=name,
        )(*hbm, *[arr for arr, _, _ in parts], *self.token)
        self.token = [token]
        return results


def heads_apart(v, first):
    return jnp.concatenate([jnp.where(first, v, 0), jnp.where(first, 0, v)], 0)


def attend(q_ref, k_ref, v_ref, probs_ref, ctx_ref, len_ref, len_at, chains):
    slots = q_ref.shape[0] // chains
    first = lax.broadcasted_iota(jnp.int32, (slots, PAIR), 1) < HDIM
    spot = lax.broadcasted_iota(jnp.int32, (slots, 2 * slots), 0)
    for chain in range(chains):
        rows = slice(chain * slots, (chain + 1) * slots)
        valid = spot < len_ref[len_at + chain]
        for at in range(0, q_ref.shape[1], PAIR):
            q_both = heads_apart(q_ref[rows, at : at + PAIR], first)
            scores = jnp.where(valid, dot_t(k_ref[rows, at : at + PAIR], q_both) * SCALING, -1e30)
            grown = jnp.exp(scores - jnp.max(scores, 0, keepdims=True))
            probs = (grown * (1.0 / jnp.sum(grown, 0, keepdims=True))).astype(BF16)
            probs_ref[(chain * q_ref.shape[1] + at) // PAIR] = probs
            both = dot_rows(probs, v_ref[rows, at : at + PAIR])
            ctx_ref[rows, at : at + PAIR] = jnp.where(first, both[:slots], both[slots:]).astype(BF16)


def attn_fwd_own_body(chains, place, get, staged, put, wait, hbm, _, len_ref):
    x_ref, wq, wk, wv, wo = staged[:5]
    later = staged[5 : len(hbm) - 3]
    q_ref, k_ref, v_ref, probs_ref, joint_ref, part_ref, bq, bv = staged[len(hbm) - 3 :]
    width = q_ref.shape[1]
    half = joint_ref.shape[1] - width
    ctx_ref = joint_ref.at[:, :width]
    lens = put(hbm[-1], len_ref)
    first = [put(hbm[0], x_ref), put(hbm[1], wq), put(hbm[-3], bq)]
    second = [put(hbm[2], wk), put(hbm[3], wv), put(hbm[-2], bv)]
    wait(*first)
    third = put(hbm[4], wo)
    put(hbm[0].at[:, strip(1 - place.core, half)], joint_ref.at[:, width:])
    x = x_ref[...]
    q_ref[...] = (dot(x, wq[...]) + lanes_of(bq)).astype(BF16)
    wait(*second)
    for src, dst in zip(hbm[5:-3], later):
        put(src, dst)
    k_ref[...] = dot(x, wk[...]).astype(BF16)
    v_ref[...] = (dot(x, wv[...]) + lanes_of(bv)).astype(BF16)
    wait(lens)
    attend(q_ref, k_ref, v_ref, probs_ref, ctx_ref, len_ref, place.t * chains, chains)
    wait(third)
    part_ref[...] = dot(ctx_ref[...], wo[...])


def attn_fwd_oth_body(chains, width, place, get, staged, put, wait, hbm, _, len_ref):
    X, BQ, BV, ACC, OB, FG, FS, MINE, OTHER, OWN = range(10)
    q_ref, k_ref, v_ref, probs_ref, r1_ref, joint_ref, w_ref, wo_ref = staged
    copies = []
    for core, i in ((place.core, MINE), (1 - place.core, OTHER)):
        ref = get(i)
        half = ref.shape[0]
        copies.append(put(ref.at[:, : 3 * width], w_ref.at[strip(core, half), :]))
        copies.append(put(ref.at[:, 3 * width :], wo_ref.at[:, strip(core, half)]))
    model = r1_ref.shape[1]
    hid_ref, ctx_ref = joint_ref.at[:, :model], joint_ref.at[:, model : model + width]
    put(get(OWN), joint_ref.at[:, model + width :])
    lens = put(hbm[0], len_ref)
    x = get(X)[...]
    wait(*copies)
    wq, wk, wv = (w_ref.at[:, i * width : (i + 1) * width] for i in range(3))
    q_ref[...] = (dot(x, wq[...]) + lanes_of(get(BQ))).astype(BF16)
    k_ref[...] = dot(x, wk[...]).astype(BF16)
    v_ref[...] = (dot(x, wv[...]) + lanes_of(get(BV))).astype(BF16)
    wait(lens)
    attend(q_ref, k_ref, v_ref, probs_ref, ctx_ref, len_ref, place.t * chains, chains)
    r1_ref[...] = dot(ctx_ref[...], wo_ref[...])
    acc_ref, x_ref = get(ACC), get(X)
    bias, gain, shift = lanes_of(get(OB)), lanes_of(get(FG)), lanes_of(get(FS))

    for at in range(0, x.shape[0], ROWS):
        rows = slice(at, at + ROWS)
        r1 = x_ref[rows, :].astype(F32) + (r1_ref[rows, :] + acc_ref[rows, :]) + bias
        r1_ref[rows, :] = r1
        normed, _ = row_stats(r1)
        hid_ref[rows, :] = (normed * gain + shift).astype(BF16)


def gelu_all(hid, weights, biases, acts, slopes):
    for wi_ref, bi_ref, act_ref, slope_ref in zip(weights, biases, acts, slopes):
        pre = dot(hid, wi_ref[...]) + lanes_of(bi_ref)
        cdf = 0.5 + 0.5 * lax.erf(pre * math.sqrt(0.5))
        act_ref[...] = (pre * cdf).astype(BF16)
        bell = jnp.exp(pre * pre * -0.5) * (1.0 / math.sqrt(2 * math.pi))
        slope_ref[...] = (cdf + pre * bell).astype(BF16)


def ffn_own_body(place, get, staged, put, *_):
    HID, WIA, BIA, WIB, BIB, WOA, WOB = range(7)
    acts = staged[:2]
    gelu_all(get(HID)[...], (get(WIA), get(WIB)), (get(BIA), get(BIB)), acts, staged[2:4])
    staged[4][...] = dot(acts[0][...], get(WOA)[...]) + dot(acts[1][...], get(WOB)[...])


def ffn_pre_body(place, get, staged, put, *_):
    HID, WIA, BIA, WIB, BIB = range(5)
    gelu_all(get(HID)[...], (get(WIA), get(WIB)), (get(BIA), get(BIB)), staged[:2], staged[2:])


def ffn_post_body(place, get, staged, put, *_):
    ACTA, ACTB, WOA, WOB, ACC, R1, FG, FS, OB, SG, SS, COT = range(12)
    out_ref, dr2_ref, low_ref, sums_ref = staged
    dr2_ref[...] = dot(get(ACTA)[...], get(WOA)[...]) + dot(get(ACTB)[...], get(WOB)[...])
    acc_ref, r1_ref, cot_ref = get(ACC), get(R1), get(COT)
    first_gain, first_shift, bias = lanes_of(get(FG)), lanes_of(get(FS)), lanes_of(get(OB))
    gain, shift = lanes_of(get(SG)), lanes_of(get(SS))
    sums_ref[...] = jnp.zeros(sums_ref.shape, F32)

    for at in range(0, dr2_ref.shape[0], ROWS):
        rows = slice(at, at + ROWS)
        normed, _ = row_stats(r1_ref[rows, :])
        r2 = normed * first_gain + first_shift + (dr2_ref[rows, :] + acc_ref[rows, :]) + bias
        normed, inverse = row_stats(r2)
        out_ref[rows, :] = (normed * gain + shift).astype(BF16)
        cot = cot_ref[rows, :].astype(F32)
        dr2 = norm_back(cot * gain, normed, inverse)
        low = dr2.astype(BF16)
        low_ref[rows, :] = low
        dr2_ref[rows, :] = dr2
        for i, v in enumerate((cot * normed, cot, low.astype(F32))):
            sums_ref[8 * i : 8 * i + 8, :] += jnp.sum(v.reshape(-1, 8, v.shape[1]), 0)


def ffn_bwd_body(last, place, get, staged, put, *_):
    LOW, WOA, DGA, WOB, DGB, WIA, WIB, ACC = range(8)
    low2 = get(LOW)[...]
    if last:
        joint_ref, *staged = staged
        group = staged[0].shape[1]
        staged = [joint_ref.at[:, :group], *staged]
    for g, (wo, dg) in enumerate(((WOA, DGA), (WOB, DGB))):
        dp_ref = staged[g]
        dp_ref[...] = (dot_t(low2, get(wo)[...]) * get(dg)[...].astype(F32)).astype(BF16)
    total = dot_t(staged[0][...], get(WIA)[...]) + dot_t(staged[1][...], get(WIB)[...])
    if not last:
        staged[2][...] = total + get(ACC)[...]
        return
    R1, FG, SUMS2 = 8, 9, 10
    dr1_ref, low_ref, sums_ref = staged[2:]
    dr1_ref[...] = total
    acc_ref, r1_ref, gain = get(ACC), get(R1), lanes_of(get(FG))
    half = low_ref.shape[1] // 2
    sums_ref[:24, :] = get(SUMS2)[...]
    sums_ref[24:, :] = jnp.zeros((24, sums_ref.shape[1]), F32)

    for at in range(0, low2.shape[0], ROWS):
        rows = slice(at, at + ROWS)
        dhid = dr1_ref[rows, :] + acc_ref[rows, :]
        normed, inverse = row_stats(r1_ref[rows, :])
        dr1 = norm_back(dhid * gain, normed, inverse)
        low = dr1.astype(BF16)
        low_ref[rows, :] = low
        dr1_ref[rows, :] = dr1
        for i, v in enumerate((dhid * normed, dhid, low.astype(F32))):
            sums_ref[24 + 8 * i : 32 + 8 * i, :] += jnp.sum(v.reshape(-1, 8, v.shape[1]), 0)

    joint_ref[:, group:] = low_ref[:, strip(1 - place.core, half)]


def attn_bwd_body(first_pair, last_pair, chains, place, get, staged, put, wait, *_):
    LOW, ACC = 0, 1
    d_ref, out_ref, dc_ref, w_ref = staged
    wide = dc_ref.shape[1]
    slots = d_ref.shape[0] // chains
    first = lax.broadcasted_iota(jnp.int32, (slots, PAIR), 1) < HDIM
    cols = slice(first_pair * PAIR, last_pair * PAIR)
    copies = [
        put(get(7 + 8 * half + i).at[:, cols], w_ref.at[:, (3 * half + i) * wide : (3 * half + i + 1) * wide])
        for half in range(2)
        for i in range(3)
    ]
    for half in range(2):
        wo_ref, q_ref, k_ref, v_ref, probs_ref = (get(2 + 8 * half + i) for i in range(5))
        base = 3 * half * wide
        dc_ref[...] = dot_t(get(LOW)[...], wo_ref[cols, :]).astype(BF16)
        for chain in range(chains):
            rows = slice(chain * slots, (chain + 1) * slots)
            for pair in range(first_pair, last_pair):
                lanes = slice(pair * PAIR, (pair + 1) * PAIR)
                at = (pair - first_pair) * PAIR
                k = k_ref[rows, lanes]
                q_both = heads_apart(q_ref[rows, lanes], first)
                dc_both = heads_apart(dc_ref[rows, at : at + PAIR], first)
                probs_low = probs_ref[chain * (q_ref.shape[1] // PAIR) + pair]
                probs = probs_low.astype(F32)
                dprobs = dot_t(v_ref[rows, lanes], dc_both)
                dscores = (probs * (dprobs - jnp.sum(probs * dprobs, 0, keepdims=True))).astype(BF16)
                dq = dot_rows(dscores, k)
                dq = jnp.where(first, dq[:slots], dq[slots:])
                at += base
                d_ref[rows, at : at + PAIR] = (dq * SCALING).astype(BF16)
                d_ref[rows, at + wide : at + wide + PAIR] = (dot(dscores, q_both) * SCALING).astype(BF16)
                d_ref[rows, at + 2 * wide : at + 2 * wide + PAIR] = dot(probs_low, dc_both).astype(BF16)
    wait(*copies)
    out_ref[...] = get(ACC)[...] + dot_t(d_ref[...], w_ref[...])


def block_index(order, stage, m, mine, place):
    left = [d for d in "tyz" if d not in order[:stage]]
    rest = [d for d in left if d != order[stage]]
    here = {"t": 0, "y": place.y, "z": place.z}[order[stage]]
    index = 0
    for d in left:
        if d == order[stage]:
            bit = here if mine else 1 - here
        else:
            bit = (m >> (len(rest) - 1 - rest.index(d))) & 1
        index = index * 2 + bit
    return index


def split_index(orders, stage, m, mine, place):
    a, b = (block_index(order, stage, m, mine, place) for order in orders)
    return a + place.core * (b - a)


def give_split(orders, blocks, sent, kept, place):
    for mine, ref in ((False, sent), (True, kept)):
        for m in range(ref.shape[0]):
            ref[m] = blocks[split_index(orders, 0, m, mine, place)]


def outer_grad_body(orders, place, get, staged, put, *_):
    LOW, LOW_NBR = 0, 1
    sent, kept, g_ref = staged
    size = g_ref.shape[1]
    for t in range(2):
        grad = dot_rows(get(2 + 2 * t)[...], get(LOW)[...]) + dot_rows(get(3 + 2 * t)[...], get(LOW_NBR)[...])
        for b in range(4):
            g_ref[4 * t + b] = grad[b * size : (b + 1) * size].astype(BF16)
    give_split(orders, g_ref, sent, kept, place)


def inner_grad_body(orders, place, get, staged, put, *_):
    HID, HID_NBR, LOW, LOW_NBR = range(4)
    sent, kept, sums_ref, g_ref = staged
    for t in range(2):
        dp, dp_nbr, ctx, ctx_nbr = (get(4 + 4 * t + i) for i in range(4))
        grad = dot_rows(get(HID)[...], dp[...]) + dot_rows(get(HID_NBR)[...], dp_nbr[...])
        out = dot_rows(ctx[...], get(LOW)[...]) + dot_rows(ctx_nbr[...], get(LOW_NBR)[...])
        size, piece = grad.shape[0] // 4, out.shape[0] // 8
        for b in range(4):
            g_ref[4 * t + b, :size, :] = grad[b * size : (b + 1) * size].astype(BF16)
            for side in range(2):
                at = (2 * b + side) * piece
                lanes = slice(side * out.shape[1], (side + 1) * out.shape[1])
                g_ref[4 * t + b, size:, lanes] = out[at : at + piece].astype(BF16)
        sums_ref[t : t + 1, :] = jnp.sum(dp[...].astype(F32), 0, keepdims=True) + jnp.sum(
            dp_nbr[...].astype(F32), 0, keepdims=True
        )
    give_split(orders, g_ref, sent, kept, place)


def attn_grad_body(last, orders, place, get, staged, put, *_):
    X, X_NBR, D, D_NBR, BIAS, UNITS, SUMS, SUMS_NBR = range(8)
    if last:
        sent, kept, g_ref = staged
        shared = [
            jnp.sum(get(SUMS)[8 * i : 8 * i + 8, :] + get(SUMS_NBR)[8 * i : 8 * i + 8, :], 0, keepdims=True)
            for i in range(6)
        ]
    else:
        sent, kept, bias_ref, g_ref = staged
    size = g_ref.shape[1]
    wide = g_ref.shape[2] - (128 if last else 0)
    for t in range(2):
        cols = slice(t * wide, (t + 1) * wide)
        d, d_nbr = get(D)[:, cols], get(D_NBR)[:, cols]
        grad = dot_rows(get(X)[...], d) + dot_rows(get(X_NBR)[...], d_nbr)
        for b in range(4):
            g_ref[4 * t + b, :, :wide] = grad[b * size : (b + 1) * size].astype(BF16)
        total = jnp.sum(d.astype(F32), 0, keepdims=True) + jnp.sum(d_nbr.astype(F32), 0, keepdims=True)
        if not last:
            bias_ref[t : t + 1, :] = total
            continue
        before = get(BIAS)[t : t + 1, :]
        third, before_third = wide // 3, before.shape[1] // 3
        rows = [
            *shared, before[:, :before_third], total[:, :third], before[:, 2 * before_third :],
            total[:, 2 * third :], get(UNITS)[t : t + 1, :],
        ]
        flat = jnp.concatenate(
            [row[:, i : i + 128] for row in rows for i in range(0, row.shape[1], 128)], 0
        )
        for b in range(4):
            g_ref[4 * t + b, :, wide:] = jnp.zeros((size, 128), BF16)
        g_ref[4 * t, : flat.shape[0], wide:] = flat.astype(BF16)
    give_split(orders, g_ref, sent, kept, place)


def halve_body(orders, stage, place, get, staged, put, *_):
    a, b = get(0), get(1)
    for mine, ref in ((False, staged[0]), (True, staged[1])):
        for m in range(ref.shape[0]):
            k = split_index(orders, stage, m, mine, place)
            ref[m] = (a[k].astype(F32) + b[k].astype(F32)).astype(BF16)


def add_body(place, get, staged, put, *_):
    staged[0][...] = (get(0)[...].astype(F32) + get(1)[...].astype(F32)).astype(BF16)


def square(place):
    y, z = place.y, place.z
    return (2 * y + z, 2 - 2 * y + z, 2 * y + 1 - z, 3 - 2 * y - z)


def pairs(place):
    y, z = place.y, place.z
    return (y, 1 - y, 2 + z, 3 - z)


def join_body(where, place, get, staged, put, *_):
    ref = staged[0]
    size = ref.shape[0] // 4
    for i, at in enumerate(where(place)):
        ref[strip(at, size), :] = get(i)[...]


def blend(place, pair):
    return pair[0] + place.core * (pair[1] - pair[0])


def join_pair_body(axes, place, get, staged, put, *_):
    at = blend(place, [{"y": place.y, "z": place.z}[axis[0]] for axis in axes])
    staged[0][at] = get(0)[0]
    staged[0][1 - at] = get(1)[0]


def join_blocks_body(axes, place, get, staged, put, *_):
    for i in range(2):
        y, z = (place.y, place.z) if i == 0 else (1 - place.y, 1 - place.z)
        for b in range(2):
            at = blend(place, [2 * y + b if axis[0] == "z" else 2 * b + z for axis in axes])
            staged[0][at] = get(i)[b]


def cores(place, get):
    return (place.core, get(0)), (1 - place.core, get(1))


def outer_out_body(place, get, staged, put, _, __, outs):
    for i in (1, 2):
        put(get(1 + i), outs[i])
    for i, (core, ref) in enumerate(cores(place, get)):
        for b in range(4):
            held = staged[4 * i + b]
            held[...] = ref[b].astype(F32)
            put(held, outs[0].at[strip(4 * core + b, held.shape[0]), :])


def inner_out_body(size, place, get, staged, put, _, __, outs):
    for i, (core, ref) in enumerate(cores(place, get)):
        for b in range(4):
            held = staged[4 * i + b]
            held[...] = ref[b].astype(F32)
            wide = held.shape[1]
            piece = held.shape[0] - size
            put(held.at[:size], outs[0].at[b * size : (b + 1) * size, strip(core, wide)])
            for side in range(2):
                at = (2 * b + side) * piece
                put(
                    held.at[size:, side * (wide // 2) : (side + 1) * (wide // 2)],
                    outs[1].at[at : at + piece, strip(core, wide // 2)],
                )


def attn_out_body(first_col, sizes, place, get, staged, put, _, __, outs):
    for i, (core, ref) in enumerate(cores(place, get)):
        for b in range(4):
            held = staged[4 * i + b]
            held[...] = ref[b].astype(F32)
            size, wide = held.shape[0], held.shape[1] - (128 if sizes else 0)
            rows = strip(4 * core + b, size)
            third = wide // 3
            for part in range(3):
                cols = slice(first_col, first_col + third)
                put(held.at[:, part * third : (part + 1) * third], outs[part].at[rows, cols])
    if not sizes:
        return

    def flat(held, at, size):
        wide = held.shape[1] - 128
        parts = [held[at + i : at + i + 1, wide:] for i in range(size // 128)]
        return jnp.concatenate(parts, 1).reshape(size)

    at = 0
    for ref, out, size in zip(staged[8:], outs[3:], sizes):
        ref[...] = jnp.where(place.core == 0, flat(staged[0], at, size), flat(staged[4], at, size))
        put(ref, out)
        at += size // 128
    size = staged[-1].shape[0]
    for ref, held, core in ((staged[-2], staged[0], place.core), (staged[-1], staged[4], 1 - place.core)):
        ref[...] = flat(held, at, size)
        put(ref, outs[-1].at[strip(core, size)])


def local(
    dp,
    inputs,
    lengths,
    query_weight,
    query_bias,
    key_weight,
    value_weight,
    value_bias,
    output_weight,
    output_bias,
    first_gain,
    first_shift,
    inner_weight,
    inner_bias,
    outer_weight,
    outer_bias,
    second_gain,
    second_shift,
    cotangent,
):
    chains, slots, model = inputs.shape
    rows = chains * slots
    width = query_weight.shape[1]
    units = inner_weight.shape[1]
    group = units // 2
    half = model // 2
    levels = int(math.log2(dp))
    line = Line()

    def bit_swap(v, bit):
        return lax.ppermute(v, DP, [(i, i ^ (1 << bit)) for i in range(dp)])

    def named(swap):
        def run(name, *v):
            with jax.named_scope(name):
                return swap(*v)

        return run

    @named
    def core_swap(v):
        return bit_swap(v, 0)

    @named
    def y_swap(v):
        return bit_swap(v, 1)

    @named
    def z_swap(v):
        return bit_swap(v, 2)

    @named
    def x_swap(v):
        return lax.ppermute(v, TENSOR, [(0, 1), (1, 0)])

    @named
    def diagonal_swap(v):
        return lax.ppermute(v, DP, [(i, i ^ 6) for i in range(dp)])

    @named
    def gather_swap(v, axes, step):
        return lax.ppermute(v, DP, [(i, i ^ (2 if axes[i % 2][step] == "y" else 4)) for i in range(dp)])

    @named
    def order_swap(v, orders, stage):
        pairs = []
        for spot in range(dp):
            for t in range(2):
                d = orders[spot % 2][stage]
                to = (spot, 1 - t) if d == "t" else (spot ^ (2 if d == "y" else 4), t)
                pairs.append((2 * spot + t, 2 * to[0] + to[1]))
        return lax.ppermute(v, (DP, TENSOR), pairs)

    x = inputs.reshape(rows, model)
    cot = cotangent.reshape(rows, model)

    quarter, bit, eighth = model // 4, model // 8, units // 8
    all_rows = slice(None)
    low_width = ((rows, width), BF16)
    low_wide = ((rows, model), BF16)
    wide = ((rows, model), F32)
    act = ((rows, group), BF16)
    pairs_here = width // PAIR
    probs_shape = ((chains * pairs_here, slots, 2 * slots), BF16)
    len_smem = [(lengths.shape, jnp.int32)]
    g = SimpleNamespace()

    def lanes(arr, at, count):
        return piece(arr, (rows, count), lambda p: (all_rows, slice(at, at + count)))

    def spacer(name):
        line(name, lambda *_: None, [], [])

    def pack_attn():
        def body(place, get, staged, put, wait, refs, _):
            core, y, z, _ = place
            for at, row in ((0, y), (1, 2 + z)):
                to = staged[0].at[at * bit : (at + 1) * bit]
                for i, w in enumerate(refs[:3]):
                    put(w.at[strip(4 * core + row, bit), :], to.at[:, i * width : (i + 1) * width])
                put(refs[3].at[strip(row, bit), strip(core, half)], to.at[:, 3 * width :])

        (cut,) = line(
            "p1", body, [], [((2 * bit, 3 * width + half), BF16)],
            hbm=[query_weight, key_weight, value_weight, output_weight],
        )
        g.attn_mine = x_swap("ax", cut)

    def pack_rest():
        def body(place, get, staged, put, wait, refs, _):
            w_in, w_out, bq, bv, bi = refs
            wi_ref, wo_ref, bias_ref = staged
            core, y, z, _ = place
            put(w_in.at[strip(2 * y + z, quarter), strip(core, group)], wi_ref)
            put(w_out.at[strip(4 * core + y, eighth), :], wo_ref.at[:eighth])
            put(w_out.at[strip(4 * core + 2 + z, eighth), :], wo_ref.at[eighth:])
            put(bq, bias_ref.at[pl.ds(0, width)])
            put(bv, bias_ref.at[pl.ds(width, width)])
            put(bi, bias_ref.at[pl.ds(2 * width, units)])

        wi_cut, wo_cut, biases = line(
            "p2", body, [],
            [
                ((quarter, group), BF16), ((2 * eighth, model), BF16), ((2 * width + units,), F32),
            ],
            hbm=[inner_weight, outer_weight, query_bias, value_bias, inner_bias],
        )
        g.biases = x_swap("bx", biases)
        g.wi_mine = x_swap("wix", wi_cut)
        g.wo_mine = x_swap("wox", wo_cut)

    def relay(name, arr, parts, seen=()):
        dims = (arr.shape[0] // parts, arr.shape[1])
        return line(
            name, lambda p, get, staged, put, *_: [put(get(i), staged[i]) for i in range(parts)],
            [
                piece(arr, dims, lambda p, i=i: (slice(i * dims[0], (i + 1) * dims[0]), all_rows))
                for i in range(parts)
            ],
            [(dims, BF16)] * parts, seen=seen,
        )

    def join_four(name, where, pieces):
        dims = (4 * pieces[0].shape[0], pieces[0].shape[1])
        (own,) = line(name, lambda *a: join_body(where, *a), [load(v) for v in pieces], [(dims, BF16)])
        return own, core_swap(name + "c", own)

    def relay_attn():
        g.attn_a, g.attn_b = relay("ra", g.attn_mine, 2, [g.biases])
        g.attn_y, g.attn_z = y_swap("ay", g.attn_a), z_swap("az", g.attn_b)

    def relay_in():
        (g.wi_own,) = relay("rw", g.wi_mine, 1)
        v = g.wi_own
        g.wi_pieces = [v, y_swap("wiy", v), z_swap("wiz", v), diagonal_swap("wid", v)]

    def relay_out():
        g.wo_a, g.wo_b = relay("ro", g.wo_mine, 2)
        g.wo_y, g.wo_z = y_swap("woy", g.wo_a), z_swap("woz", g.wo_b)

    def join_attn():
        g.attn_weights = join_four("ja", pairs, [g.attn_a, g.attn_y, g.attn_b, g.attn_z])

    def join_in():
        g.wi_b, g.wi_a = join_four("jw", square, g.wi_pieces)

    def join_out():
        g.wo_b, g.wo_a = join_four("jo", pairs, [g.wo_a, g.wo_y, g.wo_b, g.wo_z])

    def attn_fwd_own():
        args = [
            x, query_weight, key_weight, value_weight, output_weight, inner_bias, cot, output_bias, first_gain,
            first_shift, outer_bias, second_gain, second_shift,
        ]
        *args, q, k, v, probs, g.joint, g.part_own = line(
            "f1", lambda *a: attn_fwd_own_body(chains, *a), [],
            [(arr.shape, arr.dtype) for arr in args] + [low_width] * 3 + [probs_shape, ((rows, width + half), BF16), wide],
            hbm=[*args, query_bias, value_bias, lengths],
            scratch=[(query_bias.shape, F32), (value_bias.shape, F32)], smem=len_smem, copies=len(args) + 4,
        )
        (
            g.x, g.wq, g.wk, g.wv, g.wo_attn, g.bi, g.cot,
            g.output_bias, g.first_gain, g.first_shift, g.outer_bias, g.second_gain, g.second_shift,
        ) = args
        g.wi, g.wo = inner_weight, outer_weight
        g.own = [load(arr) for arr in (g.wo_attn, q, k, v, probs, g.wq, g.wk, g.wv)]

    def bias_oth(at, size):
        return Load((size,), F32, [(g.biases, lambda p: (pl.ds(pl.multiple_of(at(p), 128), size),), None)])

    def attn_fwd_oth():
        q, k, v, probs, g.r1, joint, w, wo = line(
            "f2", lambda *a: attn_fwd_oth_body(chains, width, *a),
            [
                load(g.x), bias_oth(lambda p: 0, width), bias_oth(lambda p: width, width),
                *(load(v) for v in (g.part_own, g.output_bias, g.first_gain, g.first_shift, *g.attn_weights, g.joint)),
            ],
            [low_width] * 3
            + [probs_shape, wide, ((rows, model + 2 * width + half), BF16)]
            + [((model, 3 * width), BF16), ((width, model), BF16)],
            hbm=[lengths], smem=len_smem,
        )
        g.oth = [load(arr) for arr in (wo, q, k, v, probs)] + [
            piece(w, (model, width), lambda p, i=i: (all_rows, slice(i * width, (i + 1) * width))) for i in range(3)
        ]
        g.hid, g.ctx_oth = lanes(joint, 0, model), lanes(joint, model, width)
        g.hid_nbr_all = core_swap("hc", joint)
        g.hid_nbr, g.ctx_oth_nbr = lanes(g.hid_nbr_all, 0, model), lanes(g.hid_nbr_all, model, width)
        g.ctx_own, g.ctx_own_nbr = (lanes(v, model + width, width) for v in (joint, g.hid_nbr_all))
        g.x_nbr = lanes(g.hid_nbr_all, model + 2 * width, half)

    def flipped(p, flip):
        return 1 - p.core if flip else p.core

    def wi_own(flip):
        return piece(g.wi, (model, group), lambda p: (all_rows, strip(flipped(p, flip), group)))

    def wo_own(flip):
        return piece(g.wo, (group, model), lambda p: (strip(flipped(p, flip), group), all_rows))

    def bi_own(flip):
        return piece(g.bi, (group,), lambda p: (strip(flipped(p, flip), group),))

    def bi_oth(flip):
        return bias_oth(lambda p: 2 * width + flipped(p, flip) * group, group)

    def ffn_own():
        g.acta_own, g.actb_own, g.dga_own, g.dgb_own, g.ffn_own = line(
            "n1", ffn_own_body,
            [g.hid, wi_own(True), bi_own(True), wi_own(False), bi_own(False), wo_own(True), wo_own(False)],
            [act] * 4 + [wide],
        )
        g.acta_own_nbr = core_swap("a1", g.acta_own)

    def ffn_oth_pre():
        g.acta_oth, g.actb_oth, g.dga_oth, g.dgb_oth = line(
            "m2", ffn_pre_body, [g.hid, load(g.wi_a), bi_oth(True), load(g.wi_b), bi_oth(False)], [act] * 4,
            seen=[g.hid_nbr_all],
        )
        g.acta_oth_nbr = core_swap("a2", g.acta_oth)

    def ffn_oth_post():
        names = (g.outer_bias, g.second_gain, g.second_shift, g.cot)
        g.result, g.dr2, g.low2, g.sums2 = line(
            "n2", ffn_post_body,
            [
                load(v)
                for v in (
                    g.acta_oth, g.actb_oth, g.wo_a, g.wo_b, g.ffn_own, g.r1, g.first_gain, g.first_shift, *names,
                )
            ],
            [low_wide, wide, low_wide, ((24, model), F32)], seen=[g.acta_own_nbr],
        )
        g.low2_nbr = core_swap("lo", g.low2)

    def ffn_bwd_oth():
        g.dpa_oth, g.dpb_oth, g.back = line(
            "k2", lambda *a: ffn_bwd_body(False, *a),
            [load(v) for v in (g.low2, g.wo_a, g.dga_oth, g.wo_b, g.dgb_oth, g.wi_a, g.wi_b, g.dr2)],
            [act] * 2 + [wide],
        )
        g.dpa_oth_nbr = core_swap("pb", g.dpa_oth)

    def ffn_bwd_own():
        joint, g.dpb_own, g.dr1, g.low1, g.sums = line(
            "k1", lambda *a: ffn_bwd_body(True, *a),
            [
                load(g.low2), wo_own(True), load(g.dga_own), wo_own(False), load(g.dgb_own),
                wi_own(True), wi_own(False), load(g.back), load(g.r1), load(g.first_gain), load(g.sums2),
            ],
            [((rows, group + half), BF16), act, wide, low_wide, ((48, model), F32)],
        )
        joint_nbr = core_swap("pl", joint)
        g.dpa_own_nbr, g.low1_nbr = lanes(joint_nbr, 0, group), lanes(joint_nbr, group, half)
        g.sums_nbr = core_swap("s", g.sums)

    def split_outs(dims):
        return [((4, *dims), BF16), ((4, *dims), BF16)]

    dims_of = {
        OUTER: (group // 4, model),
        INNER: (model // 4 + width // 8, group),
        ATTN: (half // 4, 3 * (pairs_here - 1) * PAIR),
        LAST: (half // 4, 3 * PAIR + 128),
    }
    held, made = {}, {}

    def grad(name, body, loads, outs=(), seen=()):
        sent, kept, *rest = line(
            name + "0", lambda *a: body(ORDERS[name], *a), loads, split_outs(dims_of[name]) + [*outs],
            scratch=[((8, *dims_of[name]), BF16)], seen=seen,
        )
        held[name] = kept, order_swap(name + "0", sent, ORDERS[name], 0)
        return rest

    def outer_grad():
        names = (g.low2, g.low2_nbr, g.actb_own, g.acta_own_nbr, g.actb_oth, g.acta_oth_nbr)
        grad(OUTER, outer_grad_body, [load(v) for v in names])

    def inner_grad():
        loads = [
            g.hid, g.hid_nbr, piece(g.low1, (rows, half), lambda p: (all_rows, strip(p.core, half))), g.low1_nbr,
            load(g.dpb_own), g.dpa_own_nbr, g.ctx_own, g.ctx_own_nbr,
            load(g.dpb_oth), load(g.dpa_oth_nbr), g.ctx_oth, g.ctx_oth_nbr,
        ]
        (g.unit_sums,) = grad(INNER, inner_grad_body, loads, [((8, group), F32)])

    def attn_bwd(name, first_pair, last_pair, acc):
        count = last_pair - first_pair
        d, g.back_in = line(
            name, lambda *a: attn_bwd_body(first_pair, last_pair, chains, *a),
            [load(g.low1), load(acc), *g.own, *g.oth],
            [((rows, 6 * count * PAIR), BF16), wide],
            scratch=[((rows, count * PAIR), BF16), ((model, 6 * count * PAIR), BF16)],
        )
        return d, core_swap(name + "c", d)

    def attn_bwd_most():
        g.d_most = attn_bwd("ba", 0, pairs_here - 1, g.dr1)

    def attn_bwd_rest():
        g.d_rest = attn_bwd("bb", pairs_here - 1, pairs_here, g.back_in)

    def attn_grad(name, d, more, outs=()):
        x_cut = piece(g.x, (rows, half), lambda p: (all_rows, strip(p.core, half)))
        loads = [x_cut, g.x_nbr, *(load(v) for v in (*d, *more))]
        return grad(name, lambda *a: attn_grad_body(name == LAST, *a), loads, outs)

    def attn_grad_most():
        (g.bias_sums,) = attn_grad(ATTN, g.d_most, [], [((8, dims_of[ATTN][1]), F32)])

    def attn_grad_rest():
        attn_grad(LAST, g.d_rest, [g.bias_sums, g.unit_sums, g.sums, g.sums_nbr])

    def halve(name, stage):
        kept, recv = held[name]
        orders = ORDERS[name]
        out = ((kept.shape[0] // 2, *kept.shape[1:]), BF16)
        sent, kept = line(
            name + str(stage), lambda *a: halve_body(orders, stage, *a), [load(kept), load(recv)], [out, out]
        )
        held[name] = kept, order_swap(name + str(stage), sent, orders, stage)

    def add(kernel, name, bit):
        a, b = held[name]
        (v,) = line(kernel, add_body, [load(a), load(b)], [(a.shape, BF16)])
        if bit < levels:
            with jax.named_scope(name + str(bit)):
                held[name] = v, bit_swap(v, bit)
            return
        held[name] = v, gather_swap(name + "n", v, GATHER[name], 0)

    def level(name):
        for bit in range(4, levels + 1):
            add(name + "l", name, bit)

    def join_pair(name):
        (v,) = line(
            name + "m", lambda *a: join_pair_body(GATHER[name], *a), [load(v) for v in held[name]],
            [((2, *dims_of[name]), BF16)],
        )
        held[name] = v, gather_swap(name + "p", v, GATHER[name], 1)

    def join(name):
        (v,) = line(
            name + "j", lambda *a: join_blocks_body(GATHER[name], *a), [load(v) for v in held[name]],
            [((4, *dims_of[name]), BF16)],
        )
        held[name] = v, core_swap(name + "c", v)

    def write(name, body, outs, copies, more=(), onto=(), loads=(), low_outs=()):
        made[name] = line(
            name + "w", body, [load(v) for v in (*held[name], *loads)], [], hbm=onto,
            hbm_outs=[(dims, F32) for dims in outs] + [(dims, BF16) for dims in low_outs],
            scratch=[(dims_of[name], F32)] * 8 + [((size,), F32) for size in more], copies=copies,
            aliases={i: i for i in range(len(onto))},
        )

    sizes = [model] * 6 + [width] * 2
    attn_outs = [(model, width)] * 3
    last_outs = attn_outs + [(size,) for size in sizes] + [(units,)]
    steps = {
        "p1": pack_attn, "p2": pack_rest, "ra": relay_attn, "rw": relay_in, "ro": relay_out,
        "ja": join_attn, "jw": join_in, "jo": join_out,
        "f1": attn_fwd_own, "f2": attn_fwd_oth, "n1": ffn_own, "m2": ffn_oth_pre, "n2": ffn_oth_post,
        "k2": ffn_bwd_oth, "k1": ffn_bwd_own, "ba": attn_bwd_most, "bb": attn_bwd_rest,
        "O0": outer_grad, "I0": inner_grad, "A0": attn_grad_most, "B0": attn_grad_rest,
        "Ow": lambda: write(
            OUTER, outer_out_body, [(units, model), (rows, model)], 10, loads=[g.back_in, g.result],
            low_outs=[(rows, model)],
        ),
        "Iw": lambda: write(
            INNER, lambda *a: inner_out_body(model // 4, *a), [(model, units), (width, model)], 24
        ),
        "Aw": lambda: write(ATTN, lambda *a: attn_out_body(0, (), *a), attn_outs, 24),
        "Bw": lambda: write(
            LAST, lambda *a: attn_out_body((pairs_here - 1) * PAIR, sizes, *a), last_outs, 34,
            [*sizes, group, group], made[ATTN],
        ),
    }
    for name in (OUTER, INNER, ATTN, LAST):
        steps[name + "1"] = lambda name=name: halve(name, 1)
        steps[name + "2"] = lambda name=name: halve(name, 2)
        steps[name + "3"] = lambda name=name: add(name + "3", name, 3)
        steps[name + "l"] = lambda name=name: level(name)
        steps[name + "m"] = lambda name=name: join_pair(name)
        steps[name + "j"] = lambda name=name: join(name)
    for step in ORDER:
        steps.get(step, lambda step=step: spacer(step))()
    grad_outer, grad_inputs, result = made[OUTER]
    grad_inner, grad_out = made[INNER]
    grad_q, grad_k, grad_v, g_sg, g_ss, g_ob2, g_fg, g_fs, g_ob1, g_qb, g_vb, g_ib = made[LAST]

    def back_to(v):
        return v.reshape(chains, slots, model)

    return (
        back_to(result), back_to(grad_inputs),
        grad_q, g_qb, grad_k, grad_v, g_vb, grad_out, g_ob1, g_fg, g_fs,
        grad_inner, g_ib, grad_outer, g_ob2, g_sg, g_ss,
    )


def solution(mesh):
    dp = mesh.shape[DP]
    rows, cols, low = P((DP, TENSOR), None, None), P(None, TENSOR), P(TENSOR, None)
    part, full = P(TENSOR), P()
    in_specs = (
        rows, P(DP), cols, part, cols, cols, part, low, full, full, full, cols, part, low, full, full, full, rows,
    )
    out_specs = (
        rows, rows, cols, part, cols, cols, part, low, full, full, full, cols, part, low, full, full, full,
    )

    def run(*args):
        return local(dp, *args)

    return jax.shard_map(run, mesh=mesh, in_specs=in_specs, out_specs=out_specs, check_vma=False)
```

```python
import math
from types import SimpleNamespace
from typing import NamedTuple

import jax
import jax.numpy as jnp
from jax import lax
from jax.experimental import pallas as pl
from jax.experimental.pallas import tpu as pltpu
from jax.sharding import PartitionSpec as P

HDIM = 64
PAIR = 2 * HDIM
SCALING = 1.0 / math.sqrt(HDIM)
ORDER = (
    "p1", "p2", "f1", "ra", "rw", "ja", "ro", "f2", "jw", "n1", "jo", "m2", "n2", "k2", "O0", "k1", "ba", "O1",
    "I0", "A0", "bb", "O2", "I1", "A1", "O3", "B0", "I2", "A2", "Ol", "B1", "I3", "A3", "Om", "Il", "B2", "Oj",
    "B3", "Al", "Im", "Bl", "Am", "Ow", "Ij", "Bm", "Aj", "Iw", "Bj", "Aw", "Bw",
)
COSTS = {
    "p1": 150, "p2": 150, "f1": 0, "ra": 150, "rw": 150, "ja": 150, "ro": 150, "f2": 150, "jw": 150, "n1": 10,
    "jo": 150, "m2": 150, "n2": 10, "k2": 150, "O0": 150, "k1": 0, "ba": 10, "O1": 150, "I0": 150, "A0": 150,
    "bb": 0, "O2": 150, "I1": 0, "A1": 0, "O3": 0, "B0": 150, "I2": 0, "A2": 150, "Ol": 0, "I3": 150, "B1": 30,
    "A3": 150, "Om": 0, "Il": 150, "B2": 30, "Oj": 150, "Al": 150, "B3": 150, "Im": 150, "Am": 150, "Bl": 150,
    "Ow": 150, "Ij": 150, "Bm": 150, "Aj": 150, "Iw": 150, "Bj": 150, "Aw": 150, "Bw": 150,
}
ROWS = 160
VMEM = {"p1": 56, "p2": 56, "f1": 30, "n2": 14}
BF16 = jnp.bfloat16
F32 = jnp.float32

DP, TENSOR = "dp", "tensor"
OUTER, INNER, ATTN, LAST = "O", "I", "A", "B"
ORDERS = {OUTER: ("yzt", "tzy"), INNER: ("tyz", "yzt"), ATTN: ("zty", "zyt"), LAST: ("yzt", "tyz")}
GATHER = {OUTER: ("zy", "yz"), INNER: ("yz", "zy"), ATTN: ("yz", "zy"), LAST: ("zy", "yz")}


def dot(a, b):
    return lax.dot_general(a, b, (((1,), (0,)), ((), ())), preferred_element_type=F32)


def dot_t(a, b):
    return lax.dot_general(a, b, (((1,), (1,)), ((), ())), preferred_element_type=F32)


def dot_rows(a, b):
    return lax.dot_general(a, b, (((0,), (0,)), ((), ())), preferred_element_type=F32)


def row_stats(rows):
    center = rows - jnp.mean(rows, -1, keepdims=True)
    inverse = lax.rsqrt(jnp.mean(center * center, -1, keepdims=True) + 1e-05)
    return center * inverse, inverse


def norm_back(scaled, normed, inverse):
    return inverse * (
        scaled
        - jnp.mean(scaled, -1, keepdims=True)
        - normed * jnp.mean(scaled * normed, -1, keepdims=True)
    )


def lanes_of(ref):
    return ref[...].reshape(1, -1)


def strip(index, size, base=0):
    return pl.ds(pl.multiple_of(base + index * size, size), size)


class Place(NamedTuple):
    core: jax.Array
    y: jax.Array
    z: jax.Array
    t: jax.Array


class Load(NamedTuple):
    shape: tuple
    dtype: jnp.dtype
    parts: list


def load(arr):
    return Load(arr.shape, arr.dtype, [(arr, None, None)])


def piece(arr, dims, src):
    return Load(dims, arr.dtype, [(arr, src, None)])


def view(ref, at, place):
    return ref if at is None else ref.at[at(place)]


class Line:
    def __init__(self):
        self.token = []

    def __call__(self, name, body, loads, outs, hbm=(), hbm_outs=(), scratch=(), smem=(), copies=8,
                 seen=(), aliases=None):
        loads = [*loads, *(load(arr) for arr in seen)]
        parts = [part for item in loads for part in item.parts]
        copied = [item for item in loads if len(item.parts) > 1 or len(item.shape) == 1 and item.parts[0][1]]
        n_copied = sum(len(item.parts) for item in copied)
        n_token = len(self.token)

        def run(*refs):
            refs = list(refs)

            def take(count):
                got = refs[:count]
                del refs[:count]
                return got

            hbm_refs, part_refs = take(len(hbm)), take(len(parts))
            take(n_token)
            out_refs, hbm_out_refs, (token_ref,) = take(len(outs)), take(len(hbm_outs)), take(1)
            joined, scratch_refs, smem_refs = take(len(copied)), take(len(scratch)), take(len(smem))
            in_sem, out_sem = refs
            spot = lax.axis_index(DP)
            place = Place(
                lax.rem(spot, 2), lax.rem(spot // 2, 2), lax.rem(spot // 4, 2), lax.axis_index(TENSOR)
            )
            ready, pending = [], []
            sem = 0
            for item in loads:
                own = [part_refs.pop(0) for _ in item.parts]
                waits = []
                if any(item is c for c in copied):
                    ref = joined.pop(0)
                    for src_ref, (_, src, dst) in zip(own, item.parts):
                        waits.append(
                            pltpu.make_async_copy(
                                view(src_ref, src, place), view(ref, dst, place), in_sem.at[sem]
                            )
                        )
                        waits[-1].start()
                        sem += 1
                else:
                    ref = view(own[0], item.parts[0][1], place)
                ready.append(ref)
                pending.append(waits)
            stores, waited = [], []

            def wait(*copies):
                for copy in copies:
                    copy.wait()
                    waited.append(copy)

            def get(i):
                for copy in pending[i]:
                    copy.wait()
                pending[i] = []
                return ready[i]

            def put(src, dst):
                copy = pltpu.make_async_copy(src, dst, out_sem.at[len(stores)])
                copy.start()
                stores.append(copy)
                return copy

            body(place, get, [*out_refs, *scratch_refs], put, wait, hbm_refs, hbm_out_refs, *smem_refs)
            token_ref[...] = jnp.zeros(token_ref.shape, F32)
            for i in range(len(loads)):
                get(i)
            for copy in stores:
                if all(copy is not done for done in waited):
                    copy.wait()

        in_vmem = pl.BlockSpec(memory_space=pltpu.VMEM)
        in_hbm = pl.BlockSpec(memory_space=pltpu.HBM)
        *results, token = pl.pallas_call(
            run,
            out_shape=[jax.ShapeDtypeStruct(s, d) for s, d in [*outs, *hbm_outs, ((8, 128), F32)]],
            in_specs=[in_hbm] * len(hbm)
            + [in_vmem] * (len(parts) + n_token),
            out_specs=[in_vmem] * len(outs) + [in_hbm] * len(hbm_outs) + [in_vmem],
            scratch_shapes=[pltpu.VMEM(item.shape, item.dtype) for item in copied]
            + [pltpu.VMEM(s, d) for s, d in scratch]
            + [pltpu.SMEM(s, d) for s, d in smem]
            + [pltpu.SemaphoreType.DMA((max(n_copied, 1),)), pltpu.SemaphoreType.DMA((copies,))],
            compiler_params=pltpu.CompilerParams(vmem_limit_bytes=VMEM.get(name, 10) << 20),
            input_output_aliases=aliases or {},
            cost_estimate=pl.CostEstimate(flops=COSTS.get(name, 0) * 10**8, bytes_accessed=0, transcendentals=0),
            name=name,
        )(*hbm, *[arr for arr, _, _ in parts], *self.token)
        self.token = [token]
        return results


def heads_apart(v, first):
    return jnp.concatenate([jnp.where(first, v, 0), jnp.where(first, 0, v)], 0)


def attend(q_ref, k_ref, v_ref, probs_ref, ctx_ref, len_ref, len_at, chains):
    slots = q_ref.shape[0] // chains
    first = lax.broadcasted_iota(jnp.int32, (slots, PAIR), 1) < HDIM
    spot = lax.broadcasted_iota(jnp.int32, (slots, 2 * slots), 0)
    for chain in range(chains):
        rows = slice(chain * slots, (chain + 1) * slots)
        valid = spot < len_ref[len_at + chain]
        for at in range(0, q_ref.shape[1], PAIR):
            q_both = heads_apart(q_ref[rows, at : at + PAIR], first)
            scores = jnp.where(valid, dot_t(k_ref[rows, at : at + PAIR], q_both) * SCALING, -1e30)
            grown = jnp.exp(scores - jnp.max(scores, 0, keepdims=True))
            probs = (grown * (1.0 / jnp.sum(grown, 0, keepdims=True))).astype(BF16)
            probs_ref[(chain * q_ref.shape[1] + at) // PAIR] = probs
            both = dot_rows(probs, v_ref[rows, at : at + PAIR])
            ctx_ref[rows, at : at + PAIR] = jnp.where(first, both[:slots], both[slots:]).astype(BF16)


def attn_fwd_own_body(chains, place, get, staged, put, wait, hbm, _, len_ref):
    x_ref, wq, wk, wv, wo = staged[:5]
    later = staged[5 : len(hbm) - 3]
    q_ref, k_ref, v_ref, probs_ref, joint_ref, part_ref, bq, bv = staged[len(hbm) - 3 :]
    width = q_ref.shape[1]
    half = joint_ref.shape[1] - width
    ctx_ref = joint_ref.at[:, :width]
    lens = put(hbm[-1], len_ref)
    first = [put(hbm[0], x_ref), put(hbm[1], wq), put(hbm[-3], bq)]
    second = [put(hbm[2], wk), put(hbm[3], wv), put(hbm[-2], bv)]
    wait(*first)
    third = put(hbm[4], wo)
    put(hbm[0].at[:, strip(1 - place.core, half)], joint_ref.at[:, width:])
    x = x_ref[...]
    q_ref[...] = (dot(x, wq[...]) + lanes_of(bq)).astype(BF16)
    wait(*second)
    for src, dst in zip(hbm[5:-3], later):
        put(src, dst)
    k_ref[...] = dot(x, wk[...]).astype(BF16)
    v_ref[...] = (dot(x, wv[...]) + lanes_of(bv)).astype(BF16)
    wait(lens)
    attend(q_ref, k_ref, v_ref, probs_ref, ctx_ref, len_ref, place.t * chains, chains)
    wait(third)
    part_ref[...] = dot(ctx_ref[...], wo[...])


def attn_fwd_oth_body(chains, width, place, get, staged, put, wait, hbm, _, len_ref):
    X, BQ, BV, ACC, OB, FG, FS, MINE, OTHER, OWN = range(10)
    q_ref, k_ref, v_ref, probs_ref, r1_ref, joint_ref, w_ref, wo_ref = staged
    copies = []
    for core, i in ((place.core, MINE), (1 - place.core, OTHER)):
        ref = get(i)
        half = ref.shape[0]
        copies.append(put(ref.at[:, : 3 * width], w_ref.at[strip(core, half), :]))
        copies.append(put(ref.at[:, 3 * width :], wo_ref.at[:, strip(core, half)]))
    model = r1_ref.shape[1]
    hid_ref, ctx_ref = joint_ref.at[:, :model], joint_ref.at[:, model : model + width]
    put(get(OWN), joint_ref.at[:, model + width :])
    lens = put(hbm[0], len_ref)
    x = get(X)[...]
    wait(*copies)
    wq, wk, wv = (w_ref.at[:, i * width : (i + 1) * width] for i in range(3))
    q_ref[...] = (dot(x, wq[...]) + lanes_of(get(BQ))).astype(BF16)
    k_ref[...] = dot(x, wk[...]).astype(BF16)
    v_ref[...] = (dot(x, wv[...]) + lanes_of(get(BV))).astype(BF16)
    wait(lens)
    attend(q_ref, k_ref, v_ref, probs_ref, ctx_ref, len_ref, place.t * chains, chains)
    r1_ref[...] = dot(ctx_ref[...], wo_ref[...])
    acc_ref, x_ref = get(ACC), get(X)
    bias, gain, shift = lanes_of(get(OB)), lanes_of(get(FG)), lanes_of(get(FS))

    for at in range(0, x.shape[0], ROWS):
        rows = slice(at, at + ROWS)
        r1 = x_ref[rows, :].astype(F32) + (r1_ref[rows, :] + acc_ref[rows, :]) + bias
        r1_ref[rows, :] = r1
        normed, _ = row_stats(r1)
        hid_ref[rows, :] = (normed * gain + shift).astype(BF16)


def gelu_all(hid, weights, biases, acts, slopes):
    for wi_ref, bi_ref, act_ref, slope_ref in zip(weights, biases, acts, slopes):
        pre = dot(hid, wi_ref[...]) + lanes_of(bi_ref)
        cdf = 0.5 + 0.5 * lax.erf(pre * math.sqrt(0.5))
        act_ref[...] = (pre * cdf).astype(BF16)
        bell = jnp.exp(pre * pre * -0.5) * (1.0 / math.sqrt(2 * math.pi))
        slope_ref[...] = (cdf + pre * bell).astype(BF16)


def ffn_own_body(place, get, staged, put, *_):
    HID, WIA, BIA, WIB, BIB, WOA, WOB = range(7)
    acts = staged[:2]
    gelu_all(get(HID)[...], (get(WIA), get(WIB)), (get(BIA), get(BIB)), acts, staged[2:4])
    staged[4][...] = dot(acts[0][...], get(WOA)[...]) + dot(acts[1][...], get(WOB)[...])


def ffn_pre_body(place, get, staged, put, *_):
    HID, WIA, BIA, WIB, BIB = range(5)
    gelu_all(get(HID)[...], (get(WIA), get(WIB)), (get(BIA), get(BIB)), staged[:2], staged[2:])


def ffn_post_body(place, get, staged, put, *_):
    ACTA, ACTB, WOA, WOB, ACC, R1, FG, FS, OB, SG, SS, COT = range(12)
    out_ref, dr2_ref, low_ref, sums_ref = staged
    dr2_ref[...] = dot(get(ACTA)[...], get(WOA)[...]) + dot(get(ACTB)[...], get(WOB)[...])
    acc_ref, r1_ref, cot_ref = get(ACC), get(R1), get(COT)
    first_gain, first_shift, bias = lanes_of(get(FG)), lanes_of(get(FS)), lanes_of(get(OB))
    gain, shift = lanes_of(get(SG)), lanes_of(get(SS))
    sums_ref[...] = jnp.zeros(sums_ref.shape, F32)

    for at in range(0, dr2_ref.shape[0], ROWS):
        rows = slice(at, at + ROWS)
        normed, _ = row_stats(r1_ref[rows, :])
        r2 = normed * first_gain + first_shift + (dr2_ref[rows, :] + acc_ref[rows, :]) + bias
        normed, inverse = row_stats(r2)
        out_ref[rows, :] = (normed * gain + shift).astype(BF16)
        cot = cot_ref[rows, :].astype(F32)
        dr2 = norm_back(cot * gain, normed, inverse)
        low = dr2.astype(BF16)
        low_ref[rows, :] = low
        dr2_ref[rows, :] = dr2
        for i, v in enumerate((cot * normed, cot, low.astype(F32))):
            sums_ref[8 * i : 8 * i + 8, :] += jnp.sum(v.reshape(-1, 8, v.shape[1]), 0)


def ffn_bwd_body(last, place, get, staged, put, *_):
    LOW, WOA, DGA, WOB, DGB, WIA, WIB, ACC = range(8)
    low2 = get(LOW)[...]
    if last:
        joint_ref, *staged = staged
        group = staged[0].shape[1]
        staged = [joint_ref.at[:, :group], *staged]
    for g, (wo, dg) in enumerate(((WOA, DGA), (WOB, DGB))):
        dp_ref = staged[g]
        dp_ref[...] = (dot_t(low2, get(wo)[...]) * get(dg)[...].astype(F32)).astype(BF16)
    total = dot_t(staged[0][...], get(WIA)[...]) + dot_t(staged[1][...], get(WIB)[...])
    if not last:
        staged[2][...] = total + get(ACC)[...]
        return
    R1, FG, SUMS2 = 8, 9, 10
    dr1_ref, low_ref, sums_ref = staged[2:]
    dr1_ref[...] = total
    acc_ref, r1_ref, gain = get(ACC), get(R1), lanes_of(get(FG))
    half = low_ref.shape[1] // 2
    sums_ref[:24, :] = get(SUMS2)[...]
    sums_ref[24:, :] = jnp.zeros((24, sums_ref.shape[1]), F32)

    for at in range(0, low2.shape[0], ROWS):
        rows = slice(at, at + ROWS)
        dhid = dr1_ref[rows, :] + acc_ref[rows, :]
        normed, inverse = row_stats(r1_ref[rows, :])
        dr1 = norm_back(dhid * gain, normed, inverse)
        low = dr1.astype(BF16)
        low_ref[rows, :] = low
        dr1_ref[rows, :] = dr1
        for i, v in enumerate((dhid * normed, dhid, low.astype(F32))):
            sums_ref[24 + 8 * i : 32 + 8 * i, :] += jnp.sum(v.reshape(-1, 8, v.shape[1]), 0)

    joint_ref[:, group:] = low_ref[:, strip(1 - place.core, half)]


def attn_bwd_body(first_pair, last_pair, chains, place, get, staged, put, wait, *_):
    LOW, ACC = 0, 1
    d_ref, out_ref, dc_ref, w_ref = staged
    wide = dc_ref.shape[1]
    slots = d_ref.shape[0] // chains
    first = lax.broadcasted_iota(jnp.int32, (slots, PAIR), 1) < HDIM
    cols = slice(first_pair * PAIR, last_pair * PAIR)
    copies = [
        put(get(7 + 8 * half + i).at[:, cols], w_ref.at[:, (3 * half + i) * wide : (3 * half + i + 1) * wide])
        for half in range(2)
        for i in range(3)
    ]
    for half in range(2):
        wo_ref, q_ref, k_ref, v_ref, probs_ref = (get(2 + 8 * half + i) for i in range(5))
        base = 3 * half * wide
        dc_ref[...] = dot_t(get(LOW)[...], wo_ref[cols, :]).astype(BF16)
        for chain in range(chains):
            rows = slice(chain * slots, (chain + 1) * slots)
            for pair in range(first_pair, last_pair):
                lanes = slice(pair * PAIR, (pair + 1) * PAIR)
                at = (pair - first_pair) * PAIR
                k = k_ref[rows, lanes]
                q_both = heads_apart(q_ref[rows, lanes], first)
                dc_both = heads_apart(dc_ref[rows, at : at + PAIR], first)
                probs_low = probs_ref[chain * (q_ref.shape[1] // PAIR) + pair]
                probs = probs_low.astype(F32)
                dprobs = dot_t(v_ref[rows, lanes], dc_both)
                dscores = (probs * (dprobs - jnp.sum(probs * dprobs, 0, keepdims=True))).astype(BF16)
                dq = dot_rows(dscores, k)
                dq = jnp.where(first, dq[:slots], dq[slots:])
                at += base
                d_ref[rows, at : at + PAIR] = (dq * SCALING).astype(BF16)
                d_ref[rows, at + wide : at + wide + PAIR] = (dot(dscores, q_both) * SCALING).astype(BF16)
                d_ref[rows, at + 2 * wide : at + 2 * wide + PAIR] = dot(probs_low, dc_both).astype(BF16)
    wait(*copies)
    out_ref[...] = get(ACC)[...] + dot_t(d_ref[...], w_ref[...])


def block_index(order, stage, m, mine, place):
    left = [d for d in "tyz" if d not in order[:stage]]
    rest = [d for d in left if d != order[stage]]
    here = {"t": 0, "y": place.y, "z": place.z}[order[stage]]
    index = 0
    for d in left:
        if d == order[stage]:
            bit = here if mine else 1 - here
        else:
            bit = (m >> (len(rest) - 1 - rest.index(d))) & 1
        index = index * 2 + bit
    return index


def split_index(orders, stage, m, mine, place):
    a, b = (block_index(order, stage, m, mine, place) for order in orders)
    return a + place.core * (b - a)


def give_split(orders, blocks, sent, kept, place):
    for mine, ref in ((False, sent), (True, kept)):
        for m in range(ref.shape[0]):
            ref[m] = blocks[split_index(orders, 0, m, mine, place)]


def outer_grad_body(orders, place, get, staged, put, *_):
    LOW, LOW_NBR = 0, 1
    sent, kept, g_ref = staged
    size = g_ref.shape[1]
    for t in range(2):
        grad = dot_rows(get(2 + 2 * t)[...], get(LOW)[...]) + dot_rows(get(3 + 2 * t)[...], get(LOW_NBR)[...])
        for b in range(4):
            g_ref[4 * t + b] = grad[b * size : (b + 1) * size].astype(BF16)
    give_split(orders, g_ref, sent, kept, place)


def inner_grad_body(orders, place, get, staged, put, *_):
    HID, HID_NBR, LOW, LOW_NBR = range(4)
    sent, kept, sums_ref, g_ref = staged
    for t in range(2):
        dp, dp_nbr, ctx, ctx_nbr = (get(4 + 4 * t + i) for i in range(4))
        grad = dot_rows(get(HID)[...], dp[...]) + dot_rows(get(HID_NBR)[...], dp_nbr[...])
        out = dot_rows(ctx[...], get(LOW)[...]) + dot_rows(ctx_nbr[...], get(LOW_NBR)[...])
        size, piece = grad.shape[0] // 4, out.shape[0] // 8
        for b in range(4):
            g_ref[4 * t + b, :size, :] = grad[b * size : (b + 1) * size].astype(BF16)
            for side in range(2):
                at = (2 * b + side) * piece
                lanes = slice(side * out.shape[1], (side + 1) * out.shape[1])
                g_ref[4 * t + b, size:, lanes] = out[at : at + piece].astype(BF16)
        sums_ref[t : t + 1, :] = jnp.sum(dp[...].astype(F32), 0, keepdims=True) + jnp.sum(
            dp_nbr[...].astype(F32), 0, keepdims=True
        )
    give_split(orders, g_ref, sent, kept, place)


def attn_grad_body(last, orders, place, get, staged, put, *_):
    X, X_NBR, D, D_NBR, BIAS, UNITS, SUMS, SUMS_NBR = range(8)
    if last:
        sent, kept, g_ref = staged
        shared = [
            jnp.sum(get(SUMS)[8 * i : 8 * i + 8, :] + get(SUMS_NBR)[8 * i : 8 * i + 8, :], 0, keepdims=True)
            for i in range(6)
        ]
    else:
        sent, kept, bias_ref, g_ref = staged
    size = g_ref.shape[1]
    wide = g_ref.shape[2] - (128 if last else 0)
    for t in range(2):
        cols = slice(t * wide, (t + 1) * wide)
        d, d_nbr = get(D)[:, cols], get(D_NBR)[:, cols]
        grad = dot_rows(get(X)[...], d) + dot_rows(get(X_NBR)[...], d_nbr)
        for b in range(4):
            g_ref[4 * t + b, :, :wide] = grad[b * size : (b + 1) * size].astype(BF16)
        total = jnp.sum(d.astype(F32), 0, keepdims=True) + jnp.sum(d_nbr.astype(F32), 0, keepdims=True)
        if not last:
            bias_ref[t : t + 1, :] = total
            continue
        before = get(BIAS)[t : t + 1, :]
        third, before_third = wide // 3, before.shape[1] // 3
        rows = [
            *shared, before[:, :before_third], total[:, :third], before[:, 2 * before_third :],
            total[:, 2 * third :], get(UNITS)[t : t + 1, :],
        ]
        flat = jnp.concatenate(
            [row[:, i : i + 128] for row in rows for i in range(0, row.shape[1], 128)], 0
        )
        for b in range(4):
            g_ref[4 * t + b, :, wide:] = jnp.zeros((size, 128), BF16)
        g_ref[4 * t, : flat.shape[0], wide:] = flat.astype(BF16)
    give_split(orders, g_ref, sent, kept, place)


def halve_body(orders, stage, place, get, staged, put, *_):
    a, b = get(0), get(1)
    for mine, ref in ((False, staged[0]), (True, staged[1])):
        for m in range(ref.shape[0]):
            k = split_index(orders, stage, m, mine, place)
            ref[m] = (a[k].astype(F32) + b[k].astype(F32)).astype(BF16)


def add_body(place, get, staged, put, *_):
    staged[0][...] = (get(0)[...].astype(F32) + get(1)[...].astype(F32)).astype(BF16)


def square(place):
    y, z = place.y, place.z
    return (2 * y + z, 2 - 2 * y + z, 2 * y + 1 - z, 3 - 2 * y - z)


def pairs(place):
    y, z = place.y, place.z
    return (y, 1 - y, 2 + z, 3 - z)


def join_body(where, place, get, staged, put, *_):
    ref = staged[0]
    size = ref.shape[0] // 4
    for i, at in enumerate(where(place)):
        ref[strip(at, size), :] = get(i)[...]


def blend(place, pair):
    return pair[0] + place.core * (pair[1] - pair[0])


def join_pair_body(axes, place, get, staged, put, *_):
    at = blend(place, [{"y": place.y, "z": place.z}[axis[0]] for axis in axes])
    staged[0][at] = get(0)[0]
    staged[0][1 - at] = get(1)[0]


def join_blocks_body(axes, place, get, staged, put, *_):
    for i in range(2):
        y, z = (place.y, place.z) if i == 0 else (1 - place.y, 1 - place.z)
        for b in range(2):
            at = blend(place, [2 * y + b if axis[0] == "z" else 2 * b + z for axis in axes])
            staged[0][at] = get(i)[b]


def cores(place, get):
    return (place.core, get(0)), (1 - place.core, get(1))


def outer_out_body(place, get, staged, put, _, __, outs):
    for i in (1, 2):
        put(get(1 + i), outs[i])
    for i, (core, ref) in enumerate(cores(place, get)):
        for b in range(4):
            held = staged[4 * i + b]
            held[...] = ref[b].astype(F32)
            put(held, outs[0].at[strip(4 * core + b, held.shape[0]), :])


def inner_out_body(size, place, get, staged, put, _, __, outs):
    for i, (core, ref) in enumerate(cores(place, get)):
        for b in range(4):
            held = staged[4 * i + b]
            held[...] = ref[b].astype(F32)
            wide = held.shape[1]
            piece = held.shape[0] - size
            put(held.at[:size], outs[0].at[b * size : (b + 1) * size, strip(core, wide)])
            for side in range(2):
                at = (2 * b + side) * piece
                put(
                    held.at[size:, side * (wide // 2) : (side + 1) * (wide // 2)],
                    outs[1].at[at : at + piece, strip(core, wide // 2)],
                )


def attn_out_body(first_col, sizes, place, get, staged, put, _, __, outs):
    for i, (core, ref) in enumerate(cores(place, get)):
        for b in range(4):
            held = staged[4 * i + b]
            held[...] = ref[b].astype(F32)
            size, wide = held.shape[0], held.shape[1] - (128 if sizes else 0)
            rows = strip(4 * core + b, size)
            third = wide // 3
            for part in range(3):
                cols = slice(first_col, first_col + third)
                put(held.at[:, part * third : (part + 1) * third], outs[part].at[rows, cols])
    if not sizes:
        return

    def flat(held, at, size):
        wide = held.shape[1] - 128
        parts = [held[at + i : at + i + 1, wide:] for i in range(size // 128)]
        return jnp.concatenate(parts, 1).reshape(size)

    at = 0
    for ref, out, size in zip(staged[8:], outs[3:], sizes):
        ref[...] = jnp.where(place.core == 0, flat(staged[0], at, size), flat(staged[4], at, size))
        put(ref, out)
        at += size // 128
    size = staged[-1].shape[0]
    for ref, held, core in ((staged[-2], staged[0], place.core), (staged[-1], staged[4], 1 - place.core)):
        ref[...] = flat(held, at, size)
        put(ref, outs[-1].at[strip(core, size)])


def local(
    dp,
    inputs,
    lengths,
    query_weight,
    query_bias,
    key_weight,
    value_weight,
    value_bias,
    output_weight,
    output_bias,
    first_gain,
    first_shift,
    inner_weight,
    inner_bias,
    outer_weight,
    outer_bias,
    second_gain,
    second_shift,
    cotangent,
):
    chains, slots, model = inputs.shape
    rows = chains * slots
    width = query_weight.shape[1]
    units = inner_weight.shape[1]
    group = units // 2
    half = model // 2
    levels = int(math.log2(dp))
    line = Line()

    def bit_swap(v, bit):
        return lax.ppermute(v, DP, [(i, i ^ (1 << bit)) for i in range(dp)])

    def named(swap):
        def run(name, *v):
            with jax.named_scope(name):
                return swap(*v)

        return run

    @named
    def core_swap(v):
        return bit_swap(v, 0)

    @named
    def y_swap(v):
        return bit_swap(v, 1)

    @named
    def z_swap(v):
        return bit_swap(v, 2)

    @named
    def x_swap(v):
        return lax.ppermute(v, TENSOR, [(0, 1), (1, 0)])

    @named
    def diagonal_swap(v):
        return lax.ppermute(v, DP, [(i, i ^ 6) for i in range(dp)])

    @named
    def gather_swap(v, axes, step):
        return lax.ppermute(v, DP, [(i, i ^ (2 if axes[i % 2][step] == "y" else 4)) for i in range(dp)])

    @named
    def order_swap(v, orders, stage):
        pairs = []
        for spot in range(dp):
            for t in range(2):
                d = orders[spot % 2][stage]
                to = (spot, 1 - t) if d == "t" else (spot ^ (2 if d == "y" else 4), t)
                pairs.append((2 * spot + t, 2 * to[0] + to[1]))
        return lax.ppermute(v, (DP, TENSOR), pairs)

    x = inputs.reshape(rows, model)
    cot = cotangent.reshape(rows, model)

    quarter, bit, eighth = model // 4, model // 8, units // 8
    all_rows = slice(None)
    low_width = ((rows, width), BF16)
    low_wide = ((rows, model), BF16)
    wide = ((rows, model), F32)
    act = ((rows, group), BF16)
    pairs_here = width // PAIR
    probs_shape = ((chains * pairs_here, slots, 2 * slots), BF16)
    len_smem = [(lengths.shape, jnp.int32)]
    g = SimpleNamespace()

    def lanes(arr, at, count):
        return piece(arr, (rows, count), lambda p: (all_rows, slice(at, at + count)))

    def spacer(name):
        line(name, lambda *_: None, [], [])

    def pack_attn():
        def body(place, get, staged, put, wait, refs, _):
            core, y, z, _ = place
            for at, row in ((0, y), (1, 2 + z)):
                to = staged[0].at[at * bit : (at + 1) * bit]
                for i, w in enumerate(refs[:3]):
                    put(w.at[strip(4 * core + row, bit), :], to.at[:, i * width : (i + 1) * width])
                put(refs[3].at[strip(row, bit), strip(core, half)], to.at[:, 3 * width :])

        (cut,) = line(
            "p1", body, [], [((2 * bit, 3 * width + half), BF16)],
            hbm=[query_weight, key_weight, value_weight, output_weight],
        )
        g.attn_mine = x_swap("ax", cut)

    def pack_rest():
        def body(place, get, staged, put, wait, refs, _):
            w_in, w_out, bq, bv, bi = refs
            wi_ref, wo_ref, bias_ref = staged
            core, y, z, _ = place
            put(w_in.at[strip(2 * y + z, quarter), strip(core, group)], wi_ref)
            put(w_out.at[strip(4 * core + y, eighth), :], wo_ref.at[:eighth])
            put(w_out.at[strip(4 * core + 2 + z, eighth), :], wo_ref.at[eighth:])
            put(bq, bias_ref.at[pl.ds(0, width)])
            put(bv, bias_ref.at[pl.ds(width, width)])
            put(bi, bias_ref.at[pl.ds(2 * width, units)])

        wi_cut, wo_cut, biases = line(
            "p2", body, [],
            [
                ((quarter, group), BF16), ((2 * eighth, model), BF16), ((2 * width + units,), F32),
            ],
            hbm=[inner_weight, outer_weight, query_bias, value_bias, inner_bias],
        )
        g.biases = x_swap("bx", biases)
        g.wi_mine = x_swap("wix", wi_cut)
        g.wo_mine = x_swap("wox", wo_cut)

    def relay(name, arr, parts, seen=()):
        dims = (arr.shape[0] // parts, arr.shape[1])
        return line(
            name, lambda p, get, staged, put, *_: [put(get(i), staged[i]) for i in range(parts)],
            [
                piece(arr, dims, lambda p, i=i: (slice(i * dims[0], (i + 1) * dims[0]), all_rows))
                for i in range(parts)
            ],
            [(dims, BF16)] * parts, seen=seen,
        )

    def join_four(name, where, pieces):
        dims = (4 * pieces[0].shape[0], pieces[0].shape[1])
        (own,) = line(name, lambda *a: join_body(where, *a), [load(v) for v in pieces], [(dims, BF16)])
        return own, core_swap(name + "c", own)

    def relay_attn():
        g.attn_a, g.attn_b = relay("ra", g.attn_mine, 2, [g.biases])
        g.attn_y, g.attn_z = y_swap("ay", g.attn_a), z_swap("az", g.attn_b)

    def relay_in():
        (g.wi_own,) = relay("rw", g.wi_mine, 1)
        v = g.wi_own
        g.wi_pieces = [v, y_swap("wiy", v), z_swap("wiz", v), diagonal_swap("wid", v)]

    def relay_out():
        g.wo_a, g.wo_b = relay("ro", g.wo_mine, 2)
        g.wo_y, g.wo_z = y_swap("woy", g.wo_a), z_swap("woz", g.wo_b)

    def join_attn():
        g.attn_weights = join_four("ja", pairs, [g.attn_a, g.attn_y, g.attn_b, g.attn_z])

    def join_in():
        g.wi_b, g.wi_a = join_four("jw", square, g.wi_pieces)

    def join_out():
        g.wo_b, g.wo_a = join_four("jo", pairs, [g.wo_a, g.wo_y, g.wo_b, g.wo_z])

    def attn_fwd_own():
        args = [
            x, query_weight, key_weight, value_weight, output_weight, inner_bias, cot, output_bias, first_gain,
            first_shift, outer_bias, second_gain, second_shift,
        ]
        *args, q, k, v, probs, g.joint, g.part_own = line(
            "f1", lambda *a: attn_fwd_own_body(chains, *a), [],
            [(arr.shape, arr.dtype) for arr in args] + [low_width] * 3 + [probs_shape, ((rows, width + half), BF16), wide],
            hbm=[*args, query_bias, value_bias, lengths],
            scratch=[(query_bias.shape, F32), (value_bias.shape, F32)], smem=len_smem, copies=len(args) + 4,
        )
        (
            g.x, g.wq, g.wk, g.wv, g.wo_attn, g.bi, g.cot,
            g.output_bias, g.first_gain, g.first_shift, g.outer_bias, g.second_gain, g.second_shift,
        ) = args
        g.wi, g.wo = inner_weight, outer_weight
        g.own = [load(arr) for arr in (g.wo_attn, q, k, v, probs, g.wq, g.wk, g.wv)]

    def bias_oth(at, size):
        return Load((size,), F32, [(g.biases, lambda p: (pl.ds(pl.multiple_of(at(p), 128), size),), None)])

    def attn_fwd_oth():
        q, k, v, probs, g.r1, joint, w, wo = line(
            "f2", lambda *a: attn_fwd_oth_body(chains, width, *a),
            [
                load(g.x), bias_oth(lambda p: 0, width), bias_oth(lambda p: width, width),
                *(load(v) for v in (g.part_own, g.output_bias, g.first_gain, g.first_shift, *g.attn_weights, g.joint)),
            ],
            [low_width] * 3
            + [probs_shape, wide, ((rows, model + 2 * width + half), BF16)]
            + [((model, 3 * width), BF16), ((width, model), BF16)],
            hbm=[lengths], smem=len_smem,
        )
        g.oth = [load(arr) for arr in (wo, q, k, v, probs)] + [
            piece(w, (model, width), lambda p, i=i: (all_rows, slice(i * width, (i + 1) * width))) for i in range(3)
        ]
        g.hid, g.ctx_oth = lanes(joint, 0, model), lanes(joint, model, width)
        g.hid_nbr_all = core_swap("hc", joint)
        g.hid_nbr, g.ctx_oth_nbr = lanes(g.hid_nbr_all, 0, model), lanes(g.hid_nbr_all, model, width)
        g.ctx_own, g.ctx_own_nbr = (lanes(v, model + width, width) for v in (joint, g.hid_nbr_all))
        g.x_nbr = lanes(g.hid_nbr_all, model + 2 * width, half)

    def flipped(p, flip):
        return 1 - p.core if flip else p.core

    def wi_own(flip):
        return piece(g.wi, (model, group), lambda p: (all_rows, strip(flipped(p, flip), group)))

    def wo_own(flip):
        return piece(g.wo, (group, model), lambda p: (strip(flipped(p, flip), group), all_rows))

    def bi_own(flip):
        return piece(g.bi, (group,), lambda p: (strip(flipped(p, flip), group),))

    def bi_oth(flip):
        return bias_oth(lambda p: 2 * width + flipped(p, flip) * group, group)

    def ffn_own():
        g.acta_own, g.actb_own, g.dga_own, g.dgb_own, g.ffn_own = line(
            "n1", ffn_own_body,
            [g.hid, wi_own(True), bi_own(True), wi_own(False), bi_own(False), wo_own(True), wo_own(False)],
            [act] * 4 + [wide],
        )
        g.acta_own_nbr = core_swap("a1", g.acta_own)

    def ffn_oth_pre():
        g.acta_oth, g.actb_oth, g.dga_oth, g.dgb_oth = line(
            "m2", ffn_pre_body, [g.hid, load(g.wi_a), bi_oth(True), load(g.wi_b), bi_oth(False)], [act] * 4,
            seen=[g.hid_nbr_all],
        )
        g.acta_oth_nbr = core_swap("a2", g.acta_oth)

    def ffn_oth_post():
        names = (g.outer_bias, g.second_gain, g.second_shift, g.cot)
        g.result, g.dr2, g.low2, g.sums2 = line(
            "n2", ffn_post_body,
            [
                load(v)
                for v in (
                    g.acta_oth, g.actb_oth, g.wo_a, g.wo_b, g.ffn_own, g.r1, g.first_gain, g.first_shift, *names,
                )
            ],
            [low_wide, wide, low_wide, ((24, model), F32)], seen=[g.acta_own_nbr],
        )
        g.low2_nbr = core_swap("lo", g.low2)

    def ffn_bwd_oth():
        g.dpa_oth, g.dpb_oth, g.back = line(
            "k2", lambda *a: ffn_bwd_body(False, *a),
            [load(v) for v in (g.low2, g.wo_a, g.dga_oth, g.wo_b, g.dgb_oth, g.wi_a, g.wi_b, g.dr2)],
            [act] * 2 + [wide],
        )
        g.dpa_oth_nbr = core_swap("pb", g.dpa_oth)

    def ffn_bwd_own():
        joint, g.dpb_own, g.dr1, g.low1, g.sums = line(
            "k1", lambda *a: ffn_bwd_body(True, *a),
            [
                load(g.low2), wo_own(True), load(g.dga_own), wo_own(False), load(g.dgb_own),
                wi_own(True), wi_own(False), load(g.back), load(g.r1), load(g.first_gain), load(g.sums2),
            ],
            [((rows, group + half), BF16), act, wide, low_wide, ((48, model), F32)],
        )
        joint_nbr = core_swap("pl", joint)
        g.dpa_own_nbr, g.low1_nbr = lanes(joint_nbr, 0, group), lanes(joint_nbr, group, half)
        g.sums_nbr = core_swap("s", g.sums)

    def split_outs(dims):
        return [((4, *dims), BF16), ((4, *dims), BF16)]

    dims_of = {
        OUTER: (group // 4, model),
        INNER: (model // 4 + width // 8, group),
        ATTN: (half // 4, 3 * (pairs_here - 1) * PAIR),
        LAST: (half // 4, 3 * PAIR + 128),
    }
    held, made = {}, {}

    def grad(name, body, loads, outs=(), seen=()):
        sent, kept, *rest = line(
            name + "0", lambda *a: body(ORDERS[name], *a), loads, split_outs(dims_of[name]) + [*outs],
            scratch=[((8, *dims_of[name]), BF16)], seen=seen,
        )
        held[name] = kept, order_swap(name + "0", sent, ORDERS[name], 0)
        return rest

    def outer_grad():
        names = (g.low2, g.low2_nbr, g.actb_own, g.acta_own_nbr, g.actb_oth, g.acta_oth_nbr)
        grad(OUTER, outer_grad_body, [load(v) for v in names])

    def inner_grad():
        loads = [
            g.hid, g.hid_nbr, piece(g.low1, (rows, half), lambda p: (all_rows, strip(p.core, half))), g.low1_nbr,
            load(g.dpb_own), g.dpa_own_nbr, g.ctx_own, g.ctx_own_nbr,
            load(g.dpb_oth), load(g.dpa_oth_nbr), g.ctx_oth, g.ctx_oth_nbr,
        ]
        (g.unit_sums,) = grad(INNER, inner_grad_body, loads, [((8, group), F32)])

    def attn_bwd(name, first_pair, last_pair, acc):
        count = last_pair - first_pair
        d, g.back_in = line(
            name, lambda *a: attn_bwd_body(first_pair, last_pair, chains, *a),
            [load(g.low1), load(acc), *g.own, *g.oth],
            [((rows, 6 * count * PAIR), BF16), wide],
            scratch=[((rows, count * PAIR), BF16), ((model, 6 * count * PAIR), BF16)],
        )
        return d, core_swap(name + "c", d)

    def attn_bwd_most():
        g.d_most = attn_bwd("ba", 0, pairs_here - 1, g.dr1)

    def attn_bwd_rest():
        g.d_rest = attn_bwd("bb", pairs_here - 1, pairs_here, g.back_in)

    def attn_grad(name, d, more, outs=()):
        x_cut = piece(g.x, (rows, half), lambda p: (all_rows, strip(p.core, half)))
        loads = [x_cut, g.x_nbr, *(load(v) for v in (*d, *more))]
        return grad(name, lambda *a: attn_grad_body(name == LAST, *a), loads, outs)

    def attn_grad_most():
        (g.bias_sums,) = attn_grad(ATTN, g.d_most, [], [((8, dims_of[ATTN][1]), F32)])

    def attn_grad_rest():
        attn_grad(LAST, g.d_rest, [g.bias_sums, g.unit_sums, g.sums, g.sums_nbr])

    def halve(name, stage):
        kept, recv = held[name]
        orders = ORDERS[name]
        out = ((kept.shape[0] // 2, *kept.shape[1:]), BF16)
        sent, kept = line(
            name + str(stage), lambda *a: halve_body(orders, stage, *a), [load(kept), load(recv)], [out, out]
        )
        held[name] = kept, order_swap(name + str(stage), sent, orders, stage)

    def add(kernel, name, bit):
        a, b = held[name]
        (v,) = line(kernel, add_body, [load(a), load(b)], [(a.shape, BF16)])
        if bit < levels:
            with jax.named_scope(name + str(bit)):
                held[name] = v, bit_swap(v, bit)
            return
        held[name] = v, gather_swap(name + "n", v, GATHER[name], 0)

    def level(name):
        for bit in range(4, levels + 1):
            add(name + "l", name, bit)

    def join_pair(name):
        (v,) = line(
            name + "m", lambda *a: join_pair_body(GATHER[name], *a), [load(v) for v in held[name]],
            [((2, *dims_of[name]), BF16)],
        )
        held[name] = v, gather_swap(name + "p", v, GATHER[name], 1)

    def join(name):
        (v,) = line(
            name + "j", lambda *a: join_blocks_body(GATHER[name], *a), [load(v) for v in held[name]],
            [((4, *dims_of[name]), BF16)],
        )
        held[name] = v, core_swap(name + "c", v)

    def write(name, body, outs, copies, more=(), onto=(), loads=(), low_outs=()):
        made[name] = line(
            name + "w", body, [load(v) for v in (*held[name], *loads)], [], hbm=onto,
            hbm_outs=[(dims, F32) for dims in outs] + [(dims, BF16) for dims in low_outs],
            scratch=[(dims_of[name], F32)] * 8 + [((size,), F32) for size in more], copies=copies,
            aliases={i: i for i in range(len(onto))},
        )

    sizes = [model] * 6 + [width] * 2
    attn_outs = [(model, width)] * 3
    last_outs = attn_outs + [(size,) for size in sizes] + [(units,)]
    steps = {
        "p1": pack_attn, "p2": pack_rest, "ra": relay_attn, "rw": relay_in, "ro": relay_out,
        "ja": join_attn, "jw": join_in, "jo": join_out,
        "f1": attn_fwd_own, "f2": attn_fwd_oth, "n1": ffn_own, "m2": ffn_oth_pre, "n2": ffn_oth_post,
        "k2": ffn_bwd_oth, "k1": ffn_bwd_own, "ba": attn_bwd_most, "bb": attn_bwd_rest,
        "O0": outer_grad, "I0": inner_grad, "A0": attn_grad_most, "B0": attn_grad_rest,
        "Ow": lambda: write(
            OUTER, outer_out_body, [(units, model), (rows, model)], 10, loads=[g.back_in, g.result],
            low_outs=[(rows, model)],
        ),
        "Iw": lambda: write(
            INNER, lambda *a: inner_out_body(model // 4, *a), [(model, units), (width, model)], 24
        ),
        "Aw": lambda: write(ATTN, lambda *a: attn_out_body(0, (), *a), attn_outs, 24),
        "Bw": lambda: write(
            LAST, lambda *a: attn_out_body((pairs_here - 1) * PAIR, sizes, *a), last_outs, 34,
            [*sizes, group, group], made[ATTN],
        ),
    }
    for name in (OUTER, INNER, ATTN, LAST):
        steps[name + "1"] = lambda name=name: halve(name, 1)
        steps[name + "2"] = lambda name=name: halve(name, 2)
        steps[name + "3"] = lambda name=name: add(name + "3", name, 3)
        steps[name + "l"] = lambda name=name: level(name)
        steps[name + "m"] = lambda name=name: join_pair(name)
        steps[name + "j"] = lambda name=name: join(name)
    for step in ORDER:
        steps.get(step, lambda step=step: spacer(step))()
    grad_outer, grad_inputs, result = made[OUTER]
    grad_inner, grad_out = made[INNER]
    grad_q, grad_k, grad_v, g_sg, g_ss, g_ob2, g_fg, g_fs, g_ob1, g_qb, g_vb, g_ib = made[LAST]

    def back_to(v):
        return v.reshape(chains, slots, model)

    return (
        back_to(result), back_to(grad_inputs),
        grad_q, g_qb, grad_k, grad_v, g_vb, grad_out, g_ob1, g_fg, g_fs,
        grad_inner, g_ib, grad_outer, g_ob2, g_sg, g_ss,
    )


def solution(mesh):
    dp = mesh.shape[DP]
    rows, cols, low = P((DP, TENSOR), None, None), P(None, TENSOR), P(TENSOR, None)
    part, full = P(TENSOR), P()
    in_specs = (
        rows, P(DP), cols, part, cols, cols, part, low, full, full, full, cols, part, low, full, full, full, rows,
    )
    out_specs = (
        rows, rows, cols, part, cols, cols, part, low, full, full, full, cols, part, low, full, full, full,
    )

    def run(*args):
        return local(dp, *args)

    return jax.shard_map(run, mesh=mesh, in_specs=in_specs, out_specs=out_specs, check_vma=False)
```
